32 devices in a mesh: head: 4 (over y, x), blk: 8 (over z, core).
Axes of the slice: x: 2, y: 2, z: 4, core: 2. Of those that a mesh axis runs over, the one named last changes fastest.
Arguments:
- layer_input: bfloat16 [2, 8, 256, 512], P(None, 'blk', 'head'), may hold values from -6 to 6
- segments: int32 [2, 2048], replicated, may hold values from 0 to 16, as said below
- token_valid: int32 [2, 2048], replicated, may hold values from 0 to 1, as said below
- attention_gain: bfloat16 [512], P(('head', 'blk')), may hold values from 0.5 to 1.5
- attention_shift: bfloat16 [512], P(('head', 'blk')), may hold values from -1.25 to 1.25
- project_weight: bfloat16 [512, 1536], P(('head', 'blk')), may hold values from -0.25 to 0.25
- project_bias: bfloat16 [1024], P(('head', 'blk')), may hold values from -1.25 to 1.25
- output_weight: bfloat16 [512, 512], P(('head', 'blk')), may hold values from -1.5 to 1.5
- output_bias: bfloat16 [512], P(('head', 'blk')), may hold values from -1.25 to 1.25
- feed_gain: bfloat16 [512], P(('head', 'blk')), may hold values from 0.5 to 1.5
- feed_shift: bfloat16 [512], P(('head', 'blk')), may hold values from -1.25 to 1.25
- up_weight: bfloat16 [512, 2048], P(('head', 'blk')), may hold values from -0.25 to 0.25
- up_bias: bfloat16 [2048], P(('head', 'blk')), may hold values from -1.25 to 1.25
- down_weight: bfloat16 [2048, 512], P(('head', 'blk')), may hold values from -0.125 to 0.125
- down_bias: bfloat16 [512], P(('head', 'blk')), may hold values from -1.25 to 1.25
- cotangent: bfloat16 [2, 8, 256, 512], P(None, 'blk', 'head'), may hold values from -6 to 6
Outputs:
- layer_output: bfloat16 [2, 8, 256, 512], P(None, 'blk', 'head')
- input_grad: bfloat16 [2, 8, 256, 512], P(None, 'blk', 'head')
- attention_gain_grad: float32 [512], P(('head', 'blk'))
- attention_shift_grad: float32 [512], P(('head', 'blk'))
- project_weight_grad: float32 [512, 1536], P(('head', 'blk'))
- project_bias_grad: float32 [1024], P(('head', 'blk'))
- output_weight_grad: float32 [512, 512], P(('head', 'blk'))
- output_bias_grad: float32 [512], P(('head', 'blk'))
- feed_gain_grad: float32 [512], P(('head', 'blk'))
- feed_shift_grad: float32 [512], P(('head', 'blk'))
- up_weight_grad: float32 [512, 2048], P(('head', 'blk'))
- up_bias_grad: float32 [2048], P(('head', 'blk'))
- down_weight_grad: float32 [2048, 512], P(('head', 'blk'))
- down_bias_grad: float32 [512], P(('head', 'blk'))
The draws below stay inside these ranges and needn't reach their ends.
Inputs may be any that keep to these rules, and one draw needn't show every extreme that they name: `segments`: in each sequence segment numbers start at 0 and never fall. In one sequence, drawn from the seed, segment 1 starts within its first 256 positions and runs to its end; in the others every segment but the last holds 12 to 127 positions, and the last segment number is the most. `token_valid`: each sequence is ones followed by zeros; its last 1 to 256 positions are zeros, and fewer than 128 of them in the sequence whose segment 1 runs to its end.
All inputs are finite; a program needn't handle non-finite values.
Results may differ from the reference program's by a relative error of at most 0.018.
Values may be sent and summed in bfloat16 or wider, within the bound.
No kernel may reach another device: no remote copies, remote signals or barrier semaphores. Data moves between devices by JAX's collectives and lax.ppermute only.
A program may use at most 128 MiB of HBM per device.

```python
import jax
import jax.numpy as jnp
from jax import lax

D = 512
H = 8
HD = 64
FF = 2048
SEQS = 2
BLOCKS = 8
BLOCK_LEN = 256
SEQLEN = 2048
DOC_MIN = 12
DOC_MAX = 128
PAD_MAX = 256


def document_tables(key):
    top_segment = (SEQLEN - 1) // (DOC_MAX - 1)
    doc_count = SEQLEN // DOC_MIN + 1
    several = jax.random.split(key, 5)
    lengths = jax.random.randint(several[0], (SEQS, doc_count), DOC_MIN, DOC_MAX)
    doc_ends = jnp.cumsum(lengths, axis=1)
    position = jnp.arange(SEQLEN, dtype=jnp.int32)
    packed = jnp.sum((doc_ends[:, :, None] <= position[None, None, :]).astype(jnp.int32), axis=1)
    packed = jnp.minimum(packed, top_segment)
    opening = jax.random.randint(several[1], (SEQS, 1), 1, BLOCK_LEN)
    single = (position[None, :] >= opening).astype(jnp.int32)
    chosen = jax.random.randint(several[2], (), 0, SEQS)
    is_long = (jnp.arange(SEQS, dtype=jnp.int32) == chosen)[:, None]
    segment_ids = jnp.where(is_long, single, packed).astype(jnp.int32)
    padding = jax.random.randint(several[3], (SEQS, 1), 1, PAD_MAX + 1)
    short_padding = jax.random.randint(several[4], (SEQS, 1), 1, max(BLOCK_LEN // 2, 2))
    padding = jnp.where(is_long, short_padding, padding)
    live_mask = (position[None, :] < SEQLEN - padding).astype(jnp.int32)
    return (segment_ids, live_mask)


def draw_segments(key, part):
    return document_tables(jax.random.fold_in(key, 7))[0]


def draw_token_valid(key, part):
    return document_tables(jax.random.fold_in(key, 7))[1]


def level_of(rng, shape, cuts, low, largest):
    loudness, own = 1.0, jax.random.fold_in(rng, 6)
    for axis_at, blocks in cuts:
        steps = jnp.exp(jax.random.uniform(jax.random.fold_in(own, axis_at), (blocks,), jnp.float32, low / len(cuts), largest / len(cuts)))
        loudness = loudness * jnp.repeat(steps, shape[axis_at] // blocks).reshape([-1 if axis == axis_at else 1 for axis in range(len(shape))])
    return loudness


def noise(rng, dims, spread, reach, cuts=(), held_as=jnp.bfloat16):
    drawn = spread * jax.random.normal(rng, dims, jnp.float32)
    if cuts:
        drawn = drawn * level_of(rng, dims, cuts, -0.22, 0.18)
    return jnp.clip(drawn, -reach, reach).astype(held_as)


def setup_inputs(seed: int = 0) -> dict:
    splits = jax.random.split(jax.random.key(seed), 17)
    layer_input = noise(splits[0], (SEQS, BLOCKS, BLOCK_LEN, D), 1.0, 6.0, ((1, 8), (2, 4)))
    segments = draw_segments(jax.random.fold_in(splits[16], 71), 0)
    token_valid = draw_token_valid(jax.random.fold_in(splits[16], 71), 0)
    attention_gain = jnp.clip(1.0 + 0.1 * jax.random.normal(splits[3], (D,), jnp.float32), 0.5, 1.5).astype(jnp.bfloat16)
    attention_shift = noise(splits[4], (D,), 0.2, 1.25, ((0, 32),))
    project_weight = noise(splits[5], (D, 3 * D), D ** -0.5, 0.25, ((0, 32),))
    project_bias = noise(splits[6], (2 * D,), 0.2, 1.25, ((0, 32),))
    output_weight = noise(splits[7], (D, D), (D // 32) ** -0.5, 1.5, ((0, 32),))
    output_bias = noise(splits[8], (D,), 0.2, 1.25, ((0, 32),))
    feed_gain = jnp.clip(1.0 + 0.1 * jax.random.normal(splits[9], (D,), jnp.float32), 0.5, 1.5).astype(jnp.bfloat16)
    feed_shift = noise(splits[10], (D,), 0.2, 1.25, ((0, 32),))
    up_weight = noise(splits[11], (D, FF), D ** -0.5, 0.25, ((0, 32),))
    up_bias = noise(splits[12], (FF,), 0.2, 1.25, ((0, 32),))
    down_weight = noise(splits[13], (FF, D), FF ** -0.5, 0.125, ((0, 32),))
    down_bias = noise(splits[14], (D,), 0.2, 1.25, ((0, 32),))
    cotangent = noise(splits[15], (SEQS, BLOCKS, BLOCK_LEN, D), 1.0, 6.0, ((1, 8), (2, 4)))
    return dict(layer_input=layer_input, segments=segments, token_valid=token_valid, attention_gain=attention_gain, attention_shift=attention_shift, project_weight=project_weight, project_bias=project_bias, output_weight=output_weight, output_bias=output_bias, feed_gain=feed_gain, feed_shift=feed_shift, up_weight=up_weight, up_bias=up_bias, down_weight=down_weight, down_bias=down_bias, cotangent=cotangent)


@jax.custom_vjp
def low(v):
    return lax.optimization_barrier(v.astype(jnp.bfloat16)).astype(jnp.float32)

@jax.custom_vjp
def low_back(v):
    return v

def low_keep(v):
    return (low(v), None)

def low_pass(kept, grad):
    return (grad,)

def back_keep(v):
    return (v, None)

def back_low(kept, grad):
    return (low(grad),)
low.defvjp(low_keep, low_pass)
low_back.defvjp(back_keep, back_low)
EPSILON = 1e-05
NEG_FILL = -1e+30

def matmul(left, right):
    return jnp.dot(left, right, precision=lax.Precision.HIGHEST)

def layer_norm(values, gain, shift):
    centred = values - lax.optimization_barrier(jnp.mean(values, axis=-1, keepdims=True))
    variance = lax.optimization_barrier(jnp.mean(centred * centred, axis=-1, keepdims=True))
    return centred * lax.rsqrt(variance + EPSILON) * gain + shift

def attention(queries, keys_all, values_all, seg_row, live_row):
    length = queries.shape[0]
    block_count = length // BLOCK_LEN
    head_q = queries.reshape(length, H, HD).transpose(1, 0, 2)
    head_k = keys_all.reshape(length, H, HD).transpose(1, 0, 2)
    head_v = values_all.reshape(length, H, HD).transpose(1, 0, 2)
    key_pos = jnp.arange(length, dtype=jnp.int32)
    scale = HD ** (-0.5)

    def one_block(index):
        head_id = index // block_count
        block_id = index % block_count
        start = (block_id * BLOCK_LEN).astype(jnp.int32)
        query_rows = lax.dynamic_slice(head_q, (head_id, start, jnp.int32(0)), (1, BLOCK_LEN, HD))[0]
        key_rows = lax.dynamic_index_in_dim(head_k, head_id, 0, keepdims=False)
        value_rows = lax.dynamic_index_in_dim(head_v, head_id, 0, keepdims=False)
        scores = low_back(scale * matmul(query_rows, key_rows.T))
        query_pos = start + jnp.arange(BLOCK_LEN, dtype=jnp.int32)
        query_seg = lax.dynamic_slice_in_dim(seg_row, start, BLOCK_LEN)
        allowed = (query_seg[:, None] == seg_row[None, :]) & (key_pos[None, :] <= query_pos[:, None])
        allowed = allowed & ((live_row[None, :] == 1) | (key_pos[None, :] == query_pos[:, None]))
        masked = jnp.where(allowed, scores, NEG_FILL)
        row_max = lax.optimization_barrier(jnp.max(masked, axis=-1, keepdims=True))
        row_total = lax.optimization_barrier(jnp.sum(jnp.exp(masked - row_max), axis=-1, keepdims=True))
        probs = jnp.where(allowed, jnp.exp(masked - row_max - jnp.log(row_total)), 0.0)
        return matmul(low(probs), value_rows)
    pieces = lax.map(jax.checkpoint(one_block), jnp.arange(H * block_count, dtype=jnp.int32))
    return pieces.reshape(H, length, HD).transpose(1, 0, 2).reshape(length, H * HD)

def layer(sequence, seg_row, live_row, params):
    attention_gain, attention_shift, project_weight, project_bias, output_weight, output_bias, feed_gain, feed_shift, up_weight, up_bias, down_weight, down_bias = params
    normed = low(layer_norm(sequence, attention_gain, attention_shift))
    bias_full = jnp.concatenate([project_bias[:D], jnp.zeros_like(project_bias[:D]), project_bias[D:]])
    projected = matmul(normed, project_weight) + bias_full
    queries = low(low_back(projected[:, :D]))
    keys_all = low(low_back(projected[:, D:2 * D]))
    values_all = low(low_back(projected[:, 2 * D:]))
    mixed = attention(queries, keys_all, values_all, seg_row, live_row)
    mixed = low(low_back(mixed))
    branch = low_back(matmul(mixed, output_weight) + output_bias)
    middle = sequence + branch
    second = low(layer_norm(middle, feed_gain, feed_shift))
    hidden = low_back(matmul(second, up_weight) + up_bias)
    activated = low(hidden * jax.nn.sigmoid(1.702 * hidden))
    feed_out = low_back(matmul(activated, down_weight) + down_bias)
    return middle + feed_out

def reference(layer_input, segments, token_valid, attention_gain, attention_shift, project_weight, project_bias, output_weight, output_bias, feed_gain, feed_shift, up_weight, up_bias, down_weight, down_bias, cotangent):
    sequences = layer_input.astype(jnp.float32).reshape(SEQS, SEQLEN, D)
    params = tuple((parameter.astype(jnp.float32) for parameter in (attention_gain, attention_shift, project_weight, project_bias, output_weight, output_bias, feed_gain, feed_shift, up_weight, up_bias, down_weight, down_bias)))

    def forward(inputs_all, weights):
        return lax.map(lambda packet: layer(packet[0], packet[1], packet[2], weights), (inputs_all, segments, token_valid))
    outputs, pullback = jax.vjp(forward, sequences, params)
    input_grad, weight_grads = pullback(cotangent.astype(jnp.float32).reshape(SEQS, SEQLEN, D))
    block_shape = (SEQS, BLOCKS, BLOCK_LEN, D)
    return (outputs.reshape(block_shape).astype(jnp.bfloat16), input_grad.reshape(block_shape).astype(jnp.bfloat16), weight_grads[0], weight_grads[1], weight_grads[2], weight_grads[3], weight_grads[4], weight_grads[5], weight_grads[6], weight_grads[7], weight_grads[8], weight_grads[9], weight_grads[10], weight_grads[11])
```

```python
import functools

import jax
import jax.numpy as jnp
from jax import lax
from jax.experimental import pallas as pl
from jax.experimental.pallas import tpu as pltpu
from jax.sharding import PartitionSpec as P

H = 8
HD = 64
LANES = 128
EPSILON = 1e-05
NEG_FILL = -1e30
TILE_Q = 256

bf16 = jnp.bfloat16
f32 = jnp.float32
i32 = jnp.int32
BOTH = ("head", "blk")


def dot_nn(a, b):
    return lax.dot_general(a, b, (((1,), (0,)), ((), ())), preferred_element_type=f32)


def dot_nt(a, b):
    return lax.dot_general(a, b, (((1,), (1,)), ((), ())), preferred_element_type=f32)


def dot_tn(a, b):
    return lax.dot_general(a, b, (((0,), (0,)), ((), ())), preferred_element_type=f32)


def norm_forward(values, gain, shift):
    centred = values - jnp.mean(values, axis=-1, keepdims=True)
    variance = jnp.mean(centred * centred, axis=-1, keepdims=True)
    inverse_root = lax.rsqrt(variance + EPSILON)
    unit_value = centred * inverse_root
    return (unit_value * gain + shift, unit_value, inverse_root)


def norm_input_grad(upstream, unit_value, inverse_root, gain):
    scaled = upstream * gain
    inner = scaled - jnp.mean(scaled, axis=-1, keepdims=True)
    inner = inner - unit_value * jnp.mean(scaled * unit_value, axis=-1, keepdims=True)
    return inverse_root * inner


class AttentionShape:
    def __init__(self, blocks, part_rows, parts, run, stride):
        self.per_tile = max(1, TILE_Q // part_rows)
        self.tiles = blocks // self.per_tile
        self.tile = self.per_tile * part_rows
        self.part_rows = part_rows
        self.parts = parts
        self.run = run
        self.stride = stride
        self.span = self.tile * parts


def unpack_tile(packed_ref, tile, geo):
    half = geo.part_rows // 2
    pieces = []
    for i in range(geo.per_tile):
        packed = packed_ref[tile * geo.per_tile + i]
        pieces += [packed[:, :HD], packed[:, HD:]]
    return jnp.concatenate(pieces, axis=0)


def key_base(geo):
    rows = lax.broadcasted_iota(i32, (geo.tile, 1), 0)
    return (rows // geo.run) * geo.stride + rows % geo.run


def forward_kernel(geo, scal_ref, q_ref, kv_ref, bounds_ref, out_ref, ot_ref, lse_ref, kvt_ref):
    base = jnp.broadcast_to(key_base(geo), (geo.tile, geo.tile))
    for part in range(geo.parts):
        for tile in range(geo.tiles):
            kvt_ref[part, tile] = kv_ref[part, tile].T
    for tile in range(geo.tiles):
        q = unpack_tile(q_ref, tile, geo) * jnp.asarray(HD**-0.5, bf16)
        qz = jnp.concatenate([q, jnp.zeros_like(q)], axis=1)
        start = bounds_ref[tile, 0:1]
        last = bounds_ref[tile, 1:2]
        own = bounds_ref[tile, 2:3]

        def chunk(part, key_tile, carry, diagonal):
            run_max, run_sum, acc = carry
            offset = key_tile * geo.span + scal_ref[part]
            scores = dot_nt(kv_ref[part, key_tile], qz)
            allowed = (base >= start - offset) & (base <= last - offset)
            if diagonal:
                allowed = allowed | (base == own - offset)
            masked = jnp.where(allowed, scores, NEG_FILL)
            new_max = jnp.maximum(run_max, jnp.max(masked, axis=0, keepdims=True))
            factor = jnp.exp(run_max - new_max)
            probs = jnp.where(allowed, jnp.exp(masked - new_max), 0.0)
            new_sum = run_sum * factor + jnp.sum(probs, axis=0, keepdims=True)
            acc = acc * factor + dot_nn(kvt_ref[part, key_tile], probs.astype(bf16))
            return (new_max, new_sum, acc)

        carry = (
            jnp.full((1, geo.tile), NEG_FILL, f32),
            jnp.zeros((1, geo.tile), f32),
            jnp.zeros((2 * HD, geo.tile), f32),
        )
        for part in range(geo.parts):
            carry = chunk(part, tile, carry, True)

        def earlier(key_tile, carry):
            for part in range(geo.parts):
                carry = chunk(part, key_tile, carry, False)
            return carry

        carry = lax.fori_loop(scal_ref[geo.parts + tile], tile, earlier, carry)
        run_max, run_sum, acc = carry
        attended = acc[HD:] / run_sum
        ot_ref[tile] = attended
        lse_ref[tile] = jnp.broadcast_to(run_max + jnp.log(run_sum), (8, geo.tile))
        rows = attended.T
        half = geo.part_rows // 2
        for i in range(geo.per_tile):
            low = rows[2 * i * half : (2 * i + 1) * half]
            high = rows[(2 * i + 1) * half : (2 * i + 2) * half]
            out_ref[tile * geo.per_tile + i] = jnp.concatenate([low, high], axis=1).astype(bf16)


def backward_kernel(
    geo, scal_ref, q_ref, kv_ref, do_ref, bounds_ref, ot_ref, lse_ref, dq_ref, dkv_ref, kvt_ref
):
    base = jnp.broadcast_to(key_base(geo), (geo.tile, geo.tile))
    dkv_ref[...] = jnp.zeros_like(dkv_ref)
    for part in range(geo.parts):
        for tile in range(geo.tiles):
            kvt_ref[part, tile] = kv_ref[part, tile].T
    for tile in range(geo.tiles):
        q = unpack_tile(q_ref, tile, geo) * jnp.asarray(HD**-0.5, bf16)
        do = unpack_tile(do_ref, tile, geo)
        zeros = jnp.zeros_like(q)
        qz = jnp.concatenate([q, zeros], axis=1)
        doz = jnp.concatenate([zeros, do], axis=1)
        delta = jnp.sum(do.astype(f32).T * ot_ref[tile], axis=0, keepdims=True)
        log_total = lse_ref[tile, 0:1]
        start = bounds_ref[tile, 0:1]
        last = bounds_ref[tile, 1:2]
        own = bounds_ref[tile, 2:3]

        def chunk(part, key_tile, acc, diagonal):
            offset = key_tile * geo.span + scal_ref[part]
            keys = kv_ref[part, key_tile]
            scores = dot_nt(keys, qz)
            allowed = (base >= start - offset) & (base <= last - offset)
            if diagonal:
                allowed = allowed | (base == own - offset)
            probs = jnp.where(allowed, jnp.exp(scores - log_total), 0.0)
            grad_probs = dot_nt(keys, doz)
            grad_scores = (probs * (grad_probs - delta)).astype(bf16)
            dkv_ref[part, key_tile] += dot_nn(grad_scores, qz) + dot_nn(probs.astype(bf16), doz)
            return acc + dot_nn(kvt_ref[part, key_tile], grad_scores)

        acc = jnp.zeros((2 * HD, geo.tile), f32)
        for part in range(geo.parts):
            acc = chunk(part, tile, acc, True)

        def earlier(key_tile, acc):
            for part in range(geo.parts):
                acc = chunk(part, key_tile, acc, False)
            return acc

        acc = lax.fori_loop(scal_ref[geo.parts + tile], tile, earlier, acc)
        rows = (acc[:HD] * (HD**-0.5)).T
        half = geo.part_rows // 2
        for i in range(geo.per_tile):
            low = rows[2 * i * half : (2 * i + 1) * half]
            high = rows[(2 * i + 1) * half : (2 * i + 2) * half]
            dq_ref[tile * geo.per_tile + i] = jnp.concatenate([low, high], axis=1).astype(bf16)


def vmem_specs(count):
    return [pl.BlockSpec(memory_space=pltpu.VMEM)] * count


def attention_forward(geo, scalars, q, kv, bounds):
    return pl.pallas_call(
        functools.partial(forward_kernel, geo),
        out_shape=(
            jax.ShapeDtypeStruct(q.shape, bf16),
            jax.ShapeDtypeStruct((geo.tiles, HD, geo.tile), f32),
            jax.ShapeDtypeStruct((geo.tiles, 8, geo.tile), f32),
        ),
        in_specs=[pl.BlockSpec(memory_space=pltpu.SMEM)] + vmem_specs(3),
        out_specs=tuple(vmem_specs(3)),
        scratch_shapes=[pltpu.VMEM((geo.parts, geo.tiles, LANES, geo.tile), bf16)],
        compiler_params=pltpu.CompilerParams(vmem_limit_bytes=48 * 2**20),
        name="attention_forward",
    )(scalars, q, kv, bounds)


def attention_backward(geo, scalars, q, kv, do, bounds, ot, lse):
    return pl.pallas_call(
        functools.partial(backward_kernel, geo),
        out_shape=(
            jax.ShapeDtypeStruct(q.shape, bf16),
            jax.ShapeDtypeStruct(kv.shape, f32),
        ),
        in_specs=[pl.BlockSpec(memory_space=pltpu.SMEM)] + vmem_specs(6),
        out_specs=tuple(vmem_specs(2)),
        scratch_shapes=[pltpu.VMEM((geo.parts, geo.tiles, LANES, geo.tile), bf16)],
        compiler_params=pltpu.CompilerParams(vmem_limit_bytes=48 * 2**20),
        name="attention_backward",
    )(scalars, q, kv, do, bounds, ot, lse)


def gather_head(x):
    return lax.all_gather(x, "head", axis=0, tiled=False)


def exchange(x, axis):
    return lax.all_to_all(x, axis, split_axis=0, concat_axis=0, tiled=True)


def on_device(
    layer_input,
    segments,
    token_valid,
    attention_gain,
    attention_shift,
    project_weight,
    project_bias,
    output_weight,
    output_bias,
    feed_gain,
    feed_shift,
    up_weight,
    up_bias,
    down_weight,
    down_bias,
    cotangent,
):
    heads = lax.axis_size("head")
    blocks = lax.axis_size("blk")
    my_head = lax.axis_index("head")
    my_blk = lax.axis_index("blk")
    devices = heads * blocks
    seqs, _, sub, width = layer_input.shape
    hidden_width = up_weight.shape[1]
    hidden_slice = hidden_width // heads
    rows = sub * heads
    length = rows * blocks
    mine = seqs * sub
    tokens = seqs * rows
    local = H // heads
    cols = local * HD
    parts = blocks // (seqs * local)
    run = sub // parts
    part_rows = heads * run
    half = part_rows // 2
    w_rows = width // devices
    f_rows = hidden_width // devices
    geo = AttentionShape(blocks, part_rows, parts, run, sub)

    wp = project_weight.reshape(w_rows, 3, heads, local, HD)
    wq = wp[:, 0].transpose(1, 0, 2, 3).reshape(heads, w_rows, cols)
    wq = jnp.pad(wq, ((0, 0), (0, 0), (0, LANES - cols)))
    wkv = wp[:, 1:].transpose(2, 3, 0, 1, 4).reshape(heads, local * w_rows, LANES)
    small = [attention_gain, attention_shift, output_bias, feed_gain, feed_shift, down_bias]
    small += [project_bias, up_bias]
    counts = [v.shape[0] for v in small]
    small = jnp.concatenate(small)
    small_rows = -(-small.shape[0] // LANES)
    small = jnp.pad(small, (0, small_rows * LANES - small.shape[0])).reshape(1, small_rows, LANES)
    chunk = jnp.concatenate([wq, wkv, jnp.broadcast_to(small, (heads, small_rows, LANES))], axis=1)
    chunk_rows = chunk.shape[1]
    send = jnp.broadcast_to(chunk[:, None], (heads, blocks, chunk_rows, LANES))
    got = exchange(send.reshape(devices, chunk_rows, LANES), BOTH)
    w_groups = [
        got[:, i * w_rows : (i + 1) * w_rows].reshape(width, LANES) for i in range(1 + local)
    ]
    w_slice = jnp.concatenate(w_groups, axis=1)
    flat = got[:, (1 + local) * w_rows :].reshape(devices, small_rows * LANES).astype(f32)
    vectors = []
    at = 0
    for count in counts:
        vectors.append(flat[:, at : at + count].reshape(-1))
        at += count
    gain_one, shift_one, b_output, gain_two, shift_two, b_down, b_project, b_up = vectors

    x_mine = layer_input.reshape(mine, width)
    g_mine = cotangent.reshape(mine, width)
    x_all = gather_head(x_mine).reshape(heads, seqs, sub, width).transpose(1, 0, 2, 3)
    g_all = gather_head(g_mine).reshape(heads, seqs, sub, width).transpose(1, 0, 2, 3)
    x_all = x_all.reshape(tokens, width).astype(f32)
    g_all = g_all.reshape(tokens, width)

    up_parts = up_weight.reshape(w_rows, heads, hidden_slice).transpose(1, 0, 2)
    out_parts = jnp.broadcast_to(output_weight[None], (heads, w_rows, width))
    if hidden_slice == width:
        both = exchange(jnp.concatenate([up_parts, out_parts], axis=1), "head")
        shard = jnp.concatenate([both.reshape(2 * heads * w_rows, width), down_weight], axis=0)
        full = lax.all_gather(shard, "blk", axis=0, tiled=False)
        pair = full[:, : 2 * heads * w_rows].reshape(blocks, heads, 2, w_rows, width)
        w_up = pair[:, :, 0].transpose(1, 0, 2, 3).reshape(width, hidden_slice)
        w_out = pair[:, :, 1].transpose(1, 0, 2, 3).reshape(width, width)
        w_down = full[:, 2 * heads * w_rows :].reshape(hidden_slice, width)
    else:
        up_parts = lax.all_gather(exchange(up_parts, "head"), "blk", axis=0, tiled=False)
        out_parts = lax.all_gather(exchange(out_parts, "head"), "blk", axis=0, tiled=False)
        w_up = up_parts.transpose(1, 0, 2, 3).reshape(width, hidden_slice)
        w_out = out_parts.transpose(1, 0, 2, 3).reshape(width, width)
        w_down = lax.all_gather(down_weight, "blk", axis=0, tiled=True)

    n_one, u_one, rs_one = norm_forward(x_all, gain_one, shift_one)
    n_one = n_one.astype(bf16)
    qkv = dot_nn(n_one, w_slice)
    b_q = lax.dynamic_slice(b_project, (my_head * cols,), (cols,))
    b_v = lax.dynamic_slice(b_project, (width + my_head * cols,), (cols,))
    queries = (qkv[:, :cols] + b_q).astype(bf16)
    pairs = qkv[:, LANES:].reshape(tokens, local, 2, HD)
    b_pair = jnp.stack([jnp.zeros((local, HD), f32), b_v.reshape(local, HD)], axis=1)
    pairs = (pairs + b_pair).astype(bf16)
    queries = queries.reshape(seqs, heads, parts, run, local, HD).transpose(0, 4, 2, 1, 3, 5)
    queries = queries.reshape(blocks, 2, half, HD).transpose(0, 2, 1, 3).reshape(blocks, half, LANES)
    pairs = pairs.reshape(seqs, heads, parts, run, local, LANES).transpose(0, 4, 2, 1, 3, 5)
    pairs = pairs.reshape(blocks, part_rows, LANES)
    got = exchange(jnp.concatenate([queries, pairs], axis=1), "blk")
    q_task = got[:, :half]
    kv_parts = [got[:, half:]]
    for step in range(1, parts):
        around = [
            (t * parts + i, t * parts + (i + step) % parts)
            for t in range(blocks // parts)
            for i in range(parts)
        ]
        kv_parts.append(lax.ppermute(kv_parts[0], "blk", around))
    kv_task = jnp.stack(kv_parts).reshape(parts, geo.tiles, geo.tile, LANES)

    my_part = my_blk % parts
    my_seq = (my_blk // parts) // local
    seg = lax.dynamic_index_in_dim(segments, my_seq, 0, keepdims=False)
    valid = jnp.sum(lax.dynamic_index_in_dim(token_valid, my_seq, 0, keepdims=False))
    index = jnp.arange(blocks * part_rows, dtype=i32)
    own = (index // run) * sub + my_part * run + index % run
    own_seg = lax.dynamic_index_in_dim(seg.reshape(length // sub, parts, run), my_part, 1, False)
    start = jnp.sum((seg[None, :] < own_seg.reshape(-1)[:, None]).astype(i32), axis=1)
    last = jnp.minimum(own, valid - 1)
    bounds = jnp.stack([start, last, own]).reshape(3, geo.tiles, geo.tile).transpose(1, 0, 2)
    bounds = jnp.pad(bounds, ((0, 0), (0, 5), (0, 0)))
    first_seg = seg.reshape(geo.tiles, geo.span)[:, :1]
    first_tile = jnp.sum((seg[None, :] < first_seg).astype(i32), axis=1) // geo.span
    part_at = ((my_part - jnp.arange(parts, dtype=i32)) % parts) * run
    scalars = jnp.concatenate([part_at, first_tile])

    o_task, ot, lse = attention_forward(geo, scalars, q_task, kv_task, bounds)

    got = exchange(o_task, "blk")
    mixed = got.reshape(seqs, local, parts, half, 2, HD).transpose(0, 1, 2, 4, 3, 5)
    mixed = mixed.reshape(seqs, local, parts, heads, run, HD).transpose(0, 3, 2, 4, 1, 5)
    mixed = mixed.reshape(tokens, cols)
    mixed_all = lax.all_gather(mixed, "head", axis=1, tiled=True)

    middle = x_all + dot_nn(mixed_all, w_out) + b_output
    n_two, u_two, rs_two = norm_forward(middle, gain_two, shift_two)
    n_two = n_two.astype(bf16)
    b_up_slice = lax.dynamic_slice(b_up, (my_head * hidden_slice,), (hidden_slice,))
    hidden = dot_nn(n_two, w_up) + b_up_slice
    sigma = jax.nn.sigmoid(1.702 * hidden)
    activated = (hidden * sigma).astype(bf16)
    feed = dot_nn(activated, w_down)
    grad_act = dot_nt(g_all, w_down)
    grad_hidden = (grad_act * (sigma + 1.702 * hidden * sigma * (1.0 - sigma))).astype(bf16)
    grad_two = dot_nt(grad_hidden, w_up)

    def to_owners(partial):
        partial = partial.astype(bf16).reshape(seqs, heads, sub, width).transpose(1, 0, 2, 3)
        return exchange(partial.reshape(heads, mine, width), "head")

    def my_tokens(values):
        values = values.reshape(seqs, heads, sub, values.shape[-1])
        values = lax.dynamic_index_in_dim(values, my_head, 1, keepdims=False)
        return values.reshape(mine, values.shape[-1])

    grad_two_mine = jnp.sum(to_owners(grad_two).astype(f32), axis=0)
    grad_middle = g_mine.astype(f32) + norm_input_grad(
        grad_two_mine, my_tokens(u_two), my_tokens(rs_two), gain_two
    )
    grad_branch = grad_middle.astype(bf16)
    grad_mixed = dot_nt(grad_branch, w_out).astype(bf16)
    grad_mixed = grad_mixed.reshape(seqs, parts, run, heads, local, HD).transpose(3, 0, 4, 1, 2, 5)
    grad_mixed = grad_mixed.reshape(heads, blocks, run // 2 * LANES // HD // 2 * 2, HD)
    grad_mixed = grad_mixed.reshape(devices, run * HD // LANES, LANES)
    got = exchange(grad_mixed, BOTH)
    do_task = got.reshape(heads, blocks, run, HD).transpose(1, 0, 2, 3)
    do_task = do_task.reshape(blocks, 2, half, HD).transpose(0, 2, 1, 3)
    do_task = do_task.reshape(blocks, half, LANES)

    feed_mine = jnp.sum(to_owners(feed).astype(f32), axis=0)
    layer_output = my_tokens(middle) + feed_mine + b_down

    grad_down = dot_tn(activated, g_all).astype(bf16).reshape(blocks, -1, width)
    grad_up = dot_tn(n_two, grad_hidden).astype(bf16)
    grad_up = grad_up.reshape(heads, blocks, w_rows, hidden_slice).transpose(1, 0, 2, 3)
    branch_all = gather_head(grad_branch).reshape(heads, seqs, sub, width).transpose(1, 0, 2, 3)
    grad_out = dot_tn(mixed, branch_all.reshape(tokens, width)).astype(bf16)

    def over_blocks(partial):
        return lax.psum_scatter(partial, "blk", scatter_dimension=0, tiled=True)

    if hidden_slice == width:
        summed = over_blocks(
            jnp.concatenate(
                [grad_down.reshape(blocks, f_rows, width), grad_up.reshape(blocks, -1, width)],
                axis=1,
            ).reshape(-1, width)
        )
        own_down = summed[:f_rows]
        own_up = summed[f_rows:]
    else:
        own_down = over_blocks(grad_down.reshape(-1, width))
        own_up = over_blocks(grad_up.reshape(-1, hidden_slice))
    own_out = over_blocks(grad_out)
    own_up = exchange(own_up.reshape(heads, w_rows, hidden_slice), "head")
    own_up = own_up.transpose(1, 0, 2).reshape(w_rows, hidden_width)

    dq_task, dkv_task = attention_backward(geo, scalars, q_task, kv_task, do_task, bounds, ot, lse)
    dkv_task = dkv_task.reshape(parts, blocks, part_rows, LANES)
    dkv = dkv_task[0]
    for step in range(1, parts):
        around = [
            (t * parts + i, t * parts + (i - step) % parts)
            for t in range(blocks // parts)
            for i in range(parts)
        ]
        dkv = dkv + lax.ppermute(dkv_task[step].astype(bf16), "blk", around).astype(f32)
    dkv = dkv * 1.0
    got = exchange(jnp.concatenate([dq_task, dkv.astype(bf16)], axis=1), "blk")
    dq = got[:, :half].reshape(blocks, half, 2, HD).transpose(0, 2, 1, 3)
    dq = dq.reshape(seqs, local, parts, heads, run, HD).transpose(0, 3, 2, 4, 1, 5)
    dq = dq.reshape(tokens, cols)
    dkv = got[:, half:].reshape(seqs, local, parts, heads, run, LANES).transpose(0, 3, 2, 4, 1, 5)
    dkv = dkv.reshape(tokens, local * LANES)
    dq = jnp.pad(dq, ((0, 0), (0, LANES - cols)))
    d_proj = jnp.concatenate([dq, dkv], axis=1)

    grad_one = dot_nt(d_proj, w_slice)
    grad_one_mine = jnp.sum(to_owners(grad_one).astype(f32), axis=0)
    x_f32 = x_mine.astype(f32)
    input_grad = grad_middle + norm_input_grad(
        grad_one_mine, my_tokens(u_one), my_tokens(rs_one), gain_one
    )

    grad_w = dot_tn(n_one, d_proj).astype(bf16)
    col_sums = jnp.sum(d_proj.astype(f32), axis=0)
    bias_q = col_sums[:cols]
    bias_v = col_sums[LANES:].reshape(local, 2, HD)[:, 1].reshape(cols)
    bias_grad = jnp.zeros((2 * width,), f32)
    bias_grad = lax.dynamic_update_slice(bias_grad, bias_q, (my_head * cols,))
    bias_grad = lax.dynamic_update_slice(bias_grad, bias_v, (width + my_head * cols,))
    up_bias_grad = lax.dynamic_update_slice(
        jnp.zeros((hidden_width,), f32),
        jnp.sum(grad_hidden.astype(f32), axis=0),
        (my_head * hidden_slice,),
    )
    tiny = [
        jnp.sum(grad_one * u_one, axis=0),
        jnp.sum(grad_one, axis=0),
        jnp.sum(grad_branch.astype(f32), axis=0),
        jnp.sum(grad_two * u_two, axis=0),
        jnp.sum(grad_two, axis=0),
        jnp.sum(g_mine.astype(f32), axis=0),
        bias_grad,
        up_bias_grad,
    ]
    tiny = jnp.concatenate([v.reshape(devices, -1) for v in tiny], axis=1)
    high = tiny.astype(bf16)
    low = (tiny - high.astype(f32)).astype(bf16)
    tiny = jnp.concatenate([high, low], axis=1)
    tiny_rows = -(-tiny.shape[1] // LANES)
    tiny = jnp.pad(tiny, ((0, 0), (0, tiny_rows * LANES - tiny.shape[1])))
    tiny = tiny.reshape(devices, tiny_rows, LANES)
    grad_w = [
        grad_w[:, i * LANES : (i + 1) * LANES].reshape(devices, w_rows, LANES)
        for i in range(1 + local)
    ]
    got = exchange(jnp.concatenate(grad_w + [tiny], axis=1), BOTH)
    got = got.astype(f32)
    n_w = (1 + local) * w_rows
    own_w = jnp.sum(got[:, :n_w].reshape(heads, blocks, n_w, LANES), axis=1)
    own_q = own_w[:, :w_rows, :cols].transpose(1, 0, 2).reshape(w_rows, width)
    own_kv = own_w[:, w_rows:].reshape(heads, local, w_rows, 2, HD)
    own_kv = own_kv.transpose(2, 3, 0, 1, 4).reshape(w_rows, 2 * width)
    own_w = jnp.concatenate([own_q, own_kv], axis=1)
    summed = jnp.sum(got[:, n_w:].reshape(devices, -1), axis=0)
    total = sum(counts)
    summed = summed[:total] + summed[total : 2 * total]
    owned = []
    at = 0
    for count in counts:
        owned.append(summed[at : at + count])
        at += count

    return (
        layer_output.astype(bf16).reshape(layer_input.shape),
        input_grad.astype(bf16).reshape(layer_input.shape),
        owned[0],
        owned[1],
        own_w,
        owned[6],
        own_out.astype(f32),
        owned[2],
        owned[3],
        owned[4],
        own_up.astype(f32),
        owned[7],
        own_down.astype(f32),
        owned[5],
    )


def solution(mesh):
    tokens = P(None, "blk", "head", None)
    vector = P(BOTH)
    matrix = P(BOTH, None)
    return jax.shard_map(
        on_device,
        mesh=mesh,
        in_specs=(
            tokens,
            P(),
            P(),
            vector,
            vector,
            matrix,
            vector,
            matrix,
            vector,
            vector,
            vector,
            matrix,
            vector,
            matrix,
            vector,
            tokens,
        ),
        out_specs=(
            tokens,
            tokens,
            vector,
            vector,
            matrix,
            vector,
            matrix,
            vector,
            vector,
            vector,
            matrix,
            vector,
            matrix,
            vector,
        ),
        check_vma=False,
    )
```

```python
import functools

import jax
import jax.numpy as jnp
from jax import lax
from jax.experimental import pallas as pl
from jax.experimental.pallas import tpu as pltpu
from jax.sharding import PartitionSpec as P

H = 8
HD = 64
LANES = 128
EPSILON = 1e-05
NEG_FILL = -1e30
TILE_Q = 256

bf16 = jnp.bfloat16
f32 = jnp.float32
i32 = jnp.int32
BOTH = ("head", "blk")


def dot_nn(a, b):
    return lax.dot_general(a, b, (((1,), (0,)), ((), ())), preferred_element_type=f32)


def dot_nt(a, b):
    return lax.dot_general(a, b, (((1,), (1,)), ((), ())), preferred_element_type=f32)


def dot_tn(a, b):
    return lax.dot_general(a, b, (((0,), (0,)), ((), ())), preferred_element_type=f32)


def norm_forward(values, gain, shift):
    centred = values - jnp.mean(values, axis=-1, keepdims=True)
    variance = jnp.mean(centred * centred, axis=-1, keepdims=True)
    inverse_root = lax.rsqrt(variance + EPSILON)
    unit_value = centred * inverse_root
    return (unit_value * gain + shift, unit_value, inverse_root)


def norm_input_grad(upstream, unit_value, inverse_root, gain):
    scaled = upstream * gain
    inner = scaled - jnp.mean(scaled, axis=-1, keepdims=True)
    inner = inner - unit_value * jnp.mean(scaled * unit_value, axis=-1, keepdims=True)
    return inverse_root * inner


class AttentionShape:
    def __init__(self, blocks, part_rows, parts, run, stride):
        self.blocks = blocks
        self.per_tile = max(1, TILE_Q // part_rows)
        self.tiles = blocks // self.per_tile
        self.tile = self.per_tile * part_rows
        self.part_rows = part_rows
        self.half = part_rows // 2
        self.parts = parts
        self.run = run
        self.stride = stride
        self.span = self.tile * parts


def unpack_rows(packed):
    return jnp.concatenate([packed[:, :HD], packed[:, HD:]], axis=0)


def pack_rows(rows):
    half = rows.shape[0] // 2
    return jnp.concatenate([rows[:half], rows[half:]], axis=1)


def key_base(geo):
    rows = lax.broadcasted_iota(i32, (geo.tile, 1), 0)
    return (rows // geo.run) * geo.stride + rows % geo.run


def task_tile(ref, geo, tile, first, count):
    block = ref[pl.ds(tile * geo.per_tile, geo.per_tile), first : first + count, :]
    return block.reshape(geo.per_tile * count, LANES)


def forward_kernel(geo, scal_ref, *refs):
    part_refs = refs[: geo.parts]
    bounds_ref, out_ref, ot_ref, lse_ref, kvt_ref = refs[geo.parts :]
    base = jnp.broadcast_to(key_base(geo), (geo.tile, geo.tile))
    for part in range(geo.parts):
        for tile in range(geo.tiles):
            keys = task_tile(part_refs[part], geo, tile, geo.half, geo.part_rows)
            kvt_ref[part, tile] = keys.T
    for tile in range(geo.tiles):
        q = unpack_rows(task_tile(part_refs[0], geo, tile, 0, geo.half))
        q = q * jnp.asarray(HD**-0.5, bf16)
        qz = jnp.concatenate([q, jnp.zeros_like(q)], axis=1)
        start = bounds_ref[tile, 0:1]
        last = bounds_ref[tile, 1:2]
        own = bounds_ref[tile, 2:3]

        def chunk(part, key_tile, carry, diagonal):
            run_max, run_sum, acc = carry
            offset = key_tile * geo.span + scal_ref[part]
            keys = task_tile(part_refs[part], geo, key_tile, geo.half, geo.part_rows)
            scores = dot_nt(keys, qz)
            allowed = (base >= start - offset) & (base <= last - offset)
            if diagonal:
                allowed = allowed | (base == own - offset)
            masked = jnp.where(allowed, scores, NEG_FILL)
            new_max = jnp.maximum(run_max, jnp.max(masked, axis=0, keepdims=True))
            factor = jnp.exp(run_max - new_max)
            probs = jnp.where(allowed, jnp.exp(masked - new_max), 0.0)
            new_sum = run_sum * factor + jnp.sum(probs, axis=0, keepdims=True)
            acc = acc * factor + dot_nn(kvt_ref[part, key_tile], probs.astype(bf16))
            return (new_max, new_sum, acc)

        carry = (
            jnp.full((1, geo.tile), NEG_FILL, f32),
            jnp.zeros((1, geo.tile), f32),
            jnp.zeros((2 * HD, geo.tile), f32),
        )
        for part in range(geo.parts):
            carry = chunk(part, tile, carry, True)

        def earlier(key_tile, carry):
            for part in range(geo.parts):
                carry = chunk(part, key_tile, carry, False)
            return carry

        carry = lax.fori_loop(scal_ref[geo.parts + tile], tile, earlier, carry)
        run_max, run_sum, acc = carry
        attended = acc[HD:] / run_sum
        ot_ref[tile] = attended
        lse_ref[tile] = jnp.broadcast_to(run_max + jnp.log(run_sum), (8, geo.tile))
        packed = pack_rows(attended.T).astype(bf16)
        for i in range(geo.per_tile):
            out_ref[tile * geo.per_tile + i] = packed[i * geo.half : (i + 1) * geo.half]


def backward_kernel(geo, do_tile, scal_ref, *refs):
    part_refs = refs[: geo.parts]
    do_ref, bounds_ref, ot_ref, lse_ref, dq_ref = refs[geo.parts : geo.parts + 5]
    grad_refs = refs[geo.parts + 5 : 2 * geo.parts + 5]
    acc_ref, kvt_ref = refs[2 * geo.parts + 5 :]
    base = jnp.broadcast_to(key_base(geo), (geo.tile, geo.tile))
    acc_ref[...] = jnp.zeros_like(acc_ref)
    for part in range(geo.parts):
        for tile in range(geo.tiles):
            keys = task_tile(part_refs[part], geo, tile, geo.half, geo.part_rows)
            kvt_ref[part, tile] = keys.T
    for tile in range(geo.tiles):
        q = unpack_rows(task_tile(part_refs[0], geo, tile, 0, geo.half))
        q = q * jnp.asarray(HD**-0.5, bf16)
        do = unpack_rows(do_tile(do_ref, geo, tile))
        zeros = jnp.zeros_like(q)
        qz = jnp.concatenate([q, zeros], axis=1)
        doz = jnp.concatenate([zeros, do], axis=1)
        delta = jnp.sum(do.astype(f32).T * ot_ref[tile], axis=0, keepdims=True)
        log_total = lse_ref[tile, 0:1]
        start = bounds_ref[tile, 0:1]
        last = bounds_ref[tile, 1:2]
        own = bounds_ref[tile, 2:3]

        def chunk(part, key_tile, acc, diagonal):
            offset = key_tile * geo.span + scal_ref[part]
            keys = task_tile(part_refs[part], geo, key_tile, geo.half, geo.part_rows)
            scores = dot_nt(keys, qz)
            allowed = (base >= start - offset) & (base <= last - offset)
            if diagonal:
                allowed = allowed | (base == own - offset)
            probs = jnp.where(allowed, jnp.exp(scores - log_total), 0.0)
            grad_probs = dot_nt(keys, doz)
            grad_scores = (probs * (grad_probs - delta)).astype(bf16)
            acc_ref[part, key_tile] += dot_nn(grad_scores, qz) + dot_nn(probs.astype(bf16), doz)
            return acc + dot_nn(kvt_ref[part, key_tile], grad_scores)

        acc = jnp.zeros((2 * HD, geo.tile), f32)
        for part in range(geo.parts):
            acc = chunk(part, tile, acc, True)

        def earlier(key_tile, acc):
            for part in range(geo.parts):
                acc = chunk(part, key_tile, acc, False)
            return acc

        acc = lax.fori_loop(scal_ref[geo.parts + tile], tile, earlier, acc)
        packed = pack_rows((acc[:HD] * (HD**-0.5)).T).astype(bf16)
        for i in range(geo.per_tile):
            dq_ref[tile * geo.per_tile + i] = packed[i * geo.half : (i + 1) * geo.half]
    for part in range(geo.parts):
        for tile in range(geo.tiles):
            for i in range(geo.per_tile):
                rows = acc_ref[part, tile, i * geo.part_rows : (i + 1) * geo.part_rows]
                grad_refs[part][tile * geo.per_tile + i] = rows.astype(grad_refs[part].dtype)


VMEM_LIMIT = 16 * 2**20


def far(shape, dtype):
    return (pltpu.HBM(shape, dtype),)


def local_call(kernel, name, scalars, arrays, outs, scratch=(), flops=10**8):
    return pl.pallas_call(
        kernel,
        out_shape=tuple(o[0] if len(o) == 1 else jax.ShapeDtypeStruct(*o) for o in outs),
        in_specs=[pl.BlockSpec(memory_space=pltpu.SMEM)]
        + [pl.BlockSpec(memory_space=pltpu.VMEM)] * len(arrays),
        out_specs=tuple([pl.BlockSpec(memory_space=pltpu.VMEM)] * len(outs)),
        scratch_shapes=list(scratch),
        compiler_params=pltpu.CompilerParams(vmem_limit_bytes=VMEM_LIMIT),
        cost_estimate=pl.CostEstimate(flops=flops, bytes_accessed=10**6, transcendentals=0),
        name=name,
    )(scalars, *arrays)


def attention_forward(geo, scalars, part_arrays, bounds):
    return local_call(
        functools.partial(forward_kernel, geo),
        "attention_forward",
        scalars,
        [*part_arrays, bounds],
        [
            ((geo.blocks, geo.half, LANES), bf16),
            far((geo.tiles, HD, geo.tile), f32),
            far((geo.tiles, 8, geo.tile), f32),
        ],
        [pltpu.VMEM((geo.parts, geo.tiles, LANES, geo.tile), bf16)],
        flops=30 * 10**9,
    )


def attention_backward(geo, do_tile, scalars, part_arrays, do, bounds, ot, lse):
    grads = [((geo.blocks, geo.part_rows, LANES), f32)]
    grads += [((geo.blocks, geo.part_rows, LANES), bf16)] * (geo.parts - 1)
    return local_call(
        functools.partial(backward_kernel, geo, do_tile),
        "attention_backward",
        scalars,
        [*part_arrays, do, bounds, ot, lse],
        [((geo.blocks, geo.half, LANES), bf16), *grads],
        [
            pltpu.VMEM((geo.parts, geo.tiles, geo.tile, LANES), f32),
            pltpu.VMEM((geo.parts, geo.tiles, LANES, geo.tile), bf16),
        ],
        flops=30 * 10**9,
    )


def do_tile_grouped(do_ref, geo, tile):
    heads = do_ref.shape[0] // geo.blocks
    pieces = []
    for i in range(geo.per_tile):
        for head in range(heads):
            pieces.append(do_ref[head * geo.blocks + tile * geo.per_tile + i])
    return jnp.concatenate(pieces, axis=0)


def do_tile_plain(do_ref, geo, tile):
    return task_tile(do_ref, geo, tile, 0, geo.half)


def query_positions(blocks, heads, run, sub, part, geo):
    half = run // 2
    block = jnp.arange(blocks, dtype=i32).reshape(geo.tiles, 1, geo.per_tile, 1, 1)
    upper = jnp.arange(2, dtype=i32).reshape(1, 2, 1, 1, 1)
    head = jnp.arange(heads, dtype=i32).reshape(1, 1, 1, heads, 1)
    row = jnp.arange(half, dtype=i32).reshape(1, 1, 1, 1, half)
    at = block * (heads * sub) + head * sub + part * run + upper * half + row
    return at.reshape(geo.tiles, 1, geo.tile)


def attention_bounds(segments, token_valid, my_seq, my_part, geo, heads, sub):
    seg = lax.dynamic_index_in_dim(segments, my_seq, 0, keepdims=False)
    valid = jnp.sum(lax.dynamic_index_in_dim(token_valid, my_seq, 0, keepdims=False))
    own = query_positions(geo.blocks, heads, geo.run, sub, my_part, geo)
    half = geo.run // 2
    own_seg = seg.reshape(geo.blocks * heads, geo.parts, geo.run)
    own_seg = lax.dynamic_index_in_dim(own_seg, my_part, 1, keepdims=False)
    own_seg = own_seg.reshape(geo.tiles, geo.per_tile, heads, 2, half).transpose(0, 3, 1, 2, 4)
    own_seg = own_seg.reshape(-1, 1)
    start = jnp.sum((seg[None, :] < own_seg).astype(i32), axis=1).reshape(geo.tiles, 1, geo.tile)
    last = jnp.minimum(own, valid - 1)
    bounds = jnp.concatenate([start, last, own, jnp.zeros((geo.tiles, 5, geo.tile), i32)], axis=1)
    first_seg = seg.reshape(geo.tiles, geo.span)[:, :1]
    first_tile = jnp.sum((seg[None, :] < first_seg).astype(i32), axis=1) // geo.span
    part_at = ((my_part - jnp.arange(geo.parts, dtype=i32)) % geo.parts) * geo.run
    return jnp.concatenate([part_at, first_tile]), bounds


def gather_head(x):
    return lax.all_gather(x, "head", axis=0, tiled=False)


def exchange(x, axis):
    return lax.all_to_all(x, axis, split_axis=0, concat_axis=0, tiled=True)


def within_group(blocks, parts, step):
    return [
        (t * parts + i, t * parts + (i + step) % parts)
        for t in range(blocks // parts)
        for i in range(parts)
    ]


def on_device_general(
    layer_input,
    segments,
    token_valid,
    attention_gain,
    attention_shift,
    project_weight,
    project_bias,
    output_weight,
    output_bias,
    feed_gain,
    feed_shift,
    up_weight,
    up_bias,
    down_weight,
    down_bias,
    cotangent,
):
    heads = lax.axis_size("head")
    blocks = lax.axis_size("blk")
    my_head = lax.axis_index("head")
    my_blk = lax.axis_index("blk")
    devices = heads * blocks
    seqs, _, sub, width = layer_input.shape
    hidden_width = up_weight.shape[1]
    hidden_slice = hidden_width // heads
    rows = sub * heads
    length = rows * blocks
    mine = seqs * sub
    tokens = seqs * rows
    local = H // heads
    cols = local * HD
    parts = blocks // (seqs * local)
    run = sub // parts
    part_rows = heads * run
    half = part_rows // 2
    w_rows = width // devices
    f_rows = hidden_width // devices
    geo = AttentionShape(blocks, part_rows, parts, run, sub)

    wp = project_weight.reshape(w_rows, 3, heads, local, HD)
    wq = wp[:, 0].transpose(1, 0, 2, 3).reshape(heads, w_rows, cols)
    wq = jnp.pad(wq, ((0, 0), (0, 0), (0, LANES - cols)))
    wkv = wp[:, 1:].transpose(2, 3, 0, 1, 4).reshape(heads, local * w_rows, LANES)
    small = [attention_gain, attention_shift, output_bias, feed_gain, feed_shift, down_bias]
    small += [project_bias, up_bias]
    counts = [v.shape[0] for v in small]
    small = jnp.concatenate(small)
    small_rows = -(-small.shape[0] // LANES)
    small = jnp.pad(small, (0, small_rows * LANES - small.shape[0])).reshape(1, small_rows, LANES)
    chunk = jnp.concatenate([wq, wkv, jnp.broadcast_to(small, (heads, small_rows, LANES))], axis=1)
    chunk_rows = chunk.shape[1]
    send = jnp.broadcast_to(chunk[:, None], (heads, blocks, chunk_rows, LANES))
    got = exchange(send.reshape(devices, chunk_rows, LANES), BOTH)
    w_groups = [
        got[:, i * w_rows : (i + 1) * w_rows].reshape(width, LANES) for i in range(1 + local)
    ]
    w_slice = jnp.concatenate(w_groups, axis=1)
    flat = got[:, (1 + local) * w_rows :].reshape(devices, small_rows * LANES).astype(f32)
    vectors = []
    at = 0
    for count in counts:
        vectors.append(flat[:, at : at + count].reshape(-1))
        at += count
    gain_one, shift_one, b_output, gain_two, shift_two, b_down, b_project, b_up = vectors

    x_mine = layer_input.reshape(mine, width)
    g_mine = cotangent.reshape(mine, width)
    x_all = gather_head(x_mine).reshape(heads, seqs, sub, width).transpose(1, 0, 2, 3)
    g_all = gather_head(g_mine).reshape(heads, seqs, sub, width).transpose(1, 0, 2, 3)
    x_all = x_all.reshape(tokens, width).astype(f32)
    g_all = g_all.reshape(tokens, width)

    up_parts = up_weight.reshape(w_rows, heads, hidden_slice).transpose(1, 0, 2)
    out_parts = jnp.broadcast_to(output_weight[None], (heads, w_rows, width))
    if hidden_slice == width:
        both = exchange(jnp.concatenate([up_parts, out_parts], axis=1), "head")
        shard = jnp.concatenate([both.reshape(2 * heads * w_rows, width), down_weight], axis=0)
        full = lax.all_gather(shard, "blk", axis=0, tiled=False)
        pair = full[:, : 2 * heads * w_rows].reshape(blocks, heads, 2, w_rows, width)
        w_up = pair[:, :, 0].transpose(1, 0, 2, 3).reshape(width, hidden_slice)
        w_out = pair[:, :, 1].transpose(1, 0, 2, 3).reshape(width, width)
        w_down = full[:, 2 * heads * w_rows :].reshape(hidden_slice, width)
    else:
        up_parts = lax.all_gather(exchange(up_parts, "head"), "blk", axis=0, tiled=False)
        out_parts = lax.all_gather(exchange(out_parts, "head"), "blk", axis=0, tiled=False)
        w_up = up_parts.transpose(1, 0, 2, 3).reshape(width, hidden_slice)
        w_out = out_parts.transpose(1, 0, 2, 3).reshape(width, width)
        w_down = lax.all_gather(down_weight, "blk", axis=0, tiled=True)

    n_one, u_one, rs_one = norm_forward(x_all, gain_one, shift_one)
    n_one = n_one.astype(bf16)
    qkv = dot_nn(n_one, w_slice)
    b_q = lax.dynamic_slice(b_project, (my_head * cols,), (cols,))
    b_v = lax.dynamic_slice(b_project, (width + my_head * cols,), (cols,))
    queries = (qkv[:, :cols] + b_q).astype(bf16)
    pairs = qkv[:, LANES:].reshape(tokens, local, 2, HD)
    b_pair = jnp.stack([jnp.zeros((local, HD), f32), b_v.reshape(local, HD)], axis=1)
    pairs = (pairs + b_pair).astype(bf16)
    queries = queries.reshape(seqs, heads, parts, 2, run // 2, local, HD)
    queries = queries.transpose(0, 5, 2, 1, 4, 3, 6).reshape(blocks, half, LANES)
    pairs = pairs.reshape(seqs, heads, parts, run, local, LANES).transpose(0, 4, 2, 1, 3, 5)
    pairs = pairs.reshape(blocks, part_rows, LANES)
    task = exchange(jnp.concatenate([queries, pairs], axis=1), "blk")
    part_arrays = [task]
    for step in range(1, parts):
        part_arrays.append(lax.ppermute(task, "blk", within_group(blocks, parts, step)))

    my_part = my_blk % parts
    my_seq = (my_blk // parts) // local
    scalars, bounds = attention_bounds(segments, token_valid, my_seq, my_part, geo, heads, sub)
    o_task, ot, lse = attention_forward(geo, scalars, part_arrays, bounds)

    got = exchange(o_task, "blk")
    mixed = got.reshape(seqs, local, parts, heads, run // 2, 2, HD)
    mixed = mixed.transpose(0, 3, 2, 5, 4, 1, 6)
    mixed = mixed.reshape(tokens, cols)
    mixed_all = lax.all_gather(mixed, "head", axis=1, tiled=True)

    middle = x_all + dot_nn(mixed_all, w_out) + b_output
    n_two, u_two, rs_two = norm_forward(middle, gain_two, shift_two)
    n_two = n_two.astype(bf16)
    b_up_slice = lax.dynamic_slice(b_up, (my_head * hidden_slice,), (hidden_slice,))
    hidden = dot_nn(n_two, w_up) + b_up_slice
    sigma = jax.nn.sigmoid(1.702 * hidden)
    activated = (hidden * sigma).astype(bf16)
    feed = dot_nn(activated, w_down)
    grad_act = dot_nt(g_all, w_down)
    grad_hidden = (grad_act * (sigma + 1.702 * hidden * sigma * (1.0 - sigma))).astype(bf16)
    grad_two = dot_nt(grad_hidden, w_up)

    def to_owners(partial):
        partial = partial.astype(bf16).reshape(seqs, heads, sub, width).transpose(1, 0, 2, 3)
        return exchange(partial.reshape(heads, mine, width), "head")

    def my_tokens(values):
        values = values.reshape(seqs, heads, sub, values.shape[-1])
        values = lax.dynamic_index_in_dim(values, my_head, 1, keepdims=False)
        return values.reshape(mine, values.shape[-1])

    grad_two_mine = jnp.sum(to_owners(grad_two).astype(f32), axis=0)
    grad_middle = g_mine.astype(f32) + norm_input_grad(
        grad_two_mine, my_tokens(u_two), my_tokens(rs_two), gain_two
    )
    grad_branch = grad_middle.astype(bf16)
    grad_mixed = dot_nt(grad_branch, w_out).astype(bf16)
    grad_mixed = grad_mixed.reshape(seqs, parts, 2, run // 2, heads, local, HD)
    grad_mixed = grad_mixed.transpose(4, 0, 5, 1, 3, 2, 6).reshape(devices, run // 2, LANES)
    got = exchange(grad_mixed, BOTH).reshape(heads, blocks, run // 2, LANES)
    do_task = got.transpose(1, 0, 2, 3).reshape(blocks, half, LANES)

    feed_mine = jnp.sum(to_owners(feed).astype(f32), axis=0)
    layer_output = my_tokens(middle) + feed_mine + b_down

    grad_down = dot_tn(activated, g_all).astype(bf16).reshape(blocks, -1, width)
    grad_up = dot_tn(n_two, grad_hidden).astype(bf16)
    grad_up = grad_up.reshape(heads, blocks, w_rows, hidden_slice).transpose(1, 0, 2, 3)
    branch_all = gather_head(grad_branch).reshape(heads, seqs, sub, width).transpose(1, 0, 2, 3)
    grad_out = dot_tn(mixed, branch_all.reshape(tokens, width)).astype(bf16)

    def over_blocks(partial):
        return lax.psum_scatter(partial, "blk", scatter_dimension=0, tiled=True)

    if hidden_slice == width:
        summed = over_blocks(
            jnp.concatenate(
                [grad_down.reshape(blocks, f_rows, width), grad_up.reshape(blocks, -1, width)],
                axis=1,
            ).reshape(-1, width)
        )
        own_down = summed[:f_rows]
        own_up = summed[f_rows:]
    else:
        own_down = over_blocks(grad_down.reshape(-1, width))
        own_up = over_blocks(grad_up.reshape(-1, hidden_slice))
    own_out = over_blocks(grad_out)
    own_up = exchange(own_up.reshape(heads, w_rows, hidden_slice), "head")
    own_up = own_up.transpose(1, 0, 2).reshape(w_rows, hidden_width)

    dq_task, dkv, *others = attention_backward(
        geo, do_tile_plain, scalars, part_arrays, do_task, bounds, ot, lse
    )
    for step in range(1, parts):
        back = within_group(blocks, parts, -step)
        dkv = dkv + lax.ppermute(others[step - 1], "blk", back).astype(f32)
    got = exchange(jnp.concatenate([dq_task, dkv.astype(bf16)], axis=1), "blk")
    dq = got[:, :half].reshape(seqs, local, parts, heads, run // 2, 2, HD)
    dq = dq.transpose(0, 3, 2, 5, 4, 1, 6)
    dq = dq.reshape(tokens, cols)
    dkv = got[:, half:].reshape(seqs, local, parts, heads, run, LANES).transpose(0, 3, 2, 4, 1, 5)
    dkv = dkv.reshape(tokens, local * LANES)
    dq = jnp.pad(dq, ((0, 0), (0, LANES - cols)))
    d_proj = jnp.concatenate([dq, dkv], axis=1)

    grad_one = dot_nt(d_proj, w_slice)
    grad_one_mine = jnp.sum(to_owners(grad_one).astype(f32), axis=0)
    x_f32 = x_mine.astype(f32)
    input_grad = grad_middle + norm_input_grad(
        grad_one_mine, my_tokens(u_one), my_tokens(rs_one), gain_one
    )

    grad_w = dot_tn(n_one, d_proj).astype(bf16)
    col_sums = jnp.sum(d_proj.astype(f32), axis=0)
    bias_q = col_sums[:cols]
    bias_v = col_sums[LANES:].reshape(local, 2, HD)[:, 1].reshape(cols)
    bias_grad = jnp.zeros((2 * width,), f32)
    bias_grad = lax.dynamic_update_slice(bias_grad, bias_q, (my_head * cols,))
    bias_grad = lax.dynamic_update_slice(bias_grad, bias_v, (width + my_head * cols,))
    up_bias_grad = lax.dynamic_update_slice(
        jnp.zeros((hidden_width,), f32),
        jnp.sum(grad_hidden.astype(f32), axis=0),
        (my_head * hidden_slice,),
    )
    tiny = [
        jnp.sum(grad_one * u_one, axis=0),
        jnp.sum(grad_one, axis=0),
        jnp.sum(grad_branch.astype(f32), axis=0),
        jnp.sum(grad_two * u_two, axis=0),
        jnp.sum(grad_two, axis=0),
        jnp.sum(g_mine.astype(f32), axis=0),
        bias_grad,
        up_bias_grad,
    ]
    tiny = jnp.concatenate([v.reshape(devices, -1) for v in tiny], axis=1)
    high = tiny.astype(bf16)
    low = (tiny - high.astype(f32)).astype(bf16)
    tiny = jnp.concatenate([high, low], axis=1)
    tiny_rows = -(-tiny.shape[1] // LANES)
    tiny = jnp.pad(tiny, ((0, 0), (0, tiny_rows * LANES - tiny.shape[1])))
    tiny = tiny.reshape(devices, tiny_rows, LANES)
    grad_w = [
        grad_w[:, i * LANES : (i + 1) * LANES].reshape(devices, w_rows, LANES)
        for i in range(1 + local)
    ]
    got = exchange(jnp.concatenate(grad_w + [tiny], axis=1), BOTH)
    got = got.astype(f32)
    n_w = (1 + local) * w_rows
    own_w = jnp.sum(got[:, :n_w].reshape(heads, blocks, n_w, LANES), axis=1)
    own_q = own_w[:, :w_rows, :cols].transpose(1, 0, 2).reshape(w_rows, width)
    own_kv = own_w[:, w_rows:].reshape(heads, local, w_rows, 2, HD)
    own_kv = own_kv.transpose(2, 3, 0, 1, 4).reshape(w_rows, 2 * width)
    own_w = jnp.concatenate([own_q, own_kv], axis=1)
    summed = jnp.sum(got[:, n_w:].reshape(devices, -1), axis=0)
    total = sum(counts)
    summed = summed[:total] + summed[total : 2 * total]
    owned = []
    at = 0
    for count in counts:
        owned.append(summed[at : at + count])
        at += count

    return (
        layer_output.astype(bf16).reshape(layer_input.shape),
        input_grad.astype(bf16).reshape(layer_input.shape),
        owned[0],
        owned[1],
        own_w,
        owned[6],
        own_out.astype(f32),
        owned[2],
        owned[3],
        owned[4],
        own_up.astype(f32),
        owned[7],
        own_down.astype(f32),
        owned[5],
    )


class Sizes:
    def __init__(self, heads, blocks, seqs, sub, width, hidden_width):
        self.heads = heads
        self.blocks = blocks
        self.seqs = seqs
        self.sub = sub
        self.width = width
        self.devices = heads * blocks
        self.mine = seqs * sub
        self.tokens = self.mine * heads
        self.local = H // heads
        self.parts = blocks // (seqs * self.local)
        self.run = sub // self.parts
        self.part_rows = heads * self.run
        self.half = self.part_rows // 2
        self.w_rows = width // self.devices
        self.f_rows = hidden_width // self.devices
        self.hidden_slice = hidden_width // heads
        self.w_chunk = (1 + self.local) * self.w_rows
        self.head_rows = self.blocks * self.w_rows
        self.groups = blocks // self.parts

    def fits(self):
        return (
            self.local == 2
            and self.parts == 2
            and self.run % 32 == 0
            and self.w_rows == 16
            and self.hidden_slice == self.width
            and self.mine % 16 == 0
            and self.f_rows % 16 == 0
        )

    def task(self, seq, local, part):
        return (seq * self.local + local) * self.parts + part


SMALL = 8


def slot_head(sz, scal_ref, slot):
    return lax.rem(scal_ref[0] - slot + sz.heads, sz.heads)


def halves(first, second):
    low = jnp.concatenate([first[:, :HD], second[:, :HD]], axis=1)
    high = jnp.concatenate([first[:, HD:], second[:, HD:]], axis=1)
    return low, high


def staged(count, refs):
    scratch = refs[len(refs) - count - 1 :]
    held, sems = scratch[:count], scratch[count]
    copies = [pltpu.make_async_copy(refs[i], held[i], sems.at[i]) for i in range(count)]
    for copy in copies:
        copy.start()
    for copy in copies:
        copy.wait()
    return held


def staged_call(kernel, name, scalars, arrays, outs, scratch=()):
    return pl.pallas_call(
        kernel,
        out_shape=tuple(jax.ShapeDtypeStruct(*o) for o in outs),
        in_specs=[pl.BlockSpec(memory_space=pltpu.SMEM)]
        + [pl.BlockSpec(memory_space=pltpu.HBM)] * len(arrays),
        out_specs=tuple([pl.BlockSpec(memory_space=pltpu.VMEM)] * len(outs)),
        scratch_shapes=list(scratch)
        + [pltpu.VMEM(v.shape, v.dtype) for v in arrays]
        + [pltpu.SemaphoreType.DMA((len(arrays),))],
        compiler_params=pltpu.CompilerParams(vmem_limit_bytes=63 * 2**20),
        name=name,
    )(scalars, *arrays)


def pack_kernel(sz, scal_ref, *refs):
    count = 1 + SMALL
    send_ref, small_scr = refs[count : count + 2]
    small_scr[...] = jnp.zeros_like(small_scr)
    wp_ref, *small_refs = staged(count, refs)
    for i, ref in enumerate(small_refs):
        small_scr[i : i + 1, : ref.shape[1]] = ref[...].astype(f32)
    small = small_scr[...].astype(bf16)
    for head in range(sz.heads):
        at = head * LANES
        q = wp_ref[:, at : at + LANES]
        k = wp_ref[:, sz.width + at : sz.width + at + LANES]
        v = wp_ref[:, 2 * sz.width + at : 2 * sz.width + at + LANES]
        low, high = halves(k, v)
        chunk = jnp.concatenate([q, low, high], axis=0)
        for blk in range(sz.blocks):
            send_ref[head * sz.blocks + blk, : sz.w_chunk] = chunk
            send_ref[head * sz.blocks + blk, sz.w_chunk :] = small


def pack_more_kernel(sz, scal_ref, *refs):
    tokens_ref, column_ref = refs[5:7]
    x_ref, g_ref, up_ref, wo_ref, down_ref = staged(5, refs)
    tokens_ref[: sz.mine] = x_ref[...]
    tokens_ref[sz.mine :] = g_ref[...]
    for head in range(sz.heads):
        part = up_ref[:, head * sz.hidden_slice : (head + 1) * sz.hidden_slice]
        column_ref[head * sz.w_rows : (head + 1) * sz.w_rows] = part
    at = sz.heads * sz.w_rows
    column_ref[at : at + sz.w_rows] = wo_ref[...]
    column_ref[at + sz.w_rows :] = down_ref[...]


def spread(small, per, offset, count):
    lane = lax.broadcasted_iota(i32, (LANES, count), 0)
    at = lax.broadcasted_iota(i32, (LANES, count), 1) + offset
    pick = jnp.where(at % per == lane, 1.0, 0.0).astype(bf16)
    wide = dot_nn(small, pick)
    source = lax.broadcasted_iota(i32, wide.shape, 0) // SMALL
    column = (lax.broadcasted_iota(i32, wide.shape, 1) + offset) // per
    wide = jnp.where(source == column, wide, 0.0)
    return jnp.sum(wide.reshape(-1, SMALL, count), axis=0)


def collect(values, per, offset, rows, devices):
    count = values.shape[1]
    tall = jnp.broadcast_to(values[None], (devices, SMALL, count)).reshape(devices * SMALL, count)
    row = lax.broadcasted_iota(i32, tall.shape, 0)
    column = (lax.broadcasted_iota(i32, tall.shape, 1) + offset) // per
    index = row % SMALL
    keep = (row // SMALL == column) & (index >= rows[0]) & (index < rows[1])
    tall = jnp.where(keep, tall, 0.0)
    lane = lax.broadcasted_iota(i32, (count, LANES), 1)
    at = lax.broadcasted_iota(i32, (count, LANES), 0) + offset
    pick = jnp.where(at % per == lane, 1.0, 0.0).astype(bf16)
    return dot_nn(tall.astype(bf16), pick)


def source_blk(sz, scal_ref, group_slot, part_slot):
    group = lax.rem(scal_ref[1] // sz.parts - group_slot + sz.groups, sz.groups)
    part = lax.rem(scal_ref[1] % sz.parts - part_slot + sz.parts, sz.parts)
    return group * sz.parts + part


def project_kernel(sz, scal_ref, got_ref, *refs):
    x_refs = refs[: sz.heads]
    send_ref, w_ref, vec_ref = refs[sz.heads :]
    head = scal_ref[0]
    for i in range(1 + sz.local):
        part = got_ref[:, i * sz.w_rows : (i + 1) * sz.w_rows, :]
        w_ref[:, i * LANES : (i + 1) * LANES] = part.reshape(sz.width, LANES)
    small = got_ref[:, sz.w_chunk :, :].astype(f32).reshape(-1, LANES).astype(bf16)
    vec = spread(small, sz.w_rows, 0, sz.width)
    per = 2 * sz.w_rows
    b_q = spread(small, per, head * LANES, LANES)[6:7]
    b_v = spread(small, per, sz.width + head * LANES, LANES)[6:7]
    b_up = spread(small, 4 * sz.w_rows, head * sz.hidden_slice, sz.hidden_slice)
    row = lax.broadcasted_iota(i32, vec.shape, 0)
    vec = jnp.where(row == 7, b_up, vec)
    vec_ref[...] = vec
    zero = jnp.zeros((1, HD), f32)
    bias = jnp.concatenate([b_q, zero, b_v[:, :HD], zero, b_v[:, HD:]], axis=1)
    gain, shift = vec[0:1], vec[1:2]
    for slot in range(sz.heads):
        x = x_refs[slot][: sz.mine].astype(f32)
        normed = norm_forward(x, gain, shift)[0].astype(bf16)
        qkv = (dot_nn(normed, w_ref[...]) + bias).astype(bf16)
        to = slot_head(sz, scal_ref, slot)
        half_run = sz.run // 2
        for seq in range(sz.seqs):
            for part in range(sz.parts):
                at = seq * sz.sub + part * sz.run
                low, high = halves(qkv[at : at + half_run, :LANES], qkv[at + half_run : at + sz.run, :LANES])
                packed = (low, high)
                for local in range(sz.local):
                    task = sz.task(seq, local, part)
                    q_at = pl.multiple_of(to * half_run, half_run)
                    send_ref[task, pl.ds(q_at, half_run)] = packed[local]
                    kv_at = pl.multiple_of(sz.half + to * sz.run, sz.run)
                    send_ref[task, pl.ds(kv_at, sz.run)] = qkv[
                        at : at + sz.run, (1 + local) * LANES : (2 + local) * LANES
                    ]


def regroup_kernel(sz, scal_ref, *refs):
    count = sz.parts * sz.groups
    column_refs, pay_refs, down_ref = refs[:count], refs[count:-1], refs[-1]
    for part_slot in range(sz.parts):
        for group_slot in range(sz.groups):
            ref = column_refs[part_slot * sz.groups + group_slot]
            blk = source_blk(sz, scal_ref, group_slot, part_slot)
            at = pl.multiple_of(blk * sz.f_rows, sz.f_rows)
            first = sz.heads * sz.w_rows
            down_ref[pl.ds(at, sz.f_rows)] = ref[first + sz.w_rows :]
            up_at = pl.multiple_of(blk * sz.w_rows, sz.w_rows)
            out_at = pl.multiple_of(sz.head_rows + blk * sz.w_rows, sz.w_rows)
            for step, pay_ref in enumerate(pay_refs):
                to = lax.rem(scal_ref[0] + step, sz.heads)
                from_at = pl.multiple_of(to * sz.w_rows, sz.w_rows)
                pay_ref[pl.ds(up_at, sz.w_rows)] = ref[pl.ds(from_at, sz.w_rows)]
                pay_ref[pl.ds(out_at, sz.w_rows)] = ref[first : first + sz.w_rows]


def output_weight_rows(sz, pay_refs):
    rows = slice(sz.head_rows, 2 * sz.head_rows)
    return jnp.concatenate([ref[rows] for ref in pay_refs], axis=0)


def feed_kernel(sz, scal_ref, vec_ref, down_ref, *refs):
    n = sz.heads
    x_refs, pay_refs, m_refs = refs[:n], refs[n : 2 * n], refs[2 * n : 3 * n]
    outs = refs[3 * n :]
    part_refs, feed_refs = outs[:n], outs[n : 2 * n]
    mid_ref, act_ref, dh_ref, n_ref, mix_own_ref, sum_ref, up_ref, mix_scr = outs[2 * n :]
    for slot in range(n):
        at = pl.multiple_of(slot_head(sz, scal_ref, slot) * sz.head_rows, sz.head_rows)
        up_ref[pl.ds(at, sz.head_rows)] = pay_refs[slot][: sz.head_rows]
    w_out = output_weight_rows(sz, pay_refs)
    half_run = sz.run // 2
    for slot in range(n):
        for seq in range(sz.seqs):
            for part in range(sz.parts):
                first = m_refs[slot][sz.task(seq, 0, part)]
                second = m_refs[slot][sz.task(seq, 1, part)]
                low, high = halves(first, second)
                for head in range(n):
                    at = seq * sz.sub + part * sz.run
                    cols = slice(slot * LANES, (slot + 1) * LANES)
                    rows = slice(head * half_run, (head + 1) * half_run)
                    mix_scr[head, at : at + half_run, cols] = low[rows]
                    mix_scr[head, at + half_run : at + sz.run, cols] = high[rows]
    w_down = down_ref[...]
    b_out, gain, shift, b_up = vec_ref[2:3], vec_ref[3:4], vec_ref[4:5], vec_ref[7:8]
    sums = jnp.zeros((3, sz.width), f32)
    group = 2
    for first in range(0, n, group):
        slots = range(first, first + group)
        x = jnp.concatenate([x_refs[s][: sz.mine] for s in slots], axis=0).astype(f32)
        g = jnp.concatenate([x_refs[s][sz.mine :] for s in slots], axis=0)
        mixed = jnp.concatenate([mix_scr[slot_head(sz, scal_ref, s)] for s in slots], axis=0)
        middle = x + dot_nn(mixed, w_out) + b_out
        normed, unit, _ = norm_forward(middle, gain, shift)
        normed = normed.astype(bf16)
        hidden = dot_nn(normed, up_ref[...]) + b_up
        sigma = 1.0 / (1.0 + jnp.exp(-1.702 * hidden))
        activated = (hidden * sigma).astype(bf16)
        slope = sigma + 1.702 * hidden * sigma * (1.0 - sigma)
        grad_hidden = (dot_nt(g, w_down) * slope).astype(bf16)
        grad_two = dot_nt(grad_hidden, up_ref[...])
        feed = dot_nn(activated, w_down)
        sums = sums + jnp.concatenate(
            [
                jnp.sum(grad_two * unit, axis=0, keepdims=True),
                jnp.sum(grad_two, axis=0, keepdims=True),
                jnp.sum(grad_hidden.astype(f32), axis=0, keepdims=True),
            ],
            axis=0,
        )
        for i, s in enumerate(slots):
            rows = slice(i * sz.mine, (i + 1) * sz.mine)
            part_refs[s][...] = grad_two[rows].astype(part_refs[s].dtype)
            feed_refs[s][...] = feed[rows].astype(feed_refs[s].dtype)
            if s == 0:
                mid_ref[...] = middle[rows]
                mix_own_ref[...] = mixed[rows]
            act_ref[s] = activated[rows]
            dh_ref[s] = grad_hidden[rows]
            n_ref[s] = normed[rows]
    sum_ref[...] = jnp.concatenate([sums, jnp.zeros((5, sz.width), f32)], axis=0)


def give_and_keep(sz, scal_ref, values, rows, keep_ref, give_ref):
    part = scal_ref[1] % sz.parts
    for blk in range(sz.blocks):
        group = blk // sz.parts
        piece = values(blk)
        @pl.when(part == blk % sz.parts)
        def _():
            keep_ref[group] = piece

        @pl.when(part != blk % sz.parts)
        def _():
            give_ref[group] = piece.astype(bf16)


def feed_grad_kernel(sz, scal_ref, act_ref, dh_ref, n_ref, *refs):
    g_refs = refs[: sz.heads]
    keep_ref, give_ref = refs[sz.heads :]
    g = jnp.concatenate([ref[sz.mine :] for ref in g_refs], axis=0)
    act = act_ref[...].reshape(sz.tokens, sz.hidden_slice)
    down = dot_tn(act, g)
    up = dot_tn(n_ref[...].reshape(sz.tokens, sz.width), dh_ref[...].reshape(sz.tokens, sz.hidden_slice))

    def piece(blk):
        pieces = [down[blk * sz.f_rows : (blk + 1) * sz.f_rows]]
        for head in range(sz.heads):
            at = head * sz.head_rows + blk * sz.w_rows
            pieces.append(up[at : at + sz.w_rows])
        return jnp.concatenate(pieces, axis=0)

    give_and_keep(sz, scal_ref, piece, sz.f_rows + sz.heads * sz.w_rows, keep_ref, give_ref)


def part_sum_kernel(sz, scal_ref, *refs):
    pairs, (own_ref, *piece_refs) = refs[: -sz.groups], refs[-sz.groups :]
    for step in range(sz.groups):
        to = lax.rem(scal_ref[1] // sz.parts + step, sz.groups)
        at = 0
        for keep_ref, got_ref in zip(pairs[::2], pairs[1::2]):
            total = keep_ref[to] + got_ref[to].astype(f32)
            ref = piece_refs[step - 1] if step else own_ref
            ref[at : at + total.shape[0]] = total.astype(ref.dtype)
            at += total.shape[0]


def middle_grad_kernel(sz, scal_ref, vec_ref, mid_ref, tokens_ref, *refs):
    n = sz.heads
    pay_refs, part_refs = refs[:n], refs[n : 2 * n]
    grad_ref, branch_ref, send_ref, sum_ref = refs[2 * n :]
    w_out = output_weight_rows(sz, pay_refs)
    upstream = part_refs[0][...]
    for ref in part_refs[1:]:
        upstream = upstream + ref[...].astype(f32)
    gain, shift = vec_ref[3:4], vec_ref[4:5]
    _, unit, root = norm_forward(mid_ref[...], gain, shift)
    g = tokens_ref[sz.mine :].astype(f32)
    grad = g + norm_input_grad(upstream, unit, root, gain)
    grad_ref[...] = grad
    branch = grad.astype(bf16)
    branch_ref[...] = branch
    sum_ref[...] = jnp.concatenate(
        [
            jnp.sum(branch.astype(f32), axis=0, keepdims=True),
            jnp.sum(g, axis=0, keepdims=True),
            jnp.zeros((6, sz.width), f32),
        ],
        axis=0,
    )
    mixed = dot_nt(branch, w_out).astype(bf16)
    half_run = sz.run // 2
    for slot in range(n):
        to = slot_head(sz, scal_ref, slot)
        for seq in range(sz.seqs):
            for part in range(sz.parts):
                at = seq * sz.sub + part * sz.run
                cols = slice(slot * LANES, (slot + 1) * LANES)
                packed = halves(mixed[at : at + half_run, cols], mixed[at + half_run : at + sz.run, cols])
                for local in range(sz.local):
                    send_ref[to * sz.blocks + sz.task(seq, local, part)] = packed[local]


def out_grad_kernel(sz, scal_ref, mix_ref, branch_ref, keep_ref, give_ref):
    grad = dot_tn(mix_ref[...], branch_ref[...])
    part = scal_ref[1] % sz.parts
    for slot in range(sz.heads):
        head = slot_head(sz, scal_ref, slot)
        to = pl.multiple_of(head * sz.w_rows, sz.w_rows)
        for blk in range(sz.blocks):
            at = slot * sz.head_rows + blk * sz.w_rows
            piece = grad[at : at + sz.w_rows]

            @pl.when(part == blk % sz.parts)
            def _():
                keep_ref[blk // sz.parts, pl.ds(to, sz.w_rows)] = piece

            @pl.when(part != blk % sz.parts)
            def _():
                give_ref[blk // sz.parts, pl.ds(to, sz.w_rows)] = piece.astype(bf16)


def norm_again_kernel(sz, scal_ref, vec_ref, *refs):
    x_refs = refs[: sz.heads]
    n_ref, u_ref = refs[sz.heads :]
    gain, shift = vec_ref[0:1], vec_ref[1:2]
    for slot in range(sz.heads):
        normed, unit, _ = norm_forward(x_refs[slot][: sz.mine].astype(f32), gain, shift)
        at = slice(slot * sz.mine, (slot + 1) * sz.mine)
        n_ref[:, at] = normed.astype(bf16).T
        u_ref[:, at] = unit.astype(bf16).T


def project_grad_kernel(sz, scal_ref, sum_a_ref, sum_b_ref, got_ref, w_ref, n_ref, u_ref, *refs):
    n = sz.heads
    send_ref, d_scr = refs
    half_run = sz.run // 2
    for slot in range(n):
        head = slot_head(sz, scal_ref, slot)
        q_at = pl.multiple_of(head * half_run, half_run)
        kv_at = pl.multiple_of(sz.half + head * sz.run, sz.run)
        for seq in range(sz.seqs):
            for part in range(sz.parts):
                at = slot * sz.mine + seq * sz.sub + part * sz.run
                first = got_ref[sz.task(seq, 0, part), pl.ds(q_at, half_run)]
                second = got_ref[sz.task(seq, 1, part), pl.ds(q_at, half_run)]
                low, high = halves(first, second)
                d_scr[at : at + half_run, :LANES] = low
                d_scr[at + half_run : at + sz.run, :LANES] = high
                for local in range(sz.local):
                    d_scr[at : at + sz.run, (1 + local) * LANES : (2 + local) * LANES] = got_ref[
                        sz.task(seq, local, part), pl.ds(kv_at, sz.run)
                    ]
    d_proj = d_scr[...]
    grad_w = dot_nn(n_ref[...], d_proj).astype(bf16)
    weights = w_ref[...].astype(f32)
    ones = jnp.ones((16, sz.tokens), bf16)
    column = dot_nn(ones, d_proj)[:SMALL]
    terms = [dot_nn(u_ref[...], d_proj) * weights, column[0:1] * weights]
    ones = jnp.ones((16, (1 + sz.local) * LANES), bf16)
    sums = []
    for term in terms:
        high = term.astype(bf16)
        low = (term - high.astype(f32)).astype(bf16)
        sums.append((dot_nt(ones, high) + dot_nt(ones, low))[0:1])
    sums = jnp.concatenate(sums, axis=0)
    for dev in range(sz.devices):
        rows = slice(dev * sz.w_rows, (dev + 1) * sz.w_rows)
        for i in range(1 + sz.local):
            cols = slice(i * LANES, (i + 1) * LANES)
            send_ref[dev, i * sz.w_rows : (i + 1) * sz.w_rows] = grad_w[rows, cols]
    sum_q = column[:, :LANES]
    sum_v = jnp.concatenate([column[:, LANES + HD : 2 * LANES], column[:, 2 * LANES + HD :]], axis=1)
    wide = jnp.concatenate(
        [sums, sum_b_ref[0:1], sum_a_ref[0:2], sum_b_ref[1:2], jnp.zeros((2, sz.width), f32)], axis=0
    )
    up_bias = jnp.broadcast_to(sum_a_ref[2:3], (SMALL, sz.width))
    head = scal_ref[0]
    per = sz.w_rows
    at = sz.w_chunk
    for low in (False, True):
        def level(v):
            high = v.astype(bf16).astype(f32)
            return v - high if low else high

        share = collect(level(wide), per, 0, (0, 6), sz.devices)
        share += collect(level(sum_q), 2 * per, head * LANES, (6, 7), sz.devices)
        share += collect(level(sum_v), 2 * per, sz.width + head * LANES, (6, 7), sz.devices)
        share += collect(level(up_bias), 4 * per, head * sz.hidden_slice, (7, 8), sz.devices)
        share = share.reshape(sz.devices, SMALL, LANES)
        if low:
            both = jnp.concatenate([kept, share], axis=1).astype(bf16)
        kept = share
    send_ref[:, at : at + 2 * SMALL, :] = both


def input_partial_kernel(sz, scal_ref, d_ref, w_ref, *part_refs):
    grad_one = dot_nt(d_ref[...], w_ref[...])
    for slot, ref in enumerate(part_refs):
        ref[...] = grad_one[slot * sz.mine : (slot + 1) * sz.mine].astype(ref.dtype)


def input_grad_kernel(sz, scal_ref, vec_ref, grad_ref, x_ref, *refs):
    out_ref = refs[sz.heads]
    upstream = refs[0][...]
    for ref in refs[1 : sz.heads]:
        upstream = upstream + ref[...].astype(f32)
    gain, shift = vec_ref[0:1], vec_ref[1:2]
    _, unit, root = norm_forward(x_ref[: sz.mine].astype(f32), gain, shift)
    out_ref[...] = (grad_ref[...] + norm_input_grad(upstream, unit, root, gain)).astype(bf16)


def split_kernel(sz, scal_ref, own_ref, *refs):
    n = sz.heads
    got_refs, feed_refs, refs = refs[: sz.groups - 1], refs[sz.groups - 1 :][: n - 1], refs[-n - 1 :]
    down_ref, piece_ref, *send_refs = refs

    def total(rows):
        value = own_ref[rows]
        for ref in got_refs:
            value = value + ref[rows].astype(f32)
        return value

    down_ref[...] = total(slice(0, sz.f_rows))
    for slot in range(n):
        to = slot_head(sz, scal_ref, slot)
        at = pl.multiple_of(sz.f_rows + to * sz.w_rows, sz.w_rows)
        up = total(pl.ds(at, sz.w_rows)).astype(bf16)
        out = total(pl.ds(at + n * sz.w_rows, sz.w_rows))
        ref = send_refs[slot - 1] if slot else piece_ref
        base = sz.mine if slot else 0
        if slot:
            ref[: sz.mine] = feed_refs[slot - 1][...]
        ref[base : base + sz.w_rows] = up
        ref[base + sz.w_rows :] = out.astype(bf16)


def final_kernel(sz, scal_ref, got_ref, *refs):
    piece_refs, refs = refs[: sz.heads], refs[sz.heads :]
    w_ref, up_ref, out_ref, *small_refs = refs
    out = piece_refs[0][sz.w_rows :].astype(f32)
    for ref in piece_refs[1:]:
        out = out + ref[sz.mine + sz.w_rows :].astype(f32)
    out_ref[...] = out
    for slot in range(sz.heads):
        at = pl.multiple_of(slot_head(sz, scal_ref, slot) * sz.hidden_slice, LANES)
        base = sz.mine if slot else 0
        piece = piece_refs[(sz.heads - slot) % sz.heads][base : base + sz.w_rows]
        up_ref[:, pl.ds(at, sz.hidden_slice)] = piece.astype(f32)
    for head in range(sz.heads):
        total = jnp.zeros((sz.w_chunk, LANES), f32)
        for blk in range(sz.blocks):
            total = total + got_ref[head * sz.blocks + blk, : sz.w_chunk].astype(f32)
        at = head * LANES
        w_ref[:, at : at + LANES] = total[: sz.w_rows]
        low, high = halves(total[sz.w_rows : 2 * sz.w_rows], total[2 * sz.w_rows :])
        w_ref[:, sz.width + at : sz.width + at + LANES] = low
        w_ref[:, 2 * sz.width + at : 2 * sz.width + at + LANES] = high
    small = jnp.sum(got_ref[:, sz.w_chunk :, :].astype(f32), axis=0)
    small = small[:SMALL] + small[SMALL:]
    for i, ref in enumerate(small_refs):
        ref[...] = small[i : i + 1, : ref.shape[1]]


def on_device_fused(
    sz,
    layer_input,
    segments,
    token_valid,
    attention_gain,
    attention_shift,
    project_weight,
    project_bias,
    output_weight,
    output_bias,
    feed_gain,
    feed_shift,
    up_weight,
    up_bias,
    down_weight,
    down_bias,
    cotangent,
):
    n = sz.heads
    my_head = lax.axis_index("head")
    my_blk = lax.axis_index("blk")
    scal = jnp.stack([my_head, my_blk]).astype(i32)
    geo = AttentionShape(sz.blocks, sz.part_rows, sz.parts, sz.run, sz.sub)
    token_shape = (sz.mine, sz.width)

    def call(kernel, name, arrays, outs, scratch=(), flops=10**8):
        return local_call(functools.partial(kernel, sz), name, scal, arrays, outs, scratch, flops)

    def around(x, step):
        return lax.ppermute(x, "head", [(i, (i + step) % n) for i in range(n)])

    def after(values, *earlier):
        return lax.optimization_barrier((values, *earlier))[0]

    def around_groups(x, step):
        pairs = [
            (g * sz.parts + p, (g + step) % sz.groups * sz.parts + p)
            for g in range(sz.groups)
            for p in range(sz.parts)
        ]
        return lax.ppermute(x, "blk", pairs)

    def around_parts(x, step):
        return lax.ppermute(x, "blk", within_group(sz.blocks, sz.parts, step))

    x_mine = layer_input.reshape(token_shape)
    g_mine = cotangent.reshape(token_shape)
    small = [attention_gain, attention_shift, output_bias, feed_gain, feed_shift, down_bias]
    small += [project_bias, up_bias]
    column_rows = (n + 1) * sz.w_rows + sz.f_rows
    (send,) = staged_call(
        functools.partial(pack_kernel, sz),
        "pack",
        scal,
        [project_weight, *[v.reshape(1, -1) for v in small]],
        [((sz.devices, sz.w_chunk + SMALL, LANES), bf16)],
        [pltpu.VMEM((SMALL, LANES), f32)],
    )
    got = lax.all_to_all(send, BOTH, split_axis=0, concat_axis=0, tiled=True)
    own_tokens, column = staged_call(
        functools.partial(pack_more_kernel, sz),
        "pack_more",
        after(scal, send),
        [x_mine, g_mine, up_weight, output_weight, down_weight],
        [((2 * sz.mine, sz.width), bf16), ((column_rows, sz.width), bf16)],
    )
    x_slots = [own_tokens] + [around(own_tokens, d) for d in range(1, n)]
    columns = [column] + [around_groups(column, d) for d in range(1, sz.groups)]

    my_part = my_blk % sz.parts
    my_seq = (my_blk // sz.parts) // sz.local
    scalars, bounds = attention_bounds(
        segments, token_valid, my_seq, my_part, geo, sz.heads, sz.sub
    )
    got = after(got, scalars, bounds, *columns)
    send, w_slice, vec = call(
        project_kernel,
        "project",
        [got, *x_slots],
        [
            ((sz.blocks, sz.half + sz.part_rows, LANES), bf16),
            far((sz.width, (1 + sz.local) * LANES), bf16),
            far((SMALL, sz.width), f32),
        ],
        flops=30 * 10**9,
    )
    columns += [around_parts(after(v, send), d) for d in range(1, sz.parts) for v in columns]
    *pays, w_down = call(
        regroup_kernel,
        "regroup",
        columns,
        [far((2 * sz.head_rows, sz.width), bf16)]
        + [((2 * sz.head_rows, sz.width), bf16)] * (n - 1)
        + [far((sz.width, sz.width), bf16)],
    )
    pays = [pays[0]] + [around(pays[d], d) for d in range(1, n)]
    turned = far((sz.width, sz.tokens), bf16)
    n_one, u_one = call(
        norm_again_kernel, "norm_again", [vec, *x_slots], [turned, turned]
    )
    task = exchange(send, "blk")
    task = after(task, w_down, n_one)
    others = [around_parts(task, step) for step in range(1, sz.parts)]
    o_task, ot, lse = attention_forward(geo, scalars, [task, *others], bounds)
    mixed = exchange(o_task, "blk")
    m_slots = [mixed] + [around(mixed, d) for d in range(1, n)]

    outs = call(
        feed_kernel,
        "feed",
        [vec, w_down, *x_slots, *pays, *m_slots],
        [far(token_shape, f32)]
        + [(token_shape, bf16)] * (n - 1)
        + [far(token_shape, f32)]
        + [far(token_shape, bf16)] * (n - 1)
        + [far(token_shape, f32)]
        + [((n, sz.mine, sz.hidden_slice), bf16)] * 2
        + [((n, *token_shape), bf16), far(token_shape, bf16), far((SMALL, sz.width), f32)],
        [
            pltpu.VMEM((sz.width, sz.hidden_slice), bf16),
            pltpu.VMEM((n, *token_shape), bf16),
        ],
        flops=30 * 10**9,
    )
    grad_two, feed = outs[:n], outs[n : 2 * n]
    middle, activated, grad_hidden, n_two, mixed_own, feed_sums = outs[2 * n :]
    grad_two = [grad_two[0]] + [around(grad_two[d], -d) for d in range(1, n)]

    def shared(rows):
        shape = (sz.groups, rows, sz.width)
        return [far(shape, f32), far(shape, bf16)]

    keep, give = call(
        feed_grad_kernel,
        "feed_grad",
        [activated, grad_hidden, n_two, *x_slots],
        shared(sz.f_rows + n * sz.w_rows),
    )
    grad_two[0] = after(grad_two[0], keep)

    grad_middle, branch, send, branch_sums = call(
        middle_grad_kernel,
        "middle_grad",
        [vec, middle, own_tokens, *pays, *grad_two],
        [
            far(token_shape, f32),
            far(token_shape, bf16),
            ((sz.devices, sz.run // 2, LANES), bf16),
            far((SMALL, sz.width), f32),
        ],
        flops=30 * 10**9,
    )
    do_task = exchange(send, BOTH)
    given = around_parts(give, 1)
    keep_out, give = call(
        out_grad_kernel,
        "out_grad",
        [mixed_own, after(branch, send)],
        shared(n * sz.w_rows),
    )
    rows = sz.f_rows + 2 * n * sz.w_rows
    w_sum = call(
        part_sum_kernel,
        "part_sum",
        [keep, given, keep_out, around_parts(give, 1)],
        [far((rows, sz.width), f32)] + [((rows, sz.width), bf16)] * (sz.groups - 1),
    )
    w_pieces = [around_groups(w_sum[d], d) for d in range(1, sz.groups)]
    dq, dkv, *dkv_others = attention_backward(
        geo, do_tile_grouped, scalars, [task, *others], do_task, bounds, ot, lse
    )
    dkv_others[0] = after(dkv_others[0], *w_pieces)
    for step in range(1, sz.parts):
        back = within_group(sz.blocks, sz.parts, -step)
        dkv = dkv + lax.ppermute(dkv_others[step - 1], "blk", back).astype(f32)
    send = jnp.concatenate([dq, dkv.astype(bf16)], axis=1)
    got = exchange(send, "blk")
    down_grad, piece, *rest = call(
        split_kernel,
        "split",
        [after(w_sum[0], send), *w_pieces, *feed[1:]],
        [((sz.f_rows, sz.width), f32), far((2 * sz.w_rows, sz.width), bf16)]
        + [far((sz.mine + 2 * sz.w_rows, sz.width), bf16)] * (n - 1),
    )
    rest = [around(v, -d - 1) for d, v in enumerate(rest)]
    got = after(got, *rest)
    send, d_proj = call(
        project_grad_kernel,
        "project_grad",
        [feed_sums, branch_sums, got, w_slice, n_one, u_one],
        [
            ((sz.devices, sz.w_chunk + 2 * SMALL, LANES), bf16),
            far((sz.tokens, (1 + sz.local) * LANES), bf16),
        ],
        flops=30 * 10**9,
    )
    got = exchange(send, BOTH)
    outs = call(
        input_partial_kernel,
        "input_partial",
        [d_proj, w_slice],
        [(token_shape, f32)] + [(token_shape, bf16)] * (n - 1),
    )
    grad_one = [outs[0]] + [around(outs[d], -d) for d in range(1, n)]
    (input_grad,) = call(
        input_grad_kernel,
        "input_grad",
        [vec, grad_middle, own_tokens, *grad_one],
        [(token_shape, bf16)],
    )
    layer_output = middle + feed[0] + vec[5:6]
    for v in rest:
        layer_output = layer_output + v[: sz.mine].astype(f32)
    layer_output = layer_output.astype(bf16)
    w_grad, up_grad, out_grad, *owned = call(
        final_kernel,
        "final",
        [got, piece, *rest],
        [
            ((sz.w_rows, 3 * sz.width), f32),
            ((sz.w_rows, n * sz.hidden_slice), f32),
            ((sz.w_rows, sz.width), f32),
        ]
        + [((1, v.shape[0]), f32) for v in small],
    )
    owned = [v.reshape(-1) for v in owned]
    return (
        layer_output.reshape(layer_input.shape),
        input_grad.reshape(layer_input.shape),
        owned[0],
        owned[1],
        w_grad,
        owned[6],
        out_grad,
        owned[2],
        owned[3],
        owned[4],
        up_grad,
        owned[7],
        down_grad,
        owned[5],
    )


def on_device(*arguments):
    layer_input, up_weight = arguments[0], arguments[11]
    seqs, _, sub, width = layer_input.shape
    sz = Sizes(
        lax.axis_size("head"), lax.axis_size("blk"), seqs, sub, width, up_weight.shape[1]
    )
    if sz.fits():
        return on_device_fused(sz, *arguments)
    return on_device_general(*arguments)


def solution(mesh):
    tokens = P(None, "blk", "head", None)
    vector = P(BOTH)
    matrix = P(BOTH, None)
    return jax.shard_map(
        on_device,
        mesh=mesh,
        in_specs=(
            tokens,
            P(),
            P(),
            vector,
            vector,
            matrix,
            vector,
            matrix,
            vector,
            vector,
            vector,
            matrix,
            vector,
            matrix,
            vector,
            tokens,
        ),
        out_specs=(
            tokens,
            tokens,
            vector,
            vector,
            matrix,
            vector,
            matrix,
            vector,
            vector,
            vector,
            matrix,
            vector,
            matrix,
            vector,
        ),
        check_vma=False,
    )
```

```python
import functools

import jax
import jax.numpy as jnp
from jax import lax
from jax.experimental import pallas as pl
from jax.experimental.pallas import tpu as pltpu
from jax.sharding import PartitionSpec as P

H = 8
HD = 64
LANES = 128
EPSILON = 1e-05
NEG_FILL = -1e30
TILE_Q = 256

bf16 = jnp.bfloat16
f32 = jnp.float32
i32 = jnp.int32
BOTH = ("head", "blk")


def dot_nn(a, b):
    return lax.dot_general(a, b, (((1,), (0,)), ((), ())), preferred_element_type=f32)


def dot_nt(a, b):
    return lax.dot_general(a, b, (((1,), (1,)), ((), ())), preferred_element_type=f32)


def dot_tn(a, b):
    return lax.dot_general(a, b, (((0,), (0,)), ((), ())), preferred_element_type=f32)


def norm_forward(values, gain, shift):
    centred = values - jnp.mean(values, axis=-1, keepdims=True)
    variance = jnp.mean(centred * centred, axis=-1, keepdims=True)
    inverse_root = lax.rsqrt(variance + EPSILON)
    unit_value = centred * inverse_root
    return (unit_value * gain + shift, unit_value, inverse_root)


def norm_input_grad(upstream, unit_value, inverse_root, gain):
    scaled = upstream * gain
    inner = scaled - jnp.mean(scaled, axis=-1, keepdims=True)
    inner = inner - unit_value * jnp.mean(scaled * unit_value, axis=-1, keepdims=True)
    return inverse_root * inner


class AttentionShape:
    def __init__(self, blocks, part_rows, parts, run, stride):
        self.blocks = blocks
        self.per_tile = max(1, TILE_Q // part_rows)
        self.tiles = blocks // self.per_tile
        self.tile = self.per_tile * part_rows
        self.part_rows = part_rows
        self.half = part_rows // 2
        self.parts = parts
        self.run = run
        self.stride = stride
        self.span = self.tile * parts


def unpack_rows(packed):
    return jnp.concatenate([packed[:, :HD], packed[:, HD:]], axis=0)


def pack_rows(rows):
    half = rows.shape[0] // 2
    return jnp.concatenate([rows[:half], rows[half:]], axis=1)


def key_base(geo):
    rows = lax.broadcasted_iota(i32, (geo.tile, 1), 0)
    return (rows // geo.run) * geo.stride + rows % geo.run


def task_tile(ref, geo, tile, first, count):
    block = ref[pl.ds(tile * geo.per_tile, geo.per_tile), first : first + count, :]
    return block.reshape(geo.per_tile * count, LANES)


ONES = 16
CHUNKS_AT_ONCE = 4


def forward_kernel(geo, scal_ref, *refs):
    part_refs = refs[: geo.parts]
    bounds_ref, out_ref, ot_ref, lse_ref, vt_ref = refs[geo.parts :]
    base = jnp.broadcast_to(key_base(geo), (geo.tile, geo.tile))
    ones = jnp.ones((ONES, geo.tile), bf16)
    for part in range(geo.parts):
        for tile in range(geo.tiles):
            keys = task_tile(part_refs[part], geo, tile, geo.half, geo.part_rows)
            vt_ref[part, tile, :ONES] = ones
            vt_ref[part, tile, ONES:] = keys.T[HD:]
    for tile in range(geo.tiles):
        q = unpack_rows(task_tile(part_refs[0], geo, tile, 0, geo.half))
        q = q * jnp.asarray(HD**-0.5, bf16)
        qz = jnp.concatenate([q, jnp.zeros_like(q)], axis=1)
        start = bounds_ref[tile, 0:1]
        last = bounds_ref[tile, 1:2]
        own = bounds_ref[tile, 2:3]

        def step(key_tiles, carry):
            chunks = [(key_tile, part) for key_tile in key_tiles for part in range(geo.parts)]
            for at in range(0, len(chunks), CHUNKS_AT_ONCE):
                carry = some(chunks[at : at + CHUNKS_AT_ONCE], carry)
            return carry

        def some(chunks, carry):
            run_max, acc = carry
            masked = []
            new_max = run_max
            for key_tile, part in chunks:
                offset = key_tile * geo.span + scal_ref[part]
                keys = task_tile(part_refs[part], geo, key_tile, geo.half, geo.part_rows)
                scores = dot_nt(keys, qz)
                allowed = (base >= start - offset) & (base <= last - offset)
                if key_tile == tile and part == 0:
                    allowed = allowed | (base == own - offset)
                masked.append(jnp.where(allowed, scores, NEG_FILL))
                new_max = jnp.maximum(new_max, jnp.max(masked[-1], axis=0, keepdims=True))
            acc = acc * jnp.exp(run_max - new_max)
            for (key_tile, part), scores in zip(chunks, masked):
                probs = jnp.exp(scores - new_max).astype(bf16)
                acc = acc + dot_nn(vt_ref[part, key_tile], probs)
            return (new_max, acc)

        carry = (
            jnp.full((1, geo.tile), NEG_FILL, f32),
            jnp.zeros((ONES + HD, geo.tile), f32),
        )
        near = max(0, tile - 1)
        carry = step(range(tile, near - 1, -1), carry)
        if near:
            carry = lax.cond(
                scal_ref[geo.parts + tile] < near,
                functools.partial(step, range(near)),
                lambda same: same,
                carry,
            )
        run_max, acc = carry
        run_sum = acc[0:1]
        attended = acc[ONES:] / run_sum
        ot_ref[tile] = attended
        lse_ref[tile] = jnp.broadcast_to(run_max + jnp.log(run_sum), (8, geo.tile))
        packed = pack_rows(attended.T).astype(bf16)
        for i in range(geo.per_tile):
            out_ref[tile * geo.per_tile + i] = packed[i * geo.half : (i + 1) * geo.half]


def backward_kernel(geo, do_tile, scal_ref, *refs):
    part_refs = refs[: geo.parts]
    do_ref, bounds_ref, ot_ref, lse_ref, dq_ref = refs[geo.parts : geo.parts + 5]
    grad_refs = refs[geo.parts + 5 : 2 * geo.parts + 5]
    acc_ref, kvt_ref = refs[2 * geo.parts + 5 :]
    base = jnp.broadcast_to(key_base(geo), (geo.tile, geo.tile))
    acc_ref[...] = jnp.zeros_like(acc_ref)
    for part in range(geo.parts):
        for tile in range(geo.tiles):
            keys = task_tile(part_refs[part], geo, tile, geo.half, geo.part_rows)
            kvt_ref[part, tile] = keys.T
    for tile in range(geo.tiles):
        q = unpack_rows(task_tile(part_refs[0], geo, tile, 0, geo.half))
        q = q * jnp.asarray(HD**-0.5, bf16)
        do = unpack_rows(do_tile(do_ref, geo, tile))
        zeros = jnp.zeros_like(q)
        qz = jnp.concatenate([q, zeros], axis=1)
        doz = jnp.concatenate([zeros, do], axis=1)
        q_do = jnp.concatenate([qz, doz], axis=0)
        delta = jnp.sum(do.astype(f32).T * ot_ref[tile], axis=0, keepdims=True)
        log_total = lse_ref[tile, 0:1]
        start = bounds_ref[tile, 0:1]
        last = bounds_ref[tile, 1:2]
        own = bounds_ref[tile, 2:3]

        def chunk(part, key_tile, acc):
            offset = key_tile * geo.span + scal_ref[part]
            keys = task_tile(part_refs[part], geo, key_tile, geo.half, geo.part_rows)
            scores = dot_nt(keys, qz)
            allowed = (base >= start - offset) & (base <= last - offset)
            if key_tile == tile and part == 0:
                allowed = allowed | (base == own - offset)
            probs = jnp.exp(jnp.where(allowed, scores, NEG_FILL) - log_total)
            grad_probs = dot_nt(keys, doz)
            grad_scores = (probs * (grad_probs - delta)).astype(bf16)
            both = jnp.concatenate([grad_scores, probs.astype(bf16)], axis=1)
            acc_ref[part, key_tile] += dot_nn(both, q_do)
            return acc + dot_nn(kvt_ref[part, key_tile], grad_scores)

        def step(key_tiles, acc):
            for key_tile in key_tiles:
                for part in range(geo.parts):
                    acc = chunk(part, key_tile, acc)
            return acc

        near = max(0, tile - 1)
        acc = step(range(tile, near - 1, -1), jnp.zeros((2 * HD, geo.tile), f32))
        if near:
            acc = lax.cond(
                scal_ref[geo.parts + tile] < near,
                functools.partial(step, range(near)),
                lambda same: same,
                acc,
            )
        packed = pack_rows((acc[:HD] * (HD**-0.5)).T).astype(bf16)
        for i in range(geo.per_tile):
            dq_ref[tile * geo.per_tile + i] = packed[i * geo.half : (i + 1) * geo.half]
    for part in range(geo.parts):
        for tile in range(geo.tiles):
            for i in range(geo.per_tile):
                rows = acc_ref[part, tile, i * geo.part_rows : (i + 1) * geo.part_rows]
                grad_refs[part][tile * geo.per_tile + i] = rows.astype(grad_refs[part].dtype)


VMEM_LIMIT = 16 * 2**20


def far(shape, dtype):
    return (pltpu.HBM(shape, dtype),)


def local_call(kernel, name, scalars, arrays, outs, scratch=(), flops=10**8, limit=VMEM_LIMIT):
    return pl.pallas_call(
        kernel,
        out_shape=tuple(o[0] if len(o) == 1 else jax.ShapeDtypeStruct(*o) for o in outs),
        in_specs=[pl.BlockSpec(memory_space=pltpu.SMEM)]
        + [pl.BlockSpec(memory_space=pltpu.VMEM)] * len(arrays),
        out_specs=tuple([pl.BlockSpec(memory_space=pltpu.VMEM)] * len(outs)),
        scratch_shapes=list(scratch),
        compiler_params=pltpu.CompilerParams(vmem_limit_bytes=limit),
        cost_estimate=pl.CostEstimate(flops=flops, bytes_accessed=10**6, transcendentals=0),
        name=name,
    )(scalars, *arrays)


def attention_limit(geo):
    return VMEM_LIMIT if geo.parts == 2 else 3 * VMEM_LIMIT


def attention_forward(geo, scalars, part_arrays, bounds):
    return local_call(
        functools.partial(forward_kernel, geo),
        "attention_forward",
        scalars,
        [*part_arrays, bounds],
        [
            ((geo.blocks, geo.half, LANES), bf16),
            far((geo.tiles, HD, geo.tile), f32),
            far((geo.tiles, 8, geo.tile), f32),
        ],
        [pltpu.VMEM((geo.parts, geo.tiles, ONES + HD, geo.tile), bf16)],
        flops=30 * 10**9,
        limit=attention_limit(geo),
    )


def attention_backward(geo, do_tile, scalars, part_arrays, do, bounds, ot, lse):
    grads = [((geo.blocks, geo.part_rows, LANES), f32)]
    grads += [((geo.blocks, geo.part_rows, LANES), bf16)] * (geo.parts - 1)
    return local_call(
        functools.partial(backward_kernel, geo, do_tile),
        "attention_backward",
        scalars,
        [*part_arrays, do, bounds, ot, lse],
        [((geo.blocks, geo.half, LANES), bf16), *grads],
        [
            pltpu.VMEM((geo.parts, geo.tiles, geo.tile, LANES), f32),
            pltpu.VMEM((geo.parts, geo.tiles, LANES, geo.tile), bf16),
        ],
        flops=30 * 10**9,
        limit=attention_limit(geo),
    )


def do_tile_grouped(do_ref, geo, tile):
    heads = do_ref.shape[0] // geo.blocks
    pieces = []
    for i in range(geo.per_tile):
        for head in range(heads):
            pieces.append(do_ref[head * geo.blocks + tile * geo.per_tile + i])
    return jnp.concatenate(pieces, axis=0)


def do_tile_plain(do_ref, geo, tile):
    return task_tile(do_ref, geo, tile, 0, geo.half)


def query_positions(blocks, heads, run, sub, part, geo):
    half = run // 2
    block = jnp.arange(blocks, dtype=i32).reshape(geo.tiles, 1, geo.per_tile, 1, 1)
    upper = jnp.arange(2, dtype=i32).reshape(1, 2, 1, 1, 1)
    head = jnp.arange(heads, dtype=i32).reshape(1, 1, 1, heads, 1)
    row = jnp.arange(half, dtype=i32).reshape(1, 1, 1, 1, half)
    at = block * (heads * sub) + head * sub + part * run + upper * half + row
    return at.reshape(geo.tiles, 1, geo.tile)


def attention_bounds(segments, token_valid, my_seq, my_part, geo, heads, sub):
    seg = lax.dynamic_index_in_dim(segments, my_seq, 0, keepdims=False)
    valid = jnp.sum(lax.dynamic_index_in_dim(token_valid, my_seq, 0, keepdims=False))
    own = query_positions(geo.blocks, heads, geo.run, sub, my_part, geo)
    half = geo.run // 2
    own_seg = seg.reshape(geo.blocks * heads, geo.parts, geo.run)
    own_seg = lax.dynamic_index_in_dim(own_seg, my_part, 1, keepdims=False)
    own_seg = own_seg.reshape(geo.tiles, geo.per_tile, heads, 2, half).transpose(0, 3, 1, 2, 4)
    own_seg = own_seg.reshape(-1, 1)
    start = jnp.sum((seg[None, :] < own_seg).astype(i32), axis=1).reshape(geo.tiles, 1, geo.tile)
    last = jnp.minimum(own, valid - 1)
    bounds = jnp.concatenate([start, last, own, jnp.zeros((geo.tiles, 5, geo.tile), i32)], axis=1)
    first_seg = seg.reshape(geo.tiles, geo.span)[:, :1]
    first_tile = jnp.sum((seg[None, :] < first_seg).astype(i32), axis=1) // geo.span
    part_at = ((my_part - jnp.arange(geo.parts, dtype=i32)) % geo.parts) * geo.run
    return jnp.concatenate([part_at, first_tile]), bounds


def gather_head(x):
    return lax.all_gather(x, "head", axis=0, tiled=False)


def exchange(x, axis):
    return lax.all_to_all(x, axis, split_axis=0, concat_axis=0, tiled=True)


def within_group(blocks, parts, step):
    return [
        (t * parts + i, t * parts + (i + step) % parts)
        for t in range(blocks // parts)
        for i in range(parts)
    ]


def on_device_general(
    layer_input,
    segments,
    token_valid,
    attention_gain,
    attention_shift,
    project_weight,
    project_bias,
    output_weight,
    output_bias,
    feed_gain,
    feed_shift,
    up_weight,
    up_bias,
    down_weight,
    down_bias,
    cotangent,
):
    heads = lax.axis_size("head")
    blocks = lax.axis_size("blk")
    my_head = lax.axis_index("head")
    my_blk = lax.axis_index("blk")
    devices = heads * blocks
    seqs, _, sub, width = layer_input.shape
    hidden_width = up_weight.shape[1]
    hidden_slice = hidden_width // heads
    rows = sub * heads
    length = rows * blocks
    mine = seqs * sub
    tokens = seqs * rows
    local = H // heads
    cols = local * HD
    parts = blocks // (seqs * local)
    run = sub // parts
    part_rows = heads * run
    half = part_rows // 2
    w_rows = width // devices
    f_rows = hidden_width // devices
    geo = AttentionShape(blocks, part_rows, parts, run, sub)

    wp = project_weight.reshape(w_rows, 3, heads, local, HD)
    wq = wp[:, 0].transpose(1, 0, 2, 3).reshape(heads, w_rows, cols)
    wq = jnp.pad(wq, ((0, 0), (0, 0), (0, LANES - cols)))
    wkv = wp[:, 1:].transpose(2, 3, 0, 1, 4).reshape(heads, local * w_rows, LANES)
    small = [attention_gain, attention_shift, output_bias, feed_gain, feed_shift, down_bias]
    small += [project_bias, up_bias]
    counts = [v.shape[0] for v in small]
    small = jnp.concatenate(small)
    small_rows = -(-small.shape[0] // LANES)
    small = jnp.pad(small, (0, small_rows * LANES - small.shape[0])).reshape(1, small_rows, LANES)
    chunk = jnp.concatenate([wq, wkv, jnp.broadcast_to(small, (heads, small_rows, LANES))], axis=1)
    chunk_rows = chunk.shape[1]
    send = jnp.broadcast_to(chunk[:, None], (heads, blocks, chunk_rows, LANES))
    got = exchange(send.reshape(devices, chunk_rows, LANES), BOTH)
    w_groups = [
        got[:, i * w_rows : (i + 1) * w_rows].reshape(width, LANES) for i in range(1 + local)
    ]
    w_slice = jnp.concatenate(w_groups, axis=1)
    flat = got[:, (1 + local) * w_rows :].reshape(devices, small_rows * LANES).astype(f32)
    vectors = []
    at = 0
    for count in counts:
        vectors.append(flat[:, at : at + count].reshape(-1))
        at += count
    gain_one, shift_one, b_output, gain_two, shift_two, b_down, b_project, b_up = vectors

    x_mine = layer_input.reshape(mine, width)
    g_mine = cotangent.reshape(mine, width)
    x_all = gather_head(x_mine).reshape(heads, seqs, sub, width).transpose(1, 0, 2, 3)
    g_all = gather_head(g_mine).reshape(heads, seqs, sub, width).transpose(1, 0, 2, 3)
    x_all = x_all.reshape(tokens, width).astype(f32)
    g_all = g_all.reshape(tokens, width)

    up_parts = up_weight.reshape(w_rows, heads, hidden_slice).transpose(1, 0, 2)
    out_parts = jnp.broadcast_to(output_weight[None], (heads, w_rows, width))
    if hidden_slice == width:
        both = exchange(jnp.concatenate([up_parts, out_parts], axis=1), "head")
        shard = jnp.concatenate([both.reshape(2 * heads * w_rows, width), down_weight], axis=0)
        full = lax.all_gather(shard, "blk", axis=0, tiled=False)
        pair = full[:, : 2 * heads * w_rows].reshape(blocks, heads, 2, w_rows, width)
        w_up = pair[:, :, 0].transpose(1, 0, 2, 3).reshape(width, hidden_slice)
        w_out = pair[:, :, 1].transpose(1, 0, 2, 3).reshape(width, width)
        w_down = full[:, 2 * heads * w_rows :].reshape(hidden_slice, width)
    else:
        up_parts = lax.all_gather(exchange(up_parts, "head"), "blk", axis=0, tiled=False)
        out_parts = lax.all_gather(exchange(out_parts, "head"), "blk", axis=0, tiled=False)
        w_up = up_parts.transpose(1, 0, 2, 3).reshape(width, hidden_slice)
        w_out = out_parts.transpose(1, 0, 2, 3).reshape(width, width)
        w_down = lax.all_gather(down_weight, "blk", axis=0, tiled=True)

    n_one, u_one, rs_one = norm_forward(x_all, gain_one, shift_one)
    n_one = n_one.astype(bf16)
    qkv = dot_nn(n_one, w_slice)
    b_q = lax.dynamic_slice(b_project, (my_head * cols,), (cols,))
    b_v = lax.dynamic_slice(b_project, (width + my_head * cols,), (cols,))
    queries = (qkv[:, :cols] + b_q).astype(bf16)
    pairs = qkv[:, LANES:].reshape(tokens, local, 2, HD)
    b_pair = jnp.stack([jnp.zeros((local, HD), f32), b_v.reshape(local, HD)], axis=1)
    pairs = (pairs + b_pair).astype(bf16)
    queries = queries.reshape(seqs, heads, parts, 2, run // 2, local, HD)
    queries = queries.transpose(0, 5, 2, 1, 4, 3, 6).reshape(blocks, half, LANES)
    pairs = pairs.reshape(seqs, heads, parts, run, local, LANES).transpose(0, 4, 2, 1, 3, 5)
    pairs = pairs.reshape(blocks, part_rows, LANES)
    task = exchange(jnp.concatenate([queries, pairs], axis=1), "blk")
    part_arrays = [task]
    for step in range(1, parts):
        part_arrays.append(lax.ppermute(task, "blk", within_group(blocks, parts, step)))

    my_part = my_blk % parts
    my_seq = (my_blk // parts) // local
    scalars, bounds = attention_bounds(segments, token_valid, my_seq, my_part, geo, heads, sub)
    o_task, ot, lse = attention_forward(geo, scalars, part_arrays, bounds)

    got = exchange(o_task, "blk")
    mixed = got.reshape(seqs, local, parts, heads, run // 2, 2, HD)
    mixed = mixed.transpose(0, 3, 2, 5, 4, 1, 6)
    mixed = mixed.reshape(tokens, cols)
    mixed_all = lax.all_gather(mixed, "head", axis=1, tiled=True)

    middle = x_all + dot_nn(mixed_all, w_out) + b_output
    n_two, u_two, rs_two = norm_forward(middle, gain_two, shift_two)
    n_two = n_two.astype(bf16)
    b_up_slice = lax.dynamic_slice(b_up, (my_head * hidden_slice,), (hidden_slice,))
    hidden = dot_nn(n_two, w_up) + b_up_slice
    sigma = jax.nn.sigmoid(1.702 * hidden)
    activated = (hidden * sigma).astype(bf16)
    feed = dot_nn(activated, w_down)
    grad_act = dot_nt(g_all, w_down)
    grad_hidden = (grad_act * (sigma + 1.702 * hidden * sigma * (1.0 - sigma))).astype(bf16)
    grad_two = dot_nt(grad_hidden, w_up)

    def to_owners(partial):
        partial = partial.astype(bf16).reshape(seqs, heads, sub, width).transpose(1, 0, 2, 3)
        return exchange(partial.reshape(heads, mine, width), "head")

    def my_tokens(values):
        values = values.reshape(seqs, heads, sub, values.shape[-1])
        values = lax.dynamic_index_in_dim(values, my_head, 1, keepdims=False)
        return values.reshape(mine, values.shape[-1])

    grad_two_mine = jnp.sum(to_owners(grad_two).astype(f32), axis=0)
    grad_middle = g_mine.astype(f32) + norm_input_grad(
        grad_two_mine, my_tokens(u_two), my_tokens(rs_two), gain_two
    )
    grad_branch = grad_middle.astype(bf16)
    grad_mixed = dot_nt(grad_branch, w_out).astype(bf16)
    grad_mixed = grad_mixed.reshape(seqs, parts, 2, run // 2, heads, local, HD)
    grad_mixed = grad_mixed.transpose(4, 0, 5, 1, 3, 2, 6).reshape(devices, run // 2, LANES)
    got = exchange(grad_mixed, BOTH).reshape(heads, blocks, run // 2, LANES)
    do_task = got.transpose(1, 0, 2, 3).reshape(blocks, half, LANES)

    feed_mine = jnp.sum(to_owners(feed).astype(f32), axis=0)
    layer_output = my_tokens(middle) + feed_mine + b_down

    grad_down = dot_tn(activated, g_all).astype(bf16).reshape(blocks, -1, width)
    grad_up = dot_tn(n_two, grad_hidden).astype(bf16)
    grad_up = grad_up.reshape(heads, blocks, w_rows, hidden_slice).transpose(1, 0, 2, 3)
    branch_all = gather_head(grad_branch).reshape(heads, seqs, sub, width).transpose(1, 0, 2, 3)
    grad_out = dot_tn(mixed, branch_all.reshape(tokens, width)).astype(bf16)

    def over_blocks(partial):
        return lax.psum_scatter(partial, "blk", scatter_dimension=0, tiled=True)

    if hidden_slice == width:
        summed = over_blocks(
            jnp.concatenate(
                [grad_down.reshape(blocks, f_rows, width), grad_up.reshape(blocks, -1, width)],
                axis=1,
            ).reshape(-1, width)
        )
        own_down = summed[:f_rows]
        own_up = summed[f_rows:]
    else:
        own_down = over_blocks(grad_down.reshape(-1, width))
        own_up = over_blocks(grad_up.reshape(-1, hidden_slice))
    own_out = over_blocks(grad_out)
    own_up = exchange(own_up.reshape(heads, w_rows, hidden_slice), "head")
    own_up = own_up.transpose(1, 0, 2).reshape(w_rows, hidden_width)

    dq_task, dkv, *others = attention_backward(
        geo, do_tile_plain, scalars, part_arrays, do_task, bounds, ot, lse
    )
    for step in range(1, parts):
        back = within_group(blocks, parts, -step)
        dkv = dkv + lax.ppermute(others[step - 1], "blk", back).astype(f32)
    got = exchange(jnp.concatenate([dq_task, dkv.astype(bf16)], axis=1), "blk")
    dq = got[:, :half].reshape(seqs, local, parts, heads, run // 2, 2, HD)
    dq = dq.transpose(0, 3, 2, 5, 4, 1, 6)
    dq = dq.reshape(tokens, cols)
    dkv = got[:, half:].reshape(seqs, local, parts, heads, run, LANES).transpose(0, 3, 2, 4, 1, 5)
    dkv = dkv.reshape(tokens, local * LANES)
    dq = jnp.pad(dq, ((0, 0), (0, LANES - cols)))
    d_proj = jnp.concatenate([dq, dkv], axis=1)

    grad_one = dot_nt(d_proj, w_slice)
    grad_one_mine = jnp.sum(to_owners(grad_one).astype(f32), axis=0)
    x_f32 = x_mine.astype(f32)
    input_grad = grad_middle + norm_input_grad(
        grad_one_mine, my_tokens(u_one), my_tokens(rs_one), gain_one
    )

    grad_w = dot_tn(n_one, d_proj).astype(bf16)
    col_sums = jnp.sum(d_proj.astype(f32), axis=0)
    bias_q = col_sums[:cols]
    bias_v = col_sums[LANES:].reshape(local, 2, HD)[:, 1].reshape(cols)
    bias_grad = jnp.zeros((2 * width,), f32)
    bias_grad = lax.dynamic_update_slice(bias_grad, bias_q, (my_head * cols,))
    bias_grad = lax.dynamic_update_slice(bias_grad, bias_v, (width + my_head * cols,))
    up_bias_grad = lax.dynamic_update_slice(
        jnp.zeros((hidden_width,), f32),
        jnp.sum(grad_hidden.astype(f32), axis=0),
        (my_head * hidden_slice,),
    )
    tiny = [
        jnp.sum(grad_one * u_one, axis=0),
        jnp.sum(grad_one, axis=0),
        jnp.sum(grad_branch.astype(f32), axis=0),
        jnp.sum(grad_two * u_two, axis=0),
        jnp.sum(grad_two, axis=0),
        jnp.sum(g_mine.astype(f32), axis=0),
        bias_grad,
        up_bias_grad,
    ]
    tiny = jnp.concatenate([v.reshape(devices, -1) for v in tiny], axis=1)
    high = tiny.astype(bf16)
    low = (tiny - high.astype(f32)).astype(bf16)
    tiny = jnp.concatenate([high, low], axis=1)
    tiny_rows = -(-tiny.shape[1] // LANES)
    tiny = jnp.pad(tiny, ((0, 0), (0, tiny_rows * LANES - tiny.shape[1])))
    tiny = tiny.reshape(devices, tiny_rows, LANES)
    grad_w = [
        grad_w[:, i * LANES : (i + 1) * LANES].reshape(devices, w_rows, LANES)
        for i in range(1 + local)
    ]
    got = exchange(jnp.concatenate(grad_w + [tiny], axis=1), BOTH)
    got = got.astype(f32)
    n_w = (1 + local) * w_rows
    own_w = jnp.sum(got[:, :n_w].reshape(heads, blocks, n_w, LANES), axis=1)
    own_q = own_w[:, :w_rows, :cols].transpose(1, 0, 2).reshape(w_rows, width)
    own_kv = own_w[:, w_rows:].reshape(heads, local, w_rows, 2, HD)
    own_kv = own_kv.transpose(2, 3, 0, 1, 4).reshape(w_rows, 2 * width)
    own_w = jnp.concatenate([own_q, own_kv], axis=1)
    summed = jnp.sum(got[:, n_w:].reshape(devices, -1), axis=0)
    total = sum(counts)
    summed = summed[:total] + summed[total : 2 * total]
    owned = []
    at = 0
    for count in counts:
        owned.append(summed[at : at + count])
        at += count

    return (
        layer_output.astype(bf16).reshape(layer_input.shape),
        input_grad.astype(bf16).reshape(layer_input.shape),
        owned[0],
        owned[1],
        own_w,
        owned[6],
        own_out.astype(f32),
        owned[2],
        owned[3],
        owned[4],
        own_up.astype(f32),
        owned[7],
        own_down.astype(f32),
        owned[5],
    )


class Sizes:
    def __init__(self, heads, blocks, seqs, sub, width, hidden_width):
        self.heads = heads
        self.blocks = blocks
        self.seqs = seqs
        self.sub = sub
        self.width = width
        self.devices = heads * blocks
        self.mine = seqs * sub
        self.tokens = self.mine * heads
        self.local = H // heads
        self.parts = blocks // (seqs * self.local)
        self.run = sub // self.parts
        self.part_rows = heads * self.run
        self.half = self.part_rows // 2
        self.w_rows = width // self.devices
        self.f_rows = hidden_width // self.devices
        self.hidden_slice = hidden_width // heads
        self.w_chunk = (1 + self.local) * self.w_rows
        self.head_rows = self.blocks * self.w_rows
        self.groups = blocks // self.parts

    def fits(self):
        return (
            self.local == 2
            and self.parts == 2
            and self.run % 32 == 0
            and self.w_rows == 16
            and self.hidden_slice == self.width
            and self.mine % 16 == 0
            and self.f_rows % 16 == 0
        )

    def task(self, seq, local, part):
        return (seq * self.local + local) * self.parts + part


SMALL = 8


def my_head_of(sz, scal_ref):
    return scal_ref[0] // sz.blocks


def my_blk_of(sz, scal_ref):
    return lax.rem(scal_ref[0], sz.blocks)


def slot_head(sz, scal_ref, slot):
    return lax.rem(my_head_of(sz, scal_ref) - slot + sz.heads, sz.heads)


def halves(first, second):
    low = jnp.concatenate([first[:, :HD], second[:, :HD]], axis=1)
    high = jnp.concatenate([first[:, HD:], second[:, HD:]], axis=1)
    return low, high


def staged(count, refs):
    scratch = refs[len(refs) - count - 1 :]
    held, sems = scratch[:count], scratch[count]
    copies = [pltpu.make_async_copy(refs[i], held[i], sems.at[i]) for i in range(count)]
    for copy in copies:
        copy.start()
    for copy in copies:
        copy.wait()
    return held


def staged_call(kernel, name, scalars, arrays, outs, scratch=()):
    return pl.pallas_call(
        kernel,
        out_shape=tuple(jax.ShapeDtypeStruct(*o) for o in outs),
        in_specs=[pl.BlockSpec(memory_space=pltpu.SMEM)]
        + [pl.BlockSpec(memory_space=pltpu.HBM)] * len(arrays),
        out_specs=tuple([pl.BlockSpec(memory_space=pltpu.VMEM)] * len(outs)),
        scratch_shapes=list(scratch)
        + [pltpu.VMEM(v.shape, v.dtype) for v in arrays]
        + [pltpu.SemaphoreType.DMA((len(arrays),))],
        compiler_params=pltpu.CompilerParams(vmem_limit_bytes=63 * 2**20),
        name=name,
    )(scalars, *arrays)


def pack_kernel(sz, scal_ref, *refs):
    count = 1 + SMALL
    send_ref, small_scr = refs[count : count + 2]
    small_scr[...] = jnp.zeros_like(small_scr)
    wp_ref, *small_refs = staged(count, refs)
    for i, ref in enumerate(small_refs):
        small_scr[i : i + 1, : ref.shape[1]] = ref[...].astype(f32)
    small = small_scr[...].astype(bf16)
    for head in range(sz.heads):
        at = head * LANES
        q = wp_ref[:, at : at + LANES]
        k = wp_ref[:, sz.width + at : sz.width + at + LANES]
        v = wp_ref[:, 2 * sz.width + at : 2 * sz.width + at + LANES]
        low, high = halves(k, v)
        chunk = jnp.concatenate([q, low, high], axis=0)
        for group in range(sz.groups):
            send_ref[head * sz.groups + group, : sz.w_chunk] = chunk
            send_ref[head * sz.groups + group, sz.w_chunk :] = small


def pieces_kernel(sz, scal_ref, *refs):
    piece_refs = refs[3 : 3 + sz.heads]
    g_ref, up_ref, wo_ref = staged(3, refs)
    for step, ref in enumerate(piece_refs):
        to = lax.rem(my_head_of(sz, scal_ref) + step, sz.heads)
        at = pl.multiple_of(to * sz.hidden_slice, LANES)
        ref[: sz.mine] = g_ref[...]
        ref[sz.mine : sz.mine + sz.w_rows] = up_ref[:, pl.ds(at, sz.hidden_slice)]
        ref[sz.mine + sz.w_rows :] = wo_ref[...]


def spread(small, per, offset, count):
    lane = lax.broadcasted_iota(i32, (LANES, count), 0)
    at = lax.broadcasted_iota(i32, (LANES, count), 1) + offset
    pick = jnp.where(at % per == lane, 1.0, 0.0).astype(bf16)
    wide = dot_nn(small, pick)
    source = lax.broadcasted_iota(i32, wide.shape, 0) // SMALL
    column = (lax.broadcasted_iota(i32, wide.shape, 1) + offset) // per
    wide = jnp.where(source == column, wide, 0.0)
    return jnp.sum(wide.reshape(-1, SMALL, count), axis=0)


def collect(values, per, offset, rows, devices):
    count = values.shape[1]
    tall = jnp.broadcast_to(values[None], (devices, SMALL, count)).reshape(devices * SMALL, count)
    row = lax.broadcasted_iota(i32, tall.shape, 0)
    column = (lax.broadcasted_iota(i32, tall.shape, 1) + offset) // per
    index = row % SMALL
    keep = (row // SMALL == column) & (index >= rows[0]) & (index < rows[1])
    tall = jnp.where(keep, tall, 0.0)
    lane = lax.broadcasted_iota(i32, (count, LANES), 1)
    at = lax.broadcasted_iota(i32, (count, LANES), 0) + offset
    pick = jnp.where(at % per == lane, 1.0, 0.0).astype(bf16)
    return dot_nn(tall.astype(bf16), pick)


def source_blk(sz, scal_ref, group_slot, part_slot):
    group = lax.rem(my_blk_of(sz, scal_ref) // sz.parts - group_slot + sz.groups, sz.groups)
    part = lax.rem(my_blk_of(sz, scal_ref) % sz.parts - part_slot + sz.parts, sz.parts)
    return group * sz.parts + part


def project_kernel(sz, scal_ref, *refs):
    got_refs, refs = refs[: sz.parts], refs[sz.parts :]
    x_refs = refs[: sz.heads]
    send_ref, w_ref, vec_ref, small_scr = refs[sz.heads :]
    head = my_head_of(sz, scal_ref)
    for part_slot, ref in enumerate(got_refs):
        part = lax.rem(my_blk_of(sz, scal_ref) + sz.parts - part_slot, sz.parts)
        for src in range(sz.heads * sz.groups):
            dev = src // sz.groups * sz.blocks + src % sz.groups * sz.parts + part
            at = pl.multiple_of(dev * sz.w_rows, sz.w_rows)
            for i in range(1 + sz.local):
                piece = ref[src, i * sz.w_rows : (i + 1) * sz.w_rows]
                w_ref[pl.ds(at, sz.w_rows), i * LANES : (i + 1) * LANES] = piece
            at = pl.multiple_of(dev * SMALL, SMALL)
            small_scr[pl.ds(at, SMALL)] = ref[src, sz.w_chunk :].astype(f32)
    small = small_scr[...].astype(bf16)
    vec = spread(small, sz.w_rows, 0, sz.width)
    per = 2 * sz.w_rows
    b_q = spread(small, per, head * LANES, LANES)[6:7]
    b_v = spread(small, per, sz.width + head * LANES, LANES)[6:7]
    b_up = spread(small, 4 * sz.w_rows, head * sz.hidden_slice, sz.hidden_slice)
    row = lax.broadcasted_iota(i32, vec.shape, 0)
    vec = jnp.where(row == 7, b_up, vec)
    vec_ref[...] = vec
    zero = jnp.zeros((1, HD), f32)
    bias = jnp.concatenate([b_q, zero, b_v[:, :HD], zero, b_v[:, HD:]], axis=1)
    gain, shift = vec[0:1], vec[1:2]
    for slot in range(sz.heads):
        x = x_refs[slot][...].astype(f32)
        normed = norm_forward(x, gain, shift)[0].astype(bf16)
        qkv = (dot_nn(normed, w_ref[...]) + bias).astype(bf16)
        to = slot_head(sz, scal_ref, slot)
        half_run = sz.run // 2
        for seq in range(sz.seqs):
            for part in range(sz.parts):
                at = seq * sz.sub + part * sz.run
                low, high = halves(qkv[at : at + half_run, :LANES], qkv[at + half_run : at + sz.run, :LANES])
                packed = (low, high)
                for local in range(sz.local):
                    task = sz.task(seq, local, part)
                    q_at = pl.multiple_of(to * half_run, half_run)
                    send_ref[task, pl.ds(q_at, half_run)] = packed[local]
                    kv_at = pl.multiple_of(sz.half + to * sz.run, sz.run)
                    send_ref[task, pl.ds(kv_at, sz.run)] = qkv[
                        at : at + sz.run, (1 + local) * LANES : (2 + local) * LANES
                    ]


def assemble_kernel(sz, scal_ref, *refs):
    chunks = sz.parts * sz.groups
    mixed_refs, down_refs = refs[:chunks], refs[chunks : 2 * chunks]
    up_ref, wo_ref, down_ref = refs[2 * chunks :]
    for part_slot in range(sz.parts):
        for group_slot in range(sz.groups):
            i = part_slot * sz.groups + group_slot
            blk = source_blk(sz, scal_ref, group_slot, part_slot)
            at = pl.multiple_of(blk * sz.f_rows, sz.f_rows)
            down_ref[pl.ds(at, sz.f_rows)] = down_refs[i][...]
            for slot in range(sz.heads):
                head = slot_head(sz, scal_ref, slot)
                at = pl.multiple_of(head * sz.head_rows + blk * sz.w_rows, sz.w_rows)
                first = 2 * slot * sz.w_rows
                up_ref[pl.ds(at, sz.w_rows)] = mixed_refs[i][first : first + sz.w_rows]
                at = pl.multiple_of(slot * sz.head_rows + blk * sz.w_rows, sz.w_rows)
                first += sz.w_rows
                wo_ref[pl.ds(at, sz.w_rows)] = mixed_refs[i][first : first + sz.w_rows]


def feed_kernel(sz, scal_ref, vec_ref, up_ref, wo_ref, down_ref, *refs):
    n = sz.heads
    x_refs, g_refs, m_refs = refs[:n], refs[n : 2 * n], refs[2 * n : 3 * n]
    outs = refs[3 * n :]
    part_refs, feed_refs = outs[:n], outs[n : 2 * n]
    mid_ref, act_ref, dh_ref, n_ref, mix_own_ref, sum_ref, mix_scr = outs[2 * n :]
    half_run = sz.run // 2
    for slot in range(n):
        for seq in range(sz.seqs):
            for part in range(sz.parts):
                first = m_refs[slot][sz.task(seq, 0, part)]
                second = m_refs[slot][sz.task(seq, 1, part)]
                low, high = halves(first, second)
                for head in range(n):
                    at = seq * sz.sub + part * sz.run
                    cols = slice(slot * LANES, (slot + 1) * LANES)
                    rows = slice(head * half_run, (head + 1) * half_run)
                    mix_scr[head, at : at + half_run, cols] = low[rows]
                    mix_scr[head, at + half_run : at + sz.run, cols] = high[rows]
    w_down = down_ref[...]
    b_out, gain, shift, b_up = vec_ref[2:3], vec_ref[3:4], vec_ref[4:5], vec_ref[7:8]
    sums = jnp.zeros((3, sz.width), f32)
    group = 2
    for first in range(0, n, group):
        slots = range(first, first + group)
        x = jnp.concatenate([x_refs[s][...] for s in slots], axis=0).astype(f32)
        g = jnp.concatenate([g_refs[s][: sz.mine] for s in slots], axis=0)
        mixed = jnp.concatenate([mix_scr[slot_head(sz, scal_ref, s)] for s in slots], axis=0)
        middle = x + dot_nn(mixed, wo_ref[...]) + b_out
        normed, unit, _ = norm_forward(middle, gain, shift)
        normed = normed.astype(bf16)
        hidden = dot_nn(normed, up_ref[...]) + b_up
        sigma = 1.0 / (1.0 + jnp.exp(-1.702 * hidden))
        activated = (hidden * sigma).astype(bf16)
        slope = sigma + 1.702 * hidden * sigma * (1.0 - sigma)
        grad_hidden = (dot_nt(g, w_down) * slope).astype(bf16)
        grad_two = dot_nt(grad_hidden, up_ref[...])
        feed = dot_nn(activated, w_down)
        sums = sums + jnp.concatenate(
            [
                jnp.sum(grad_two * unit, axis=0, keepdims=True),
                jnp.sum(grad_two, axis=0, keepdims=True),
                jnp.sum(grad_hidden.astype(f32), axis=0, keepdims=True),
            ],
            axis=0,
        )
        for i, s in enumerate(slots):
            rows = slice(i * sz.mine, (i + 1) * sz.mine)
            part_refs[s][...] = grad_two[rows].astype(part_refs[s].dtype)
            feed_refs[s][...] = feed[rows].astype(feed_refs[s].dtype)
            if s == 0:
                mid_ref[...] = middle[rows]
                mix_own_ref[...] = mixed[rows]
            act_ref[s] = activated[rows]
            dh_ref[s] = grad_hidden[rows]
            n_ref[s] = normed[rows]
    sum_ref[...] = jnp.concatenate([sums, jnp.zeros((5, sz.width), f32)], axis=0)


def give_and_keep(sz, scal_ref, values, rows, keep_ref, give_ref):
    part = my_blk_of(sz, scal_ref) % sz.parts
    for blk in range(sz.blocks):
        group = blk // sz.parts
        piece = values(blk)
        @pl.when(part == blk % sz.parts)
        def _():
            keep_ref[group] = piece

        @pl.when(part != blk % sz.parts)
        def _():
            give_ref[group] = piece.astype(bf16)


def feed_grad_kernel(sz, scal_ref, act_ref, dh_ref, n_ref, *refs):
    g_refs = refs[: sz.heads]
    keep_ref, give_ref = refs[sz.heads :]
    g = jnp.concatenate([ref[: sz.mine] for ref in g_refs], axis=0)
    act = act_ref[...].reshape(sz.tokens, sz.hidden_slice)
    down = dot_tn(act, g)
    up = dot_tn(n_ref[...].reshape(sz.tokens, sz.width), dh_ref[...].reshape(sz.tokens, sz.hidden_slice))

    def piece(blk):
        pieces = [down[blk * sz.f_rows : (blk + 1) * sz.f_rows]]
        for head in range(sz.heads):
            at = head * sz.head_rows + blk * sz.w_rows
            pieces.append(up[at : at + sz.w_rows])
        return jnp.concatenate(pieces, axis=0)

    give_and_keep(sz, scal_ref, piece, sz.f_rows + sz.heads * sz.w_rows, keep_ref, give_ref)


def part_sum_kernel(sz, scal_ref, *refs):
    keep_ref, got_ref, keep_out_ref, got_out_ref, *refs = refs
    down_refs, rest_refs = refs[: sz.groups], refs[sz.groups :]
    rows = keep_ref.shape[1] - sz.f_rows
    for step in range(sz.groups):
        to = lax.rem(my_blk_of(sz, scal_ref) // sz.parts + step, sz.groups)
        total = keep_ref[to] + got_ref[to].astype(f32)
        total_out = keep_out_ref[to] + got_out_ref[to].astype(f32)
        dtype = rest_refs[step].dtype
        down_refs[step][...] = total[: sz.f_rows].astype(dtype)
        rest_refs[step][:rows] = total[sz.f_rows :].astype(dtype)
        rest_refs[step][rows:] = total_out.astype(dtype)


def middle_grad_kernel(sz, scal_ref, vec_ref, wo_ref, mid_ref, g_ref, mix_ref, *refs):
    n = sz.heads
    part_refs = refs[:n]
    grad_ref, branch_ref, send_ref, sum_ref, keep_ref, give_ref = refs[n:]
    upstream = part_refs[0][...]
    for ref in part_refs[1:]:
        upstream = upstream + ref[...].astype(f32)
    gain, shift = vec_ref[3:4], vec_ref[4:5]
    _, unit, root = norm_forward(mid_ref[...], gain, shift)
    g = g_ref[...].astype(f32)
    grad = g + norm_input_grad(upstream, unit, root, gain)
    grad_ref[...] = grad
    branch = grad.astype(bf16)
    branch_ref[...] = branch
    sum_ref[...] = jnp.concatenate(
        [
            jnp.sum(branch.astype(f32), axis=0, keepdims=True),
            jnp.sum(g, axis=0, keepdims=True),
            jnp.zeros((6, sz.width), f32),
        ],
        axis=0,
    )
    mixed = dot_nt(branch, wo_ref[...]).astype(bf16)
    half_run = sz.run // 2
    for slot in range(n):
        to = slot_head(sz, scal_ref, slot)
        for seq in range(sz.seqs):
            for part in range(sz.parts):
                at = seq * sz.sub + part * sz.run
                cols = slice(slot * LANES, (slot + 1) * LANES)
                packed = halves(mixed[at : at + half_run, cols], mixed[at + half_run : at + sz.run, cols])
                for local in range(sz.local):
                    send_ref[to * sz.blocks + sz.task(seq, local, part)] = packed[local]
    out_grad(sz, scal_ref, mix_ref[...], branch, keep_ref, give_ref)


def out_grad(sz, scal_ref, mixed, branch, keep_ref, give_ref):
    grad = dot_tn(mixed, branch)
    part = my_blk_of(sz, scal_ref) % sz.parts
    for slot in range(sz.heads):
        head = slot_head(sz, scal_ref, slot)
        to = pl.multiple_of(head * sz.w_rows, sz.w_rows)
        for blk in range(sz.blocks):
            at = slot * sz.head_rows + blk * sz.w_rows
            piece = grad[at : at + sz.w_rows]

            @pl.when(part == blk % sz.parts)
            def _():
                keep_ref[blk // sz.parts, pl.ds(to, sz.w_rows)] = piece

            @pl.when(part != blk % sz.parts)
            def _():
                give_ref[blk // sz.parts, pl.ds(to, sz.w_rows)] = piece.astype(bf16)


def norm_again_kernel(sz, scal_ref, vec_ref, *refs):
    x_refs = refs[: sz.heads]
    n_ref, u_ref = refs[sz.heads :]
    gain, shift = vec_ref[0:1], vec_ref[1:2]
    for slot in range(sz.heads):
        normed, unit, _ = norm_forward(x_refs[slot][...].astype(f32), gain, shift)
        at = slice(slot * sz.mine, (slot + 1) * sz.mine)
        n_ref[:, at] = normed.astype(bf16).T
        u_ref[:, at] = unit.astype(bf16).T


def both_levels(values, *where):
    high = values.astype(bf16).astype(f32)
    return collect(high, *where) + collect(values - high, *where)


def project_grad_kernel(sz, scal_ref, early_ref, *refs):
    far_refs, (send_ref, d_out_ref), refs = refs[:4], refs[4:6], refs[6:]
    got_ref, n_ref, u_ref, w_ref, d_ref, send_scr, sems = refs
    copies = [
        pltpu.make_async_copy(far_refs[i], ref, sems.at[i])
        for i, ref in enumerate((got_ref, n_ref, u_ref, w_ref))
    ]
    n_w = sz.w_chunk
    copies += [
        pltpu.make_async_copy(d_ref, d_out_ref, sems.at[4]),
        pltpu.make_async_copy(send_scr.at[:, :n_w], send_ref.at[:, :n_w], sems.at[5]),
        pltpu.make_async_copy(send_scr.at[:, n_w:], send_ref.at[:, n_w:], sems.at[6]),
    ]
    for copy in copies[:4]:
        copy.start()
    head = my_head_of(sz, scal_ref)
    half_run = sz.run // 2
    copies[0].wait()
    for slot in range(sz.heads):
        to = slot_head(sz, scal_ref, slot)
        q_at = pl.multiple_of(to * half_run, half_run)
        kv_at = pl.multiple_of(sz.half + to * sz.run, sz.run)
        for seq in range(sz.seqs):
            for part in range(sz.parts):
                at = slot * sz.mine + seq * sz.sub + part * sz.run
                first = got_ref[sz.task(seq, 0, part), pl.ds(q_at, half_run)]
                second = got_ref[sz.task(seq, 1, part), pl.ds(q_at, half_run)]
                low, high = halves(first, second)
                d_ref[at : at + half_run, :LANES] = low
                d_ref[at + half_run : at + sz.run, :LANES] = high
                for local in range(sz.local):
                    d_ref[at : at + sz.run, (1 + local) * LANES : (2 + local) * LANES] = got_ref[
                        sz.task(seq, local, part), pl.ds(kv_at, sz.run)
                    ]
    d_proj = d_ref[...]
    copies[4].start()
    copies[1].wait()
    grad_w = dot_nn(n_ref[...], d_proj).astype(bf16)
    for dev in range(sz.devices):
        rows = slice(dev * sz.w_rows, (dev + 1) * sz.w_rows)
        for i in range(1 + sz.local):
            cols = slice(i * LANES, (i + 1) * LANES)
            send_scr[dev, i * sz.w_rows : (i + 1) * sz.w_rows] = grad_w[rows, cols]
    copies[5].start()
    copies[2].wait()
    copies[3].wait()
    weights = w_ref[...].astype(f32)
    ones = jnp.ones((16, sz.tokens), bf16)
    column = dot_nn(ones, d_proj)[:SMALL]
    terms = [dot_nn(u_ref[...], d_proj) * weights, column[0:1] * weights]
    ones = jnp.ones((16, (1 + sz.local) * LANES), bf16)
    sums = []
    for term in terms:
        high = term.astype(bf16)
        low = (term - high.astype(f32)).astype(bf16)
        sums.append((dot_nt(ones, high) + dot_nt(ones, low))[0:1])
    wide = jnp.concatenate([*sums, jnp.zeros((SMALL - 2, sz.width), f32)], axis=0)
    sum_q = column[:, :LANES]
    sum_v = jnp.concatenate([column[:, LANES + HD : 2 * LANES], column[:, 2 * LANES + HD :]], axis=1)
    per = sz.w_rows
    small = (
        early_ref[...]
        + both_levels(wide, per, 0, (0, 2), sz.devices)
        + both_levels(sum_q, 2 * per, head * LANES, (6, 7), sz.devices)
        + both_levels(sum_v, 2 * per, sz.width + head * LANES, (6, 7), sz.devices)
    )
    send_scr[:, n_w:, :] = two_levels(small.reshape(sz.devices, SMALL, LANES))
    copies[6].start()
    for copy in copies[4:]:
        copy.wait()


def two_levels(small):
    high = small.astype(bf16).astype(f32)
    return jnp.concatenate([high, small - high], axis=-2).astype(bf16)


def input_partial_kernel(sz, scal_ref, d_ref, w_ref, *part_refs):
    grad_one = dot_nt(d_ref[...], w_ref[...])
    for slot, ref in enumerate(part_refs):
        ref[...] = grad_one[slot * sz.mine : (slot + 1) * sz.mine].astype(ref.dtype)


def input_grad_kernel(sz, scal_ref, vec_ref, grad_ref, x_ref, *refs):
    out_ref = refs[sz.heads]
    upstream = refs[0][...]
    for ref in refs[1 : sz.heads]:
        upstream = upstream + ref[...].astype(f32)
    gain, shift = vec_ref[0:1], vec_ref[1:2]
    _, unit, root = norm_forward(x_ref[...].astype(f32), gain, shift)
    out_ref[...] = (grad_ref[...] + norm_input_grad(upstream, unit, root, gain)).astype(bf16)


def split_kernel(sz, scal_ref, sum_a_ref, sum_b_ref, own_ref, *refs):
    n = sz.heads
    early_ref, refs = refs[-1], refs[:-1]
    wide = jnp.concatenate(
        [sum_a_ref[0:2], sum_b_ref[0:1], sum_a_ref[0:2], sum_b_ref[1:2], sum_a_ref[2:3]]
        + [jnp.zeros((1, sz.width), f32)],
        axis=0,
    )
    up_bias = jnp.broadcast_to(sum_a_ref[2:3], (SMALL, sz.width))
    at = my_head_of(sz, scal_ref) * sz.hidden_slice
    early_ref[...] = both_levels(wide, sz.w_rows, 0, (2, 6), sz.devices) + both_levels(
        up_bias, 4 * sz.w_rows, at, (7, 8), sz.devices
    )
    got_refs, feed_refs, refs = refs[: sz.groups - 1], refs[sz.groups - 1 :][: n - 1], refs[-n:]
    piece_ref, *send_refs = refs

    def total(rows):
        value = own_ref[rows]
        for ref in got_refs:
            value = value + ref[rows].astype(f32)
        return value

    for slot in range(n):
        to = slot_head(sz, scal_ref, slot)
        at = pl.multiple_of(to * sz.w_rows, sz.w_rows)
        up = total(pl.ds(at, sz.w_rows)).astype(bf16)
        out = total(pl.ds(at + n * sz.w_rows, sz.w_rows))
        ref = send_refs[slot - 1] if slot else piece_ref
        base = sz.mine if slot else 0
        if slot:
            ref[: sz.mine] = feed_refs[slot - 1][...]
        ref[base : base + sz.w_rows] = up
        ref[base + sz.w_rows :] = out.astype(bf16)


def final_kernel(sz, scal_ref, got_ref, *refs):
    piece_refs, refs = refs[: sz.heads], refs[sz.heads :]
    w_ref, up_ref, out_ref, *small_refs = refs
    out = piece_refs[0][sz.w_rows :].astype(f32)
    for ref in piece_refs[1:]:
        out = out + ref[sz.mine + sz.w_rows :].astype(f32)
    out_ref[...] = out
    for slot in range(sz.heads):
        at = pl.multiple_of(slot_head(sz, scal_ref, slot) * sz.hidden_slice, LANES)
        base = sz.mine if slot else 0
        piece = piece_refs[(sz.heads - slot) % sz.heads][base : base + sz.w_rows]
        up_ref[:, pl.ds(at, sz.hidden_slice)] = piece.astype(f32)
    for head in range(sz.heads):
        total = jnp.zeros((sz.w_chunk, LANES), f32)
        for blk in range(sz.blocks):
            total = total + got_ref[head * sz.blocks + blk, : sz.w_chunk].astype(f32)
        at = head * LANES
        w_ref[:, at : at + LANES] = total[: sz.w_rows]
        low, high = halves(total[sz.w_rows : 2 * sz.w_rows], total[2 * sz.w_rows :])
        w_ref[:, sz.width + at : sz.width + at + LANES] = low
        w_ref[:, 2 * sz.width + at : 2 * sz.width + at + LANES] = high
    small = jnp.sum(got_ref[:, sz.w_chunk :, :].astype(f32), axis=0)
    small = small[:SMALL] + small[SMALL:]
    for i, ref in enumerate(small_refs):
        ref[...] = small[i : i + 1, : ref.shape[1]]


BLK = ("group", "part")
ALL = ("head", "group", "part")


def on_device_fused(
    sz,
    layer_input,
    segments,
    token_valid,
    attention_gain,
    attention_shift,
    project_weight,
    project_bias,
    output_weight,
    output_bias,
    feed_gain,
    feed_shift,
    up_weight,
    up_bias,
    down_weight,
    down_bias,
    cotangent,
):
    n = sz.heads
    my_head = lax.axis_index("head")
    my_blk = lax.axis_index(BLK)
    scal = (my_head * sz.blocks + my_blk).astype(i32).reshape(1)
    geo = AttentionShape(sz.blocks, sz.part_rows, sz.parts, sz.run, sz.sub)
    token_shape = (sz.mine, sz.width)

    def call(kernel, name, arrays, outs, scratch=(), flops=10**8):
        return local_call(functools.partial(kernel, sz), name, scal, arrays, outs, scratch, flops)

    def around(x, step):
        return lax.ppermute(x, "head", [(i, (i + step) % n) for i in range(n)])

    def after(values, *earlier):
        return lax.optimization_barrier((values, *earlier))[0]

    def around_groups(x, step):
        pairs = [
            (g * sz.parts + p, (g + step) % sz.groups * sz.parts + p)
            for g in range(sz.groups)
            for p in range(sz.parts)
        ]
        return lax.ppermute(x, BLK, pairs)

    def around_parts(x, step):
        return lax.ppermute(x, BLK, within_group(sz.blocks, sz.parts, step))

    x_mine = layer_input.reshape(token_shape)
    g_mine = cotangent.reshape(token_shape)
    small = [attention_gain, attention_shift, output_bias, feed_gain, feed_shift, down_bias]
    small += [project_bias, up_bias]
    (send,) = staged_call(
        functools.partial(pack_kernel, sz),
        "pack",
        scal,
        [project_weight, *[v.reshape(1, -1) for v in small]],
        [((n * sz.groups, sz.w_chunk + SMALL, LANES), bf16)],
        [pltpu.VMEM((SMALL, LANES), f32)],
    )
    got = exchange(send, ("head", "group"))
    x_slots = [x_mine] + [around(after(x_mine, send), d) for d in range(1, n)]
    pieces = staged_call(
        functools.partial(pieces_kernel, sz),
        "pieces",
        after(scal, send),
        [g_mine, up_weight, output_weight],
        [((sz.mine + 2 * sz.w_rows, sz.width), bf16)] * n,
    )
    g_slots = [pieces[0]] + [around(after(pieces[d], x_slots[1]), d) for d in range(1, n)]
    got_parts = [got] + [around_parts(got, d) for d in range(1, sz.parts)]

    my_part = my_blk % sz.parts
    my_seq = (my_blk // sz.parts) // sz.local
    scalars, bounds = attention_bounds(
        segments, token_valid, my_seq, my_part, geo, sz.heads, sz.sub
    )
    got_parts[0] = after(got_parts[0], scalars, bounds, *pieces)
    send, w_slice, vec = call(
        project_kernel,
        "project",
        [*got_parts, *x_slots],
        [
            ((sz.blocks, sz.half + sz.part_rows, LANES), bf16),
            far((sz.width, (1 + sz.local) * LANES), bf16),
            far((SMALL, sz.width), f32),
        ],
        [pltpu.VMEM((sz.devices * SMALL, LANES), f32)],
        flops=30 * 10**9,
    )
    column = jnp.concatenate([v[sz.mine :] for v in g_slots], axis=0)
    columns = [column] + [around_groups(column, d) for d in range(1, sz.groups)]
    downs = [after(down_weight, x_slots[1])]
    downs += [around_groups(downs[0], d) for d in range(1, sz.groups)]
    task = exchange(send, BLK)
    task = after(task, column, *downs)
    others = [around_parts(task, step) for step in range(1, sz.parts)]
    o_task, ot, lse = attention_forward(geo, scalars, [task, *others], bounds)
    o_task = after(o_task, *columns)
    columns += [around_parts(after(v, o_task), d) for d in range(1, sz.parts) for v in columns]
    downs += [around_parts(after(v, o_task), d) for d in range(1, sz.parts) for v in downs]
    square = ((sz.width, sz.width), bf16)
    w_up, w_out, w_down = call(assemble_kernel, "assemble", [*columns, *downs], [square] * 3)
    mixed = exchange(o_task, BLK)
    turned = far((sz.width, sz.tokens), bf16)
    n_one, u_one = call(
        norm_again_kernel, "norm_again", [after(vec, o_task), *x_slots], [turned, turned]
    )
    mixed = after(mixed, n_one)
    m_slots = [mixed] + [around(mixed, d) for d in range(1, n)]

    outs = call(
        feed_kernel,
        "feed",
        [vec, w_up, w_out, w_down, *x_slots, *g_slots, *m_slots],
        [far(token_shape, f32)]
        + [(token_shape, bf16)] * (n - 1)
        + [far(token_shape, f32)]
        + [far(token_shape, bf16)] * (n - 1)
        + [far(token_shape, f32)]
        + [((n, sz.mine, sz.hidden_slice), bf16)] * 2
        + [((n, *token_shape), bf16), far(token_shape, bf16), far((SMALL, sz.width), f32)],
        [
            pltpu.VMEM((n, *token_shape), bf16),
        ],
        flops=30 * 10**9,
    )
    grad_two, feed = outs[:n], outs[n : 2 * n]
    middle, activated, grad_hidden, n_two, mixed_own, feed_sums = outs[2 * n :]
    grad_two = [grad_two[0]] + [around(grad_two[d], -d) for d in range(1, n)]

    def shared(rows):
        shape = (sz.groups, rows, sz.width)
        return [far(shape, f32), far(shape, bf16)]

    keep, give = call(
        feed_grad_kernel,
        "feed_grad",
        [activated, grad_hidden, n_two, *g_slots],
        shared(sz.f_rows + n * sz.w_rows),
    )
    grad_two[0] = after(grad_two[0], keep)

    grad_middle, branch, send, branch_sums, keep_out, give_out = call(
        middle_grad_kernel,
        "middle_grad",
        [vec, w_out, middle, g_mine, mixed_own, *grad_two],
        [
            far(token_shape, f32),
            far(token_shape, bf16),
            ((sz.devices, sz.run // 2, LANES), bf16),
            far((SMALL, sz.width), f32),
            *shared(n * sz.w_rows),
        ],
        flops=30 * 10**9,
    )
    do_task = exchange(send, ALL)
    given = around_parts(give, 1)
    down_shape, rest_shape = (sz.f_rows, sz.width), (2 * n * sz.w_rows, sz.width)
    sums = call(
        part_sum_kernel,
        "part_sum",
        [keep, given, keep_out, around_parts(give_out, 1)],
        [far(down_shape, f32)]
        + [far(down_shape, bf16)] * (sz.groups - 1)
        + [far(rest_shape, f32)]
        + [(rest_shape, bf16)] * (sz.groups - 1),
    )
    down_sum, w_sum = sums[: sz.groups], sums[sz.groups :]
    w_pieces = [around_groups(w_sum[d], d) for d in range(1, sz.groups)]
    dq, dkv, *dkv_others = attention_backward(
        geo, do_tile_grouped, scalars, [task, *others], do_task, bounds, ot, lse
    )
    dkv_others[0] = after(dkv_others[0], *w_pieces)
    for step in range(1, sz.parts):
        back = within_group(sz.blocks, sz.parts, -step)
        dkv = dkv + lax.ppermute(dkv_others[step - 1], BLK, back).astype(f32)
    send = jnp.concatenate([dq, dkv.astype(bf16)], axis=1)
    got = exchange(send, BLK)
    piece, *rest = call(
        split_kernel,
        "split",
        [feed_sums, branch_sums, after(w_sum[0], send), *w_pieces, *feed[1:]],
        [far((2 * sz.w_rows, sz.width), bf16)]
        + [far((sz.mine + 2 * sz.w_rows, sz.width), bf16)] * (n - 1)
        + [far((sz.devices * SMALL, LANES), f32)],
    )
    early = rest.pop()
    rest = [around(v, -d - 1) for d, v in enumerate(rest)]
    got = after(got, *rest)
    wide = (1 + sz.local) * LANES
    send_shape = (sz.devices, sz.w_chunk + 2 * SMALL, LANES)
    send, d_proj = pl.pallas_call(
        functools.partial(project_grad_kernel, sz),
        out_shape=(pltpu.HBM(send_shape, bf16), pltpu.HBM((sz.tokens, wide), bf16)),
        in_specs=[pl.BlockSpec(memory_space=pltpu.SMEM), pl.BlockSpec(memory_space=pltpu.VMEM)]
        + [pl.BlockSpec(memory_space=pltpu.HBM)] * 4,
        out_specs=tuple([pl.BlockSpec(memory_space=pltpu.HBM)] * 2),
        scratch_shapes=[
            pltpu.VMEM(got.shape, bf16),
            pltpu.VMEM((sz.width, sz.tokens), bf16),
            pltpu.VMEM((sz.width, sz.tokens), bf16),
            pltpu.VMEM((sz.width, wide), bf16),
            pltpu.VMEM((sz.tokens, wide), bf16),
            pltpu.VMEM(send_shape, bf16),
            pltpu.SemaphoreType.DMA((7,)),
        ],
        compiler_params=pltpu.CompilerParams(vmem_limit_bytes=63 * 2**20),
        cost_estimate=pl.CostEstimate(flops=30 * 10**9, bytes_accessed=10**6, transcendentals=0),
        name="project_grad",
    )(scal, early, got, n_one, u_one, w_slice)
    got = exchange(send, ALL)
    outs = call(
        input_partial_kernel,
        "input_partial",
        [d_proj, w_slice],
        [(token_shape, f32)] + [(token_shape, bf16)] * (n - 1),
    )
    grad_one = [outs[0]] + [around(outs[d], -d) for d in range(1, n)]
    down_grad = down_sum[0]
    for d in range(1, sz.groups):
        down_grad = down_grad + around_groups(after(down_sum[d], grad_one[1]), d).astype(f32)
    (input_grad,) = call(
        input_grad_kernel,
        "input_grad",
        [vec, grad_middle, x_mine, *grad_one],
        [(token_shape, bf16)],
    )
    layer_output = middle + feed[0] + vec[5:6]
    for v in rest:
        layer_output = layer_output + v[: sz.mine].astype(f32)
    layer_output = layer_output.astype(bf16)
    w_grad, up_grad, out_grad, *owned = call(
        final_kernel,
        "final",
        [got, piece, *rest],
        [
            ((sz.w_rows, 3 * sz.width), f32),
            ((sz.w_rows, n * sz.hidden_slice), f32),
            ((sz.w_rows, sz.width), f32),
        ]
        + [((1, v.shape[0]), f32) for v in small],
    )
    owned = [v.reshape(-1) for v in owned]
    return (
        layer_output.reshape(layer_input.shape),
        input_grad.reshape(layer_input.shape),
        owned[0],
        owned[1],
        w_grad,
        owned[6],
        out_grad,
        owned[2],
        owned[3],
        owned[4],
        up_grad,
        owned[7],
        down_grad,
        owned[5],
    )


def solution(mesh):
    heads, blocks = mesh.shape["head"], mesh.shape["blk"]

    def layer(*arguments):
        layer_input, up_weight = arguments[0], arguments[11]
        seqs, _, tokens, width = layer_input.shape
        sz = Sizes(heads, blocks, seqs, tokens // heads, width, up_weight.shape[1])
        if sz.fits():
            split = (heads, blocks // sz.parts, sz.parts)
            inner = jax.sharding.Mesh(mesh.devices.reshape(split), ALL)
            body, blk, everywhere = functools.partial(on_device_fused, sz), BLK, ALL
        else:
            inner, body, blk, everywhere = mesh, on_device_general, "blk", BOTH
        rows = P(None, blk, "head", None)
        vector, matrix = P(everywhere), P(everywhere, None)
        weights = (vector, vector, matrix, vector, matrix, vector)
        weights += (vector, vector, matrix, vector, matrix, vector)
        return jax.shard_map(
            body,
            mesh=inner,
            in_specs=(rows, P(), P(), *weights, rows),
            out_specs=(rows, rows, *weights),
            check_vma=False,
        )(*arguments)

    return layer
```

```python
import functools

import jax
import jax.numpy as jnp
from jax import lax
from jax.experimental import pallas as pl
from jax.experimental.pallas import tpu as pltpu
from jax.sharding import PartitionSpec as P

H = 8
HD = 64
LANES = 128
EPSILON = 1e-05
NEG_FILL = -1e30
TILE_Q = 256

bf16 = jnp.bfloat16
f32 = jnp.float32
i32 = jnp.int32
BOTH = ("head", "blk")


def dot_nn(a, b):
    return lax.dot_general(a, b, (((1,), (0,)), ((), ())), preferred_element_type=f32)


def dot_nt(a, b):
    return lax.dot_general(a, b, (((1,), (1,)), ((), ())), preferred_element_type=f32)


def dot_tn(a, b):
    return lax.dot_general(a, b, (((0,), (0,)), ((), ())), preferred_element_type=f32)


def norm_forward(values, gain, shift):
    centred = values - jnp.mean(values, axis=-1, keepdims=True)
    variance = jnp.mean(centred * centred, axis=-1, keepdims=True)
    inverse_root = lax.rsqrt(variance + EPSILON)
    unit_value = centred * inverse_root
    return (unit_value * gain + shift, unit_value, inverse_root)


def norm_input_grad(upstream, unit_value, inverse_root, gain):
    scaled = upstream * gain
    inner = scaled - jnp.mean(scaled, axis=-1, keepdims=True)
    inner = inner - unit_value * jnp.mean(scaled * unit_value, axis=-1, keepdims=True)
    return inverse_root * inner


class AttentionShape:
    def __init__(self, blocks, part_rows, parts, run, stride):
        self.blocks = blocks
        self.per_tile = max(1, TILE_Q // part_rows)
        self.tiles = blocks // self.per_tile
        self.tile = self.per_tile * part_rows
        self.part_rows = part_rows
        self.half = part_rows // 2
        self.parts = parts
        self.run = run
        self.stride = stride
        self.span = self.tile * parts


def unpack_rows(packed):
    return jnp.concatenate([packed[:, :HD], packed[:, HD:]], axis=0)


def pack_rows(rows):
    half = rows.shape[0] // 2
    return jnp.concatenate([rows[:half], rows[half:]], axis=1)


def key_base(geo):
    rows = lax.broadcasted_iota(i32, (geo.tile, 1), 0)
    return (rows // geo.run) * geo.stride + rows % geo.run


def task_tile(ref, geo, tile, first, count):
    block = ref[pl.ds(tile * geo.per_tile, geo.per_tile), first : first + count, :]
    return block.reshape(geo.per_tile * count, LANES)


ONES = 16
CHUNKS_AT_ONCE = 4


def forward_kernel(geo, scal_ref, *refs):
    part_refs = refs[: geo.parts]
    bounds_ref, out_ref, ot_ref, lse_ref, vt_ref = refs[geo.parts :]
    base = jnp.broadcast_to(key_base(geo), (geo.tile, geo.tile))
    ones = jnp.ones((ONES, geo.tile), bf16)
    for part in range(geo.parts):
        for tile in range(geo.tiles):
            keys = task_tile(part_refs[part], geo, tile, geo.half, geo.part_rows)
            vt_ref[part, tile, :ONES] = ones
            vt_ref[part, tile, ONES:] = keys.T[HD:]
    for tile in range(geo.tiles):
        q = unpack_rows(task_tile(part_refs[0], geo, tile, 0, geo.half))
        q = q * jnp.asarray(HD**-0.5, bf16)
        qz = jnp.concatenate([q, jnp.zeros_like(q)], axis=1)
        start = bounds_ref[tile, 0:1]
        last = bounds_ref[tile, 1:2]
        own = bounds_ref[tile, 2:3]

        def step(key_tiles, carry):
            chunks = [(key_tile, part) for key_tile in key_tiles for part in range(geo.parts)]
            for at in range(0, len(chunks), CHUNKS_AT_ONCE):
                carry = some(chunks[at : at + CHUNKS_AT_ONCE], carry)
            return carry

        def some(chunks, carry):
            run_max, acc = carry
            masked = []
            new_max = run_max
            for key_tile, part in chunks:
                offset = key_tile * geo.span + scal_ref[part]
                keys = task_tile(part_refs[part], geo, key_tile, geo.half, geo.part_rows)
                scores = dot_nt(keys, qz)
                allowed = (base >= start - offset) & (base <= last - offset)
                if key_tile == tile and part == 0:
                    allowed = allowed | (base == own - offset)
                masked.append(jnp.where(allowed, scores, NEG_FILL))
                new_max = jnp.maximum(new_max, jnp.max(masked[-1], axis=0, keepdims=True))
            acc = acc * jnp.exp(run_max - new_max)
            for (key_tile, part), scores in zip(chunks, masked):
                probs = jnp.exp(scores - new_max).astype(bf16)
                acc = acc + dot_nn(vt_ref[part, key_tile], probs)
            return (new_max, acc)

        carry = (
            jnp.full((1, geo.tile), NEG_FILL, f32),
            jnp.zeros((ONES + HD, geo.tile), f32),
        )
        near = max(0, tile - 1)
        carry = step(range(tile, near - 1, -1), carry)
        if near:
            carry = lax.cond(
                scal_ref[geo.parts + tile] < near,
                functools.partial(step, range(near)),
                lambda same: same,
                carry,
            )
        run_max, acc = carry
        run_sum = acc[0:1]
        attended = acc[ONES:] / run_sum
        ot_ref[tile] = attended
        lse_ref[tile] = jnp.broadcast_to(run_max + jnp.log(run_sum), (8, geo.tile))
        packed = pack_rows(attended.T).astype(bf16)
        for i in range(geo.per_tile):
            out_ref[tile * geo.per_tile + i] = packed[i * geo.half : (i + 1) * geo.half]


def backward_kernel(geo, do_tile, scal_ref, *refs):
    part_refs = refs[: geo.parts]
    do_ref, bounds_ref, ot_ref, lse_ref, dq_ref = refs[geo.parts : geo.parts + 5]
    grad_refs = refs[geo.parts + 5 : 2 * geo.parts + 5]
    acc_ref, kvt_ref = refs[2 * geo.parts + 5 :]
    base = jnp.broadcast_to(key_base(geo), (geo.tile, geo.tile))
    acc_ref[...] = jnp.zeros_like(acc_ref)
    for part in range(geo.parts):
        for tile in range(geo.tiles):
            keys = task_tile(part_refs[part], geo, tile, geo.half, geo.part_rows)
            kvt_ref[part, tile] = keys.T
    for tile in range(geo.tiles):
        q = unpack_rows(task_tile(part_refs[0], geo, tile, 0, geo.half))
        q = q * jnp.asarray(HD**-0.5, bf16)
        do = unpack_rows(do_tile(do_ref, geo, tile))
        zeros = jnp.zeros_like(q)
        qz = jnp.concatenate([q, zeros], axis=1)
        doz = jnp.concatenate([zeros, do], axis=1)
        q_do = jnp.concatenate([qz, doz], axis=0)
        delta = jnp.sum(do.astype(f32).T * ot_ref[tile], axis=0, keepdims=True)
        log_total = lse_ref[tile, 0:1]
        start = bounds_ref[tile, 0:1]
        last = bounds_ref[tile, 1:2]
        own = bounds_ref[tile, 2:3]

        def chunk(part, key_tile, acc):
            offset = key_tile * geo.span + scal_ref[part]
            keys = task_tile(part_refs[part], geo, key_tile, geo.half, geo.part_rows)
            scores = dot_nt(keys, qz)
            allowed = (base >= start - offset) & (base <= last - offset)
            if key_tile == tile and part == 0:
                allowed = allowed | (base == own - offset)
            probs = jnp.exp(jnp.where(allowed, scores, NEG_FILL) - log_total)
            grad_probs = dot_nt(keys, doz)
            grad_scores = (probs * (grad_probs - delta)).astype(bf16)
            both = jnp.concatenate([grad_scores, probs.astype(bf16)], axis=1)
            acc_ref[part, key_tile] += dot_nn(both, q_do)
            return acc + dot_nn(kvt_ref[part, key_tile], grad_scores)

        def step(key_tiles, acc):
            for key_tile in key_tiles:
                for part in range(geo.parts):
                    acc = chunk(part, key_tile, acc)
            return acc

        near = max(0, tile - 1)
        acc = step(range(tile, near - 1, -1), jnp.zeros((2 * HD, geo.tile), f32))
        if near:
            acc = lax.cond(
                scal_ref[geo.parts + tile] < near,
                functools.partial(step, range(near)),
                lambda same: same,
                acc,
            )
        packed = pack_rows((acc[:HD] * (HD**-0.5)).T).astype(bf16)
        for i in range(geo.per_tile):
            dq_ref[tile * geo.per_tile + i] = packed[i * geo.half : (i + 1) * geo.half]
    for part in range(geo.parts):
        for tile in range(geo.tiles):
            for i in range(geo.per_tile):
                rows = acc_ref[part, tile, i * geo.part_rows : (i + 1) * geo.part_rows]
                grad_refs[part][tile * geo.per_tile + i] = rows.astype(grad_refs[part].dtype)


COST = {
    "assemble": 100000000,
    "attention_backward": 30000000000,
    "attention_forward": 30000000000,
    "feed": 30000000000,
    "feed_grad": 100000000,
    "final": 100000000,
    "fold": 30000000000,
    "input_grad": 100000000,
    "input_partial": 30000000000,
    "middle_grad": 30000000000,
    "norm_again": 100000000,
    "part_sum": 30000000000,
    "project": 30000000000,
    "project_grad": 30000000000,
    "split": 100000000,
}


VMEM_LIMIT = 16 * 2**20


def far(shape, dtype):
    return (pltpu.HBM(shape, dtype),)


def local_call(kernel, name, scalars, arrays, outs, scratch=(), limit=VMEM_LIMIT):
    return pl.pallas_call(
        kernel,
        out_shape=tuple(o[0] if len(o) == 1 else jax.ShapeDtypeStruct(*o) for o in outs),
        in_specs=[pl.BlockSpec(memory_space=pltpu.SMEM)]
        + [pl.BlockSpec(memory_space=pltpu.VMEM)] * len(arrays),
        out_specs=tuple([pl.BlockSpec(memory_space=pltpu.VMEM)] * len(outs)),
        scratch_shapes=list(scratch),
        compiler_params=pltpu.CompilerParams(vmem_limit_bytes=limit),
        cost_estimate=pl.CostEstimate(flops=COST.get(name, 10**8), bytes_accessed=10**6, transcendentals=0),
        name=name,
    )(scalars, *arrays)


def attention_limit(geo):
    return VMEM_LIMIT if geo.parts == 2 else 3 * VMEM_LIMIT


def attention_forward(geo, scalars, part_arrays, bounds):
    return local_call(
        functools.partial(forward_kernel, geo),
        "attention_forward",
        scalars,
        [*part_arrays, bounds],
        [
            ((geo.blocks, geo.half, LANES), bf16),
            far((geo.tiles, HD, geo.tile), f32),
            far((geo.tiles, 8, geo.tile), f32),
        ],
        [pltpu.VMEM((geo.parts, geo.tiles, ONES + HD, geo.tile), bf16)],
        limit=attention_limit(geo),
    )


def attention_backward(geo, do_tile, scalars, part_arrays, do, bounds, ot, lse):
    grads = [((geo.blocks, geo.part_rows, LANES), f32)]
    grads += [((geo.blocks, geo.part_rows, LANES), bf16)] * (geo.parts - 1)
    return local_call(
        functools.partial(backward_kernel, geo, do_tile),
        "attention_backward",
        scalars,
        [*part_arrays, do, bounds, ot, lse],
        [((geo.blocks, geo.half, LANES), bf16), *grads],
        [
            pltpu.VMEM((geo.parts, geo.tiles, geo.tile, LANES), f32),
            pltpu.VMEM((geo.parts, geo.tiles, LANES, geo.tile), bf16),
        ],
        limit=attention_limit(geo),
    )


def do_tile_grouped(do_ref, geo, tile):
    heads = do_ref.shape[0] // geo.blocks
    pieces = []
    for i in range(geo.per_tile):
        for head in range(heads):
            pieces.append(do_ref[head * geo.blocks + tile * geo.per_tile + i])
    return jnp.concatenate(pieces, axis=0)


def do_tile_plain(do_ref, geo, tile):
    return task_tile(do_ref, geo, tile, 0, geo.half)


def query_positions(blocks, heads, run, sub, part, geo):
    half = run // 2
    block = jnp.arange(blocks, dtype=i32).reshape(geo.tiles, 1, geo.per_tile, 1, 1)
    upper = jnp.arange(2, dtype=i32).reshape(1, 2, 1, 1, 1)
    head = jnp.arange(heads, dtype=i32).reshape(1, 1, 1, heads, 1)
    row = jnp.arange(half, dtype=i32).reshape(1, 1, 1, 1, half)
    at = block * (heads * sub) + head * sub + part * run + upper * half + row
    return at.reshape(geo.tiles, 1, geo.tile)


def attention_bounds(segments, token_valid, my_seq, my_part, geo, heads, sub):
    seg = lax.dynamic_index_in_dim(segments, my_seq, 0, keepdims=False)
    valid = jnp.sum(lax.dynamic_index_in_dim(token_valid, my_seq, 0, keepdims=False))
    own = query_positions(geo.blocks, heads, geo.run, sub, my_part, geo)
    half = geo.run // 2
    own_seg = seg.reshape(geo.blocks * heads, geo.parts, geo.run)
    own_seg = lax.dynamic_index_in_dim(own_seg, my_part, 1, keepdims=False)
    own_seg = own_seg.reshape(geo.tiles, geo.per_tile, heads, 2, half).transpose(0, 3, 1, 2, 4)
    own_seg = own_seg.reshape(-1, 1)
    start = jnp.sum((seg[None, :] < own_seg).astype(i32), axis=1).reshape(geo.tiles, 1, geo.tile)
    last = jnp.minimum(own, valid - 1)
    bounds = jnp.concatenate([start, last, own, jnp.zeros((geo.tiles, 5, geo.tile), i32)], axis=1)
    first_seg = seg.reshape(geo.tiles, geo.span)[:, :1]
    first_tile = jnp.sum((seg[None, :] < first_seg).astype(i32), axis=1) // geo.span
    part_at = ((my_part - jnp.arange(geo.parts, dtype=i32)) % geo.parts) * geo.run
    return jnp.concatenate([part_at, first_tile]), bounds


def gather_head(x):
    return lax.all_gather(x, "head", axis=0, tiled=False)


def exchange(x, axis):
    return lax.all_to_all(x, axis, split_axis=0, concat_axis=0, tiled=True)


def within_group(blocks, parts, step):
    return [
        (t * parts + i, t * parts + (i + step) % parts)
        for t in range(blocks // parts)
        for i in range(parts)
    ]


def on_device_general(
    layer_input,
    segments,
    token_valid,
    attention_gain,
    attention_shift,
    project_weight,
    project_bias,
    output_weight,
    output_bias,
    feed_gain,
    feed_shift,
    up_weight,
    up_bias,
    down_weight,
    down_bias,
    cotangent,
):
    heads = lax.axis_size("head")
    blocks = lax.axis_size("blk")
    my_head = lax.axis_index("head")
    my_blk = lax.axis_index("blk")
    devices = heads * blocks
    seqs, _, sub, width = layer_input.shape
    hidden_width = up_weight.shape[1]
    hidden_slice = hidden_width // heads
    rows = sub * heads
    length = rows * blocks
    mine = seqs * sub
    tokens = seqs * rows
    local = H // heads
    cols = local * HD
    parts = blocks // (seqs * local)
    run = sub // parts
    part_rows = heads * run
    half = part_rows // 2
    w_rows = width // devices
    f_rows = hidden_width // devices
    geo = AttentionShape(blocks, part_rows, parts, run, sub)

    wp = project_weight.reshape(w_rows, 3, heads, local, HD)
    wq = wp[:, 0].transpose(1, 0, 2, 3).reshape(heads, w_rows, cols)
    wq = jnp.pad(wq, ((0, 0), (0, 0), (0, LANES - cols)))
    wkv = wp[:, 1:].transpose(2, 3, 0, 1, 4).reshape(heads, local * w_rows, LANES)
    small = [attention_gain, attention_shift, output_bias, feed_gain, feed_shift, down_bias]
    small += [project_bias, up_bias]
    counts = [v.shape[0] for v in small]
    small = jnp.concatenate(small)
    small_rows = -(-small.shape[0] // LANES)
    small = jnp.pad(small, (0, small_rows * LANES - small.shape[0])).reshape(1, small_rows, LANES)
    chunk = jnp.concatenate([wq, wkv, jnp.broadcast_to(small, (heads, small_rows, LANES))], axis=1)
    chunk_rows = chunk.shape[1]
    send = jnp.broadcast_to(chunk[:, None], (heads, blocks, chunk_rows, LANES))
    got = exchange(send.reshape(devices, chunk_rows, LANES), BOTH)
    w_groups = [
        got[:, i * w_rows : (i + 1) * w_rows].reshape(width, LANES) for i in range(1 + local)
    ]
    w_slice = jnp.concatenate(w_groups, axis=1)
    flat = got[:, (1 + local) * w_rows :].reshape(devices, small_rows * LANES).astype(f32)
    vectors = []
    at = 0
    for count in counts:
        vectors.append(flat[:, at : at + count].reshape(-1))
        at += count
    gain_one, shift_one, b_output, gain_two, shift_two, b_down, b_project, b_up = vectors

    x_mine = layer_input.reshape(mine, width)
    g_mine = cotangent.reshape(mine, width)
    x_all = gather_head(x_mine).reshape(heads, seqs, sub, width).transpose(1, 0, 2, 3)
    g_all = gather_head(g_mine).reshape(heads, seqs, sub, width).transpose(1, 0, 2, 3)
    x_all = x_all.reshape(tokens, width).astype(f32)
    g_all = g_all.reshape(tokens, width)

    up_parts = up_weight.reshape(w_rows, heads, hidden_slice).transpose(1, 0, 2)
    out_parts = jnp.broadcast_to(output_weight[None], (heads, w_rows, width))
    if hidden_slice == width:
        both = exchange(jnp.concatenate([up_parts, out_parts], axis=1), "head")
        shard = jnp.concatenate([both.reshape(2 * heads * w_rows, width), down_weight], axis=0)
        full = lax.all_gather(shard, "blk", axis=0, tiled=False)
        pair = full[:, : 2 * heads * w_rows].reshape(blocks, heads, 2, w_rows, width)
        w_up = pair[:, :, 0].transpose(1, 0, 2, 3).reshape(width, hidden_slice)
        w_out = pair[:, :, 1].transpose(1, 0, 2, 3).reshape(width, width)
        w_down = full[:, 2 * heads * w_rows :].reshape(hidden_slice, width)
    else:
        up_parts = lax.all_gather(exchange(up_parts, "head"), "blk", axis=0, tiled=False)
        out_parts = lax.all_gather(exchange(out_parts, "head"), "blk", axis=0, tiled=False)
        w_up = up_parts.transpose(1, 0, 2, 3).reshape(width, hidden_slice)
        w_out = out_parts.transpose(1, 0, 2, 3).reshape(width, width)
        w_down = lax.all_gather(down_weight, "blk", axis=0, tiled=True)

    n_one, u_one, rs_one = norm_forward(x_all, gain_one, shift_one)
    n_one = n_one.astype(bf16)
    qkv = dot_nn(n_one, w_slice)
    b_q = lax.dynamic_slice(b_project, (my_head * cols,), (cols,))
    b_v = lax.dynamic_slice(b_project, (width + my_head * cols,), (cols,))
    queries = (qkv[:, :cols] + b_q).astype(bf16)
    pairs = qkv[:, LANES:].reshape(tokens, local, 2, HD)
    b_pair = jnp.stack([jnp.zeros((local, HD), f32), b_v.reshape(local, HD)], axis=1)
    pairs = (pairs + b_pair).astype(bf16)
    queries = queries.reshape(seqs, heads, parts, 2, run // 2, local, HD)
    queries = queries.transpose(0, 5, 2, 1, 4, 3, 6).reshape(blocks, half, LANES)
    pairs = pairs.reshape(seqs, heads, parts, run, local, LANES).transpose(0, 4, 2, 1, 3, 5)
    pairs = pairs.reshape(blocks, part_rows, LANES)
    task = exchange(jnp.concatenate([queries, pairs], axis=1), "blk")
    part_arrays = [task]
    for step in range(1, parts):
        part_arrays.append(lax.ppermute(task, "blk", within_group(blocks, parts, step)))

    my_part = my_blk % parts
    my_seq = (my_blk // parts) // local
    scalars, bounds = attention_bounds(segments, token_valid, my_seq, my_part, geo, heads, sub)
    o_task, ot, lse = attention_forward(geo, scalars, part_arrays, bounds)

    got = exchange(o_task, "blk")
    mixed = got.reshape(seqs, local, parts, heads, run // 2, 2, HD)
    mixed = mixed.transpose(0, 3, 2, 5, 4, 1, 6)
    mixed = mixed.reshape(tokens, cols)
    mixed_all = lax.all_gather(mixed, "head", axis=1, tiled=True)

    middle = x_all + dot_nn(mixed_all, w_out) + b_output
    n_two, u_two, rs_two = norm_forward(middle, gain_two, shift_two)
    n_two = n_two.astype(bf16)
    b_up_slice = lax.dynamic_slice(b_up, (my_head * hidden_slice,), (hidden_slice,))
    hidden = dot_nn(n_two, w_up) + b_up_slice
    sigma = jax.nn.sigmoid(1.702 * hidden)
    activated = (hidden * sigma).astype(bf16)
    feed = dot_nn(activated, w_down)
    grad_act = dot_nt(g_all, w_down)
    grad_hidden = (grad_act * (sigma + 1.702 * hidden * sigma * (1.0 - sigma))).astype(bf16)
    grad_two = dot_nt(grad_hidden, w_up)

    def to_owners(partial):
        partial = partial.astype(bf16).reshape(seqs, heads, sub, width).transpose(1, 0, 2, 3)
        return exchange(partial.reshape(heads, mine, width), "head")

    def my_tokens(values):
        values = values.reshape(seqs, heads, sub, values.shape[-1])
        values = lax.dynamic_index_in_dim(values, my_head, 1, keepdims=False)
        return values.reshape(mine, values.shape[-1])

    grad_two_mine = jnp.sum(to_owners(grad_two).astype(f32), axis=0)
    grad_middle = g_mine.astype(f32) + norm_input_grad(
        grad_two_mine, my_tokens(u_two), my_tokens(rs_two), gain_two
    )
    grad_branch = grad_middle.astype(bf16)
    grad_mixed = dot_nt(grad_branch, w_out).astype(bf16)
    grad_mixed = grad_mixed.reshape(seqs, parts, 2, run // 2, heads, local, HD)
    grad_mixed = grad_mixed.transpose(4, 0, 5, 1, 3, 2, 6).reshape(devices, run // 2, LANES)
    got = exchange(grad_mixed, BOTH).reshape(heads, blocks, run // 2, LANES)
    do_task = got.transpose(1, 0, 2, 3).reshape(blocks, half, LANES)

    feed_mine = jnp.sum(to_owners(feed).astype(f32), axis=0)
    layer_output = my_tokens(middle) + feed_mine + b_down

    grad_down = dot_tn(activated, g_all).astype(bf16).reshape(blocks, -1, width)
    grad_up = dot_tn(n_two, grad_hidden).astype(bf16)
    grad_up = grad_up.reshape(heads, blocks, w_rows, hidden_slice).transpose(1, 0, 2, 3)
    branch_all = gather_head(grad_branch).reshape(heads, seqs, sub, width).transpose(1, 0, 2, 3)
    grad_out = dot_tn(mixed, branch_all.reshape(tokens, width)).astype(bf16)

    def over_blocks(partial):
        return lax.psum_scatter(partial, "blk", scatter_dimension=0, tiled=True)

    if hidden_slice == width:
        summed = over_blocks(
            jnp.concatenate(
                [grad_down.reshape(blocks, f_rows, width), grad_up.reshape(blocks, -1, width)],
                axis=1,
            ).reshape(-1, width)
        )
        own_down = summed[:f_rows]
        own_up = summed[f_rows:]
    else:
        own_down = over_blocks(grad_down.reshape(-1, width))
        own_up = over_blocks(grad_up.reshape(-1, hidden_slice))
    own_out = over_blocks(grad_out)
    own_up = exchange(own_up.reshape(heads, w_rows, hidden_slice), "head")
    own_up = own_up.transpose(1, 0, 2).reshape(w_rows, hidden_width)

    dq_task, dkv, *others = attention_backward(
        geo, do_tile_plain, scalars, part_arrays, do_task, bounds, ot, lse
    )
    for step in range(1, parts):
        back = within_group(blocks, parts, -step)
        dkv = dkv + lax.ppermute(others[step - 1], "blk", back).astype(f32)
    got = exchange(jnp.concatenate([dq_task, dkv.astype(bf16)], axis=1), "blk")
    dq = got[:, :half].reshape(seqs, local, parts, heads, run // 2, 2, HD)
    dq = dq.transpose(0, 3, 2, 5, 4, 1, 6)
    dq = dq.reshape(tokens, cols)
    dkv = got[:, half:].reshape(seqs, local, parts, heads, run, LANES).transpose(0, 3, 2, 4, 1, 5)
    dkv = dkv.reshape(tokens, local * LANES)
    dq = jnp.pad(dq, ((0, 0), (0, LANES - cols)))
    d_proj = jnp.concatenate([dq, dkv], axis=1)

    grad_one = dot_nt(d_proj, w_slice)
    grad_one_mine = jnp.sum(to_owners(grad_one).astype(f32), axis=0)
    x_f32 = x_mine.astype(f32)
    input_grad = grad_middle + norm_input_grad(
        grad_one_mine, my_tokens(u_one), my_tokens(rs_one), gain_one
    )

    grad_w = dot_tn(n_one, d_proj).astype(bf16)
    col_sums = jnp.sum(d_proj.astype(f32), axis=0)
    bias_q = col_sums[:cols]
    bias_v = col_sums[LANES:].reshape(local, 2, HD)[:, 1].reshape(cols)
    bias_grad = jnp.zeros((2 * width,), f32)
    bias_grad = lax.dynamic_update_slice(bias_grad, bias_q, (my_head * cols,))
    bias_grad = lax.dynamic_update_slice(bias_grad, bias_v, (width + my_head * cols,))
    up_bias_grad = lax.dynamic_update_slice(
        jnp.zeros((hidden_width,), f32),
        jnp.sum(grad_hidden.astype(f32), axis=0),
        (my_head * hidden_slice,),
    )
    tiny = [
        jnp.sum(grad_one * u_one, axis=0),
        jnp.sum(grad_one, axis=0),
        jnp.sum(grad_branch.astype(f32), axis=0),
        jnp.sum(grad_two * u_two, axis=0),
        jnp.sum(grad_two, axis=0),
        jnp.sum(g_mine.astype(f32), axis=0),
        bias_grad,
        up_bias_grad,
    ]
    tiny = jnp.concatenate([v.reshape(devices, -1) for v in tiny], axis=1)
    high = tiny.astype(bf16)
    low = (tiny - high.astype(f32)).astype(bf16)
    tiny = jnp.concatenate([high, low], axis=1)
    tiny_rows = -(-tiny.shape[1] // LANES)
    tiny = jnp.pad(tiny, ((0, 0), (0, tiny_rows * LANES - tiny.shape[1])))
    tiny = tiny.reshape(devices, tiny_rows, LANES)
    grad_w = [
        grad_w[:, i * LANES : (i + 1) * LANES].reshape(devices, w_rows, LANES)
        for i in range(1 + local)
    ]
    got = exchange(jnp.concatenate(grad_w + [tiny], axis=1), BOTH)
    got = got.astype(f32)
    n_w = (1 + local) * w_rows
    own_w = jnp.sum(got[:, :n_w].reshape(heads, blocks, n_w, LANES), axis=1)
    own_q = own_w[:, :w_rows, :cols].transpose(1, 0, 2).reshape(w_rows, width)
    own_kv = own_w[:, w_rows:].reshape(heads, local, w_rows, 2, HD)
    own_kv = own_kv.transpose(2, 3, 0, 1, 4).reshape(w_rows, 2 * width)
    own_w = jnp.concatenate([own_q, own_kv], axis=1)
    summed = jnp.sum(got[:, n_w:].reshape(devices, -1), axis=0)
    total = sum(counts)
    summed = summed[:total] + summed[total : 2 * total]
    owned = []
    at = 0
    for count in counts:
        owned.append(summed[at : at + count])
        at += count

    return (
        layer_output.astype(bf16).reshape(layer_input.shape),
        input_grad.astype(bf16).reshape(layer_input.shape),
        owned[0],
        owned[1],
        own_w,
        owned[6],
        own_out.astype(f32),
        owned[2],
        owned[3],
        owned[4],
        own_up.astype(f32),
        owned[7],
        own_down.astype(f32),
        owned[5],
    )


class Sizes:
    def __init__(self, heads, blocks, seqs, sub, width, hidden_width):
        self.heads = heads
        self.blocks = blocks
        self.seqs = seqs
        self.sub = sub
        self.width = width
        self.devices = heads * blocks
        self.mine = seqs * sub
        self.tokens = self.mine * heads
        self.local = H // heads
        self.parts = blocks // (seqs * self.local)
        self.run = sub // self.parts
        self.part_rows = heads * self.run
        self.half = self.part_rows // 2
        self.w_rows = width // self.devices
        self.f_rows = hidden_width // self.devices
        self.hidden_slice = hidden_width // heads
        self.w_chunk = (1 + self.local) * self.w_rows
        self.head_rows = self.blocks * self.w_rows
        self.groups = blocks // self.parts

    def fits(self):
        return (
            self.local == 2
            and self.parts == 2
            and self.run % 32 == 0
            and self.w_rows == 16
            and self.hidden_slice == self.width
            and self.mine % 16 == 0
            and self.f_rows % 16 == 0
        )

    def task(self, seq, local, part):
        return (seq * self.local + local) * self.parts + part


SMALL = 8


def my_head_of(sz, scal_ref):
    return scal_ref[0] // sz.blocks


def my_blk_of(sz, scal_ref):
    return lax.rem(scal_ref[0], sz.blocks)


def slot_head(sz, scal_ref, slot):
    return lax.rem(my_head_of(sz, scal_ref) - slot + sz.heads, sz.heads)


def halves(first, second):
    low = jnp.concatenate([first[:, :HD], second[:, :HD]], axis=1)
    high = jnp.concatenate([first[:, HD:], second[:, HD:]], axis=1)
    return low, high


def staged(count, refs):
    scratch = refs[len(refs) - count - 1 :]
    held, sems = scratch[:count], scratch[count]
    copies = [pltpu.make_async_copy(refs[i], held[i], sems.at[i]) for i in range(count)]
    for copy in copies:
        copy.start()
    for copy in copies:
        copy.wait()
    return held


def staged_call(kernel, name, scalars, arrays, outs, scratch=()):
    return pl.pallas_call(
        kernel,
        out_shape=tuple(jax.ShapeDtypeStruct(*o) for o in outs),
        in_specs=[pl.BlockSpec(memory_space=pltpu.SMEM)]
        + [pl.BlockSpec(memory_space=pltpu.HBM)] * len(arrays),
        out_specs=tuple([pl.BlockSpec(memory_space=pltpu.VMEM)] * len(outs)),
        scratch_shapes=list(scratch)
        + [pltpu.VMEM(v.shape, v.dtype) for v in arrays]
        + [pltpu.SemaphoreType.DMA((len(arrays),))],
        compiler_params=pltpu.CompilerParams(vmem_limit_bytes=63 * 2**20),
        name=name,
    )(scalars, *arrays)


def pack_kernel(sz, scal_ref, *refs):
    count = 1 + SMALL
    send_ref, small_scr = refs[count : count + 2]
    small_scr[...] = jnp.zeros_like(small_scr)
    wp_ref, *small_refs = staged(count, refs)
    for i, ref in enumerate(small_refs):
        small_scr[i : i + 1, : ref.shape[1]] = ref[...].astype(f32)
    small = small_scr[...].astype(bf16)
    for head in range(sz.heads):
        at = head * LANES
        q = wp_ref[:, at : at + LANES]
        k = wp_ref[:, sz.width + at : sz.width + at + LANES]
        v = wp_ref[:, 2 * sz.width + at : 2 * sz.width + at + LANES]
        low, high = halves(k, v)
        chunk = jnp.concatenate([q, low, high], axis=0)
        for group in range(sz.groups):
            send_ref[head * sz.groups + group, : sz.w_chunk] = chunk
            send_ref[head * sz.groups + group, sz.w_chunk :] = small


def pieces_kernel(sz, scal_ref, *refs):
    piece_refs = refs[3 : 3 + sz.heads]
    g_ref, up_ref, wo_ref = staged(3, refs)
    for step, ref in enumerate(piece_refs):
        to = lax.rem(my_head_of(sz, scal_ref) + step, sz.heads)
        at = pl.multiple_of(to * sz.hidden_slice, LANES)
        ref[: sz.mine] = g_ref[...]
        ref[sz.mine : sz.mine + sz.w_rows] = up_ref[:, pl.ds(at, sz.hidden_slice)]
        ref[sz.mine + sz.w_rows :] = wo_ref[...]


def spread(small, per, offset, count):
    lane = lax.broadcasted_iota(i32, (LANES, count), 0)
    at = lax.broadcasted_iota(i32, (LANES, count), 1) + offset
    pick = jnp.where(at % per == lane, 1.0, 0.0).astype(bf16)
    wide = dot_nn(small, pick)
    source = lax.broadcasted_iota(i32, wide.shape, 0) // SMALL
    column = (lax.broadcasted_iota(i32, wide.shape, 1) + offset) // per
    wide = jnp.where(source == column, wide, 0.0)
    return jnp.sum(wide.reshape(-1, SMALL, count), axis=0)


def collect(values, per, offset, rows, devices):
    count = values.shape[1]
    tall = jnp.broadcast_to(values[None], (devices, SMALL, count)).reshape(devices * SMALL, count)
    row = lax.broadcasted_iota(i32, tall.shape, 0)
    column = (lax.broadcasted_iota(i32, tall.shape, 1) + offset) // per
    index = row % SMALL
    keep = (row // SMALL == column) & (index >= rows[0]) & (index < rows[1])
    tall = jnp.where(keep, tall, 0.0)
    lane = lax.broadcasted_iota(i32, (count, LANES), 1)
    at = lax.broadcasted_iota(i32, (count, LANES), 0) + offset
    pick = jnp.where(at % per == lane, 1.0, 0.0).astype(bf16)
    return dot_nn(tall.astype(bf16), pick)


def source_blk(sz, scal_ref, group_slot, part_slot):
    group = lax.rem(my_blk_of(sz, scal_ref) // sz.parts - group_slot + sz.groups, sz.groups)
    part = lax.rem(my_blk_of(sz, scal_ref) % sz.parts - part_slot + sz.parts, sz.parts)
    return group * sz.parts + part


def project_kernel(sz, scal_ref, *refs):
    got_refs, refs = refs[: sz.parts], refs[sz.parts :]
    x_refs = refs[: sz.heads]
    send_ref, w_ref, vec_ref, small_scr = refs[sz.heads :]
    head = my_head_of(sz, scal_ref)
    for part_slot, ref in enumerate(got_refs):
        part = lax.rem(my_blk_of(sz, scal_ref) + sz.parts - part_slot, sz.parts)
        for src in range(sz.heads * sz.groups):
            dev = src // sz.groups * sz.blocks + src % sz.groups * sz.parts + part
            at = pl.multiple_of(dev * sz.w_rows, sz.w_rows)
            for i in range(1 + sz.local):
                piece = ref[src, i * sz.w_rows : (i + 1) * sz.w_rows]
                w_ref[pl.ds(at, sz.w_rows), i * LANES : (i + 1) * LANES] = piece
            at = pl.multiple_of(dev * SMALL, SMALL)
            small_scr[pl.ds(at, SMALL)] = ref[src, sz.w_chunk :].astype(f32)
    small = small_scr[...].astype(bf16)
    vec = spread(small, sz.w_rows, 0, sz.width)
    per = 2 * sz.w_rows
    b_q = spread(small, per, head * LANES, LANES)[6:7]
    b_v = spread(small, per, sz.width + head * LANES, LANES)[6:7]
    b_up = spread(small, 4 * sz.w_rows, head * sz.hidden_slice, sz.hidden_slice)
    row = lax.broadcasted_iota(i32, vec.shape, 0)
    vec = jnp.where(row == 7, b_up, vec)
    vec_ref[...] = vec
    zero = jnp.zeros((1, HD), f32)
    bias = jnp.concatenate([b_q, zero, b_v[:, :HD], zero, b_v[:, HD:]], axis=1)
    gain, shift = vec[0:1], vec[1:2]
    for slot in range(sz.heads):
        x = x_refs[slot][...].astype(f32)
        normed = norm_forward(x, gain, shift)[0].astype(bf16)
        qkv = (dot_nn(normed, w_ref[...]) + bias).astype(bf16)
        to = slot_head(sz, scal_ref, slot)
        half_run = sz.run // 2
        for seq in range(sz.seqs):
            for part in range(sz.parts):
                at = seq * sz.sub + part * sz.run
                low, high = halves(qkv[at : at + half_run, :LANES], qkv[at + half_run : at + sz.run, :LANES])
                packed = (low, high)
                for local in range(sz.local):
                    task = sz.task(seq, local, part)
                    q_at = pl.multiple_of(to * half_run, half_run)
                    send_ref[task, pl.ds(q_at, half_run)] = packed[local]
                    kv_at = pl.multiple_of(sz.half + to * sz.run, sz.run)
                    send_ref[task, pl.ds(kv_at, sz.run)] = qkv[
                        at : at + sz.run, (1 + local) * LANES : (2 + local) * LANES
                    ]


def assemble_kernel(sz, scal_ref, *refs):
    chunks = sz.parts * sz.groups
    mixed_refs, down_refs = refs[:chunks], refs[chunks : 2 * chunks]
    up_ref, wo_ref, down_ref = refs[2 * chunks :]
    for part_slot in range(sz.parts):
        for group_slot in range(sz.groups):
            i = part_slot * sz.groups + group_slot
            blk = source_blk(sz, scal_ref, group_slot, part_slot)
            at = pl.multiple_of(blk * sz.f_rows, sz.f_rows)
            down_ref[pl.ds(at, sz.f_rows)] = down_refs[i][...]
            for slot in range(sz.heads):
                head = slot_head(sz, scal_ref, slot)
                at = pl.multiple_of(head * sz.head_rows + blk * sz.w_rows, sz.w_rows)
                first = 2 * slot * sz.w_rows
                up_ref[pl.ds(at, sz.w_rows)] = mixed_refs[i][first : first + sz.w_rows]
                at = pl.multiple_of(slot * sz.head_rows + blk * sz.w_rows, sz.w_rows)
                first += sz.w_rows
                wo_ref[pl.ds(at, sz.w_rows)] = mixed_refs[i][first : first + sz.w_rows]


def feed_kernel(sz, scal_ref, vec_ref, up_ref, wo_ref, down_ref, *refs):
    n = sz.heads
    x_refs, g_refs, m_refs = refs[:n], refs[n : 2 * n], refs[2 * n : 3 * n]
    outs = refs[3 * n :]
    part_refs, feed_refs = outs[:n], outs[n : 2 * n]
    mid_ref, act_ref, dh_ref, n_ref, mix_own_ref, sum_ref, mix_scr = outs[2 * n :]
    half_run = sz.run // 2
    for slot in range(n):
        for seq in range(sz.seqs):
            for part in range(sz.parts):
                first = m_refs[slot][sz.task(seq, 0, part)]
                second = m_refs[slot][sz.task(seq, 1, part)]
                low, high = halves(first, second)
                for head in range(n):
                    at = seq * sz.sub + part * sz.run
                    cols = slice(slot * LANES, (slot + 1) * LANES)
                    rows = slice(head * half_run, (head + 1) * half_run)
                    mix_scr[head, at : at + half_run, cols] = low[rows]
                    mix_scr[head, at + half_run : at + sz.run, cols] = high[rows]
    w_down = down_ref[...]
    b_out, gain, shift, b_up = vec_ref[2:3], vec_ref[3:4], vec_ref[4:5], vec_ref[7:8]
    sums = jnp.zeros((3, sz.width), f32)
    group = 2
    for first in range(0, n, group):
        slots = range(first, first + group)
        x = jnp.concatenate([x_refs[s][...] for s in slots], axis=0).astype(f32)
        g = jnp.concatenate([g_refs[s][: sz.mine] for s in slots], axis=0)
        mixed = jnp.concatenate([mix_scr[slot_head(sz, scal_ref, s)] for s in slots], axis=0)
        middle = x + dot_nn(mixed, wo_ref[...]) + b_out
        normed, unit, _ = norm_forward(middle, gain, shift)
        normed = normed.astype(bf16)
        hidden = dot_nn(normed, up_ref[...]) + b_up
        sigma = 1.0 / (1.0 + jnp.exp(-1.702 * hidden))
        activated = (hidden * sigma).astype(bf16)
        slope = sigma + 1.702 * hidden * sigma * (1.0 - sigma)
        grad_hidden = (dot_nt(g, w_down) * slope).astype(bf16)
        grad_two = dot_nt(grad_hidden, up_ref[...])
        feed = dot_nn(activated, w_down)
        sums = sums + jnp.concatenate(
            [
                jnp.sum(grad_two * unit, axis=0, keepdims=True),
                jnp.sum(grad_two, axis=0, keepdims=True),
                jnp.sum(grad_hidden.astype(f32), axis=0, keepdims=True),
            ],
            axis=0,
        )
        for i, s in enumerate(slots):
            rows = slice(i * sz.mine, (i + 1) * sz.mine)
            part_refs[s][...] = grad_two[rows].astype(part_refs[s].dtype)
            feed_refs[s][...] = feed[rows].astype(feed_refs[s].dtype)
            if s == 0:
                mid_ref[...] = middle[rows]
                mix_own_ref[...] = mixed[rows]
            act_ref[s] = activated[rows]
            dh_ref[s] = grad_hidden[rows]
            n_ref[s] = normed[rows]
    sum_ref[...] = jnp.concatenate([sums, jnp.zeros((5, sz.width), f32)], axis=0)


def give_and_keep(sz, scal_ref, values, rows, keep_ref, give_ref):
    part = my_blk_of(sz, scal_ref) % sz.parts
    for blk in range(sz.blocks):
        group = blk // sz.parts
        piece = values(blk)
        @pl.when(part == blk % sz.parts)
        def _():
            keep_ref[group] = piece

        @pl.when(part != blk % sz.parts)
        def _():
            give_ref[group] = piece.astype(bf16)


def feed_grad_kernel(sz, scal_ref, act_ref, dh_ref, n_ref, *refs):
    g_refs = refs[: sz.heads]
    keep_ref, give_ref = refs[sz.heads :]
    g = jnp.concatenate([ref[: sz.mine] for ref in g_refs], axis=0)
    act = act_ref[...].reshape(sz.tokens, sz.hidden_slice)
    down = dot_tn(act, g)
    up = dot_tn(n_ref[...].reshape(sz.tokens, sz.width), dh_ref[...].reshape(sz.tokens, sz.hidden_slice))

    def piece(blk):
        pieces = [down[blk * sz.f_rows : (blk + 1) * sz.f_rows]]
        for head in range(sz.heads):
            at = head * sz.head_rows + blk * sz.w_rows
            pieces.append(up[at : at + sz.w_rows])
        return jnp.concatenate(pieces, axis=0)

    give_and_keep(sz, scal_ref, piece, sz.f_rows + sz.heads * sz.w_rows, keep_ref, give_ref)


def part_sum_kernel(sz, scal_ref, *refs):
    keep_ref, got_ref, keep_out_ref, got_out_ref, *refs = refs
    down_refs, rest_refs = refs[: sz.groups], refs[sz.groups :]
    rows = keep_ref.shape[1] - sz.f_rows
    for step in range(sz.groups):
        to = lax.rem(my_blk_of(sz, scal_ref) // sz.parts + step, sz.groups)
        total = keep_ref[to] + got_ref[to].astype(f32)
        total_out = keep_out_ref[to] + got_out_ref[to].astype(f32)
        dtype = rest_refs[step].dtype
        down_refs[step][...] = total[: sz.f_rows].astype(dtype)
        rest_refs[step][:rows] = total[sz.f_rows :].astype(dtype)
        rest_refs[step][rows:] = total_out.astype(dtype)


def middle_grad_kernel(sz, scal_ref, vec_ref, wo_ref, mid_ref, g_ref, mix_ref, *refs):
    n = sz.heads
    part_refs = refs[:n]
    grad_ref, branch_ref, send_ref, sum_ref, keep_ref, give_ref = refs[n:]
    upstream = part_refs[0][...]
    for ref in part_refs[1:]:
        upstream = upstream + ref[...].astype(f32)
    gain, shift = vec_ref[3:4], vec_ref[4:5]
    _, unit, root = norm_forward(mid_ref[...], gain, shift)
    g = g_ref[...].astype(f32)
    grad = g + norm_input_grad(upstream, unit, root, gain)
    grad_ref[...] = grad
    branch = grad.astype(bf16)
    branch_ref[...] = branch
    sum_ref[...] = jnp.concatenate(
        [
            jnp.sum(branch.astype(f32), axis=0, keepdims=True),
            jnp.sum(g, axis=0, keepdims=True),
            jnp.zeros((6, sz.width), f32),
        ],
        axis=0,
    )
    mixed = dot_nt(branch, wo_ref[...]).astype(bf16)
    half_run = sz.run // 2
    for slot in range(n):
        to = slot_head(sz, scal_ref, slot)
        for seq in range(sz.seqs):
            for part in range(sz.parts):
                at = seq * sz.sub + part * sz.run
                cols = slice(slot * LANES, (slot + 1) * LANES)
                packed = halves(mixed[at : at + half_run, cols], mixed[at + half_run : at + sz.run, cols])
                for local in range(sz.local):
                    send_ref[to * sz.blocks + sz.task(seq, local, part)] = packed[local]
    out_grad(sz, scal_ref, mix_ref[...], branch, keep_ref, give_ref)


def out_grad(sz, scal_ref, mixed, branch, keep_ref, give_ref):
    grad = dot_tn(mixed, branch)
    part = my_blk_of(sz, scal_ref) % sz.parts
    for slot in range(sz.heads):
        head = slot_head(sz, scal_ref, slot)
        to = pl.multiple_of(head * sz.w_rows, sz.w_rows)
        for blk in range(sz.blocks):
            at = slot * sz.head_rows + blk * sz.w_rows
            piece = grad[at : at + sz.w_rows]

            @pl.when(part == blk % sz.parts)
            def _():
                keep_ref[blk // sz.parts, pl.ds(to, sz.w_rows)] = piece

            @pl.when(part != blk % sz.parts)
            def _():
                give_ref[blk // sz.parts, pl.ds(to, sz.w_rows)] = piece.astype(bf16)


def norm_again_kernel(sz, scal_ref, vec_ref, *refs):
    x_refs = refs[: sz.heads]
    n_ref, u_ref = refs[sz.heads :]
    gain, shift = vec_ref[0:1], vec_ref[1:2]
    for slot in range(sz.heads):
        normed, unit, _ = norm_forward(x_refs[slot][...].astype(f32), gain, shift)
        at = slice(slot * sz.mine, (slot + 1) * sz.mine)
        n_ref[:, at] = normed.astype(bf16).T
        u_ref[:, at] = unit.astype(bf16).T


def both_levels(values, *where):
    high = values.astype(bf16).astype(f32)
    return collect(high, *where) + collect(values - high, *where)


def project_grad_kernel(sz, scal_ref, early_ref, *refs):
    far_refs, (keep_ref, give_ref), refs = refs[:4], refs[4:6], refs[6:]
    part_refs, refs = refs[: sz.heads], refs[sz.heads :]
    got_ref, n_ref, u_ref, w_ref, d_ref, send_scr, own_scr, part_scr, sems = refs
    copies = [
        pltpu.make_async_copy(far_refs[i], ref, sems.at[i])
        for i, ref in enumerate((got_ref, n_ref, u_ref, w_ref))
    ]
    n_w = sz.w_chunk
    mine = lax.rem(my_blk_of(sz, scal_ref), sz.parts)
    copies += [
        pltpu.make_async_copy(send_scr.at[:, sz.parts - 1 - mine], give_ref, sems.at[4]),
        pltpu.make_async_copy(send_scr.at[:, mine], keep_ref, sems.at[5]),
        pltpu.make_async_copy(own_scr, part_refs[0], sems.at[6]),
    ]
    copies += [
        pltpu.make_async_copy(part_scr.at[s - 1], part_refs[s], sems.at[6 + s])
        for s in range(1, sz.heads)
    ]
    for copy in copies[:4]:
        copy.start()
    head = my_head_of(sz, scal_ref)
    half_run = sz.run // 2
    copies[0].wait()
    for slot in range(sz.heads):
        to = slot_head(sz, scal_ref, slot)
        q_at = pl.multiple_of(to * half_run, half_run)
        kv_at = pl.multiple_of(sz.half + to * sz.run, sz.run)
        for seq in range(sz.seqs):
            for part in range(sz.parts):
                at = slot * sz.mine + seq * sz.sub + part * sz.run
                first = got_ref[sz.task(seq, 0, part), pl.ds(q_at, half_run)]
                second = got_ref[sz.task(seq, 1, part), pl.ds(q_at, half_run)]
                low, high = halves(first, second)
                d_ref[at : at + half_run, :LANES] = low
                d_ref[at + half_run : at + sz.run, :LANES] = high
                for local in range(sz.local):
                    d_ref[at : at + sz.run, (1 + local) * LANES : (2 + local) * LANES] = got_ref[
                        sz.task(seq, local, part), pl.ds(kv_at, sz.run)
                    ]
    d_proj = d_ref[...]
    copies[1].wait()
    grad_w = dot_nn(n_ref[...], d_proj).astype(bf16)
    for dev in range(sz.devices):
        rows = slice(dev * sz.w_rows, (dev + 1) * sz.w_rows)
        for i in range(1 + sz.local):
            cols = slice(i * LANES, (i + 1) * LANES)
            to = (dev // sz.parts, dev % sz.parts)
            send_scr[*to, i * sz.w_rows : (i + 1) * sz.w_rows] = grad_w[rows, cols]
    copies[2].wait()
    copies[3].wait()
    weights = w_ref[...].astype(f32)
    ones = jnp.ones((16, sz.tokens), bf16)
    column = dot_nn(ones, d_proj)[:SMALL]
    terms = [dot_nn(u_ref[...], d_proj) * weights, column[0:1] * weights]
    ones = jnp.ones((16, (1 + sz.local) * LANES), bf16)
    sums = []
    for term in terms:
        high = term.astype(bf16)
        low = (term - high.astype(f32)).astype(bf16)
        sums.append((dot_nt(ones, high) + dot_nt(ones, low))[0:1])
    wide = jnp.concatenate([*sums, jnp.zeros((SMALL - 2, sz.width), f32)], axis=0)
    sum_q = column[:, :LANES]
    sum_v = jnp.concatenate([column[:, LANES + HD : 2 * LANES], column[:, 2 * LANES + HD :]], axis=1)
    per = sz.w_rows
    small = (
        early_ref[...]
        + both_levels(wide, per, 0, (0, 2), sz.devices)
        + both_levels(sum_q, 2 * per, head * LANES, (6, 7), sz.devices)
        + both_levels(sum_v, 2 * per, sz.width + head * LANES, (6, 7), sz.devices)
    )
    small = two_levels(small.reshape(-1, sz.parts, SMALL, LANES))
    send_scr[:, :, n_w:, :] = small
    copies[4].start()
    copies[5].start()
    grad_one = dot_nt(d_proj, w_ref[...])
    own_scr[...] = grad_one[: sz.mine]
    part_scr[...] = grad_one[sz.mine :].astype(bf16).reshape(part_scr.shape)
    for copy in copies[6:]:
        copy.start()
    for copy in copies[4:]:
        copy.wait()


def two_levels(small):
    high = small.astype(bf16).astype(f32)
    return jnp.concatenate([high, small - high], axis=-2).astype(bf16)


def fold_kernel(sz, scal_ref, keep_ref, got_ref, send_ref):
    n_w = sz.w_chunk
    total = keep_ref[...].astype(f32) + got_ref[...].astype(f32)
    send_ref[:, :n_w] = total[:, :n_w].astype(bf16)
    send_ref[:, n_w:] = two_levels(total[:, n_w : n_w + SMALL] + total[:, n_w + SMALL :])


def input_grad_kernel(sz, scal_ref, vec_ref, grad_ref, x_ref, *refs):
    out_ref = refs[sz.heads]
    upstream = refs[0][...]
    for ref in refs[1 : sz.heads]:
        upstream = upstream + ref[...].astype(f32)
    gain, shift = vec_ref[0:1], vec_ref[1:2]
    _, unit, root = norm_forward(x_ref[...].astype(f32), gain, shift)
    out_ref[...] = (grad_ref[...] + norm_input_grad(upstream, unit, root, gain)).astype(bf16)


def split_kernel(sz, scal_ref, sum_a_ref, sum_b_ref, own_ref, *refs):
    n = sz.heads
    early_ref, refs = refs[-1], refs[:-1]
    wide = jnp.concatenate(
        [sum_a_ref[0:2], sum_b_ref[0:1], sum_a_ref[0:2], sum_b_ref[1:2], sum_a_ref[2:3]]
        + [jnp.zeros((1, sz.width), f32)],
        axis=0,
    )
    up_bias = jnp.broadcast_to(sum_a_ref[2:3], (SMALL, sz.width))
    at = my_head_of(sz, scal_ref) * sz.hidden_slice
    early_ref[...] = both_levels(wide, sz.w_rows, 0, (2, 6), sz.devices) + both_levels(
        up_bias, 4 * sz.w_rows, at, (7, 8), sz.devices
    )
    got_refs, feed_refs, refs = refs[: sz.groups - 1], refs[sz.groups - 1 :][: n - 1], refs[-n:]
    piece_ref, *send_refs = refs

    def total(rows):
        value = own_ref[rows]
        for ref in got_refs:
            value = value + ref[rows].astype(f32)
        return value

    for slot in range(n):
        to = slot_head(sz, scal_ref, slot)
        at = pl.multiple_of(to * sz.w_rows, sz.w_rows)
        up = total(pl.ds(at, sz.w_rows)).astype(bf16)
        out = total(pl.ds(at + n * sz.w_rows, sz.w_rows))
        ref = send_refs[slot - 1] if slot else piece_ref
        base = sz.mine if slot else 0
        if slot:
            ref[: sz.mine] = feed_refs[slot - 1][...]
        ref[base : base + sz.w_rows] = up
        ref[base + sz.w_rows :] = out.astype(bf16)


def final_kernel(sz, scal_ref, got_ref, *refs):
    piece_refs, refs = refs[: sz.heads], refs[sz.heads :]
    w_ref, up_ref, out_ref, *small_refs = refs
    out = piece_refs[0][sz.w_rows :].astype(f32)
    for ref in piece_refs[1:]:
        out = out + ref[sz.mine + sz.w_rows :].astype(f32)
    out_ref[...] = out
    for slot in range(sz.heads):
        at = pl.multiple_of(slot_head(sz, scal_ref, slot) * sz.hidden_slice, LANES)
        base = sz.mine if slot else 0
        piece = piece_refs[(sz.heads - slot) % sz.heads][base : base + sz.w_rows]
        up_ref[:, pl.ds(at, sz.hidden_slice)] = piece.astype(f32)
    for head in range(sz.heads):
        total = jnp.zeros((sz.w_chunk, LANES), f32)
        for group in range(sz.groups):
            total = total + got_ref[head * sz.groups + group, : sz.w_chunk].astype(f32)
        at = head * LANES
        w_ref[:, at : at + LANES] = total[: sz.w_rows]
        low, high = halves(total[sz.w_rows : 2 * sz.w_rows], total[2 * sz.w_rows :])
        w_ref[:, sz.width + at : sz.width + at + LANES] = low
        w_ref[:, 2 * sz.width + at : 2 * sz.width + at + LANES] = high
    small = jnp.sum(got_ref[:, sz.w_chunk :, :].astype(f32), axis=0)
    small = small[:SMALL] + small[SMALL:]
    for i, ref in enumerate(small_refs):
        ref[...] = small[i : i + 1, : ref.shape[1]]


BLK = ("group", "part")
ALL = ("head", "group", "part")


def on_device_fused(
    sz,
    layer_input,
    segments,
    token_valid,
    attention_gain,
    attention_shift,
    project_weight,
    project_bias,
    output_weight,
    output_bias,
    feed_gain,
    feed_shift,
    up_weight,
    up_bias,
    down_weight,
    down_bias,
    cotangent,
):
    n = sz.heads
    my_head = lax.axis_index("head")
    my_blk = lax.axis_index(BLK)
    scal = (my_head * sz.blocks + my_blk).astype(i32).reshape(1)
    geo = AttentionShape(sz.blocks, sz.part_rows, sz.parts, sz.run, sz.sub)
    token_shape = (sz.mine, sz.width)

    def call(kernel, name, arrays, outs, scratch=(), limit=VMEM_LIMIT):
        kernel = functools.partial(kernel, sz)
        return local_call(kernel, name, scal, arrays, outs, scratch, limit)

    def around(x, step):
        return lax.ppermute(x, "head", [(i, (i + step) % n) for i in range(n)])

    def after(values, *earlier):
        return lax.optimization_barrier((values, *earlier))[0]

    def around_groups(x, step):
        pairs = [
            (g * sz.parts + p, (g + step) % sz.groups * sz.parts + p)
            for g in range(sz.groups)
            for p in range(sz.parts)
        ]
        return lax.ppermute(x, BLK, pairs)

    def around_parts(x, step):
        return lax.ppermute(x, BLK, within_group(sz.blocks, sz.parts, step))

    x_mine = layer_input.reshape(token_shape)
    g_mine = cotangent.reshape(token_shape)
    small = [attention_gain, attention_shift, output_bias, feed_gain, feed_shift, down_bias]
    small += [project_bias, up_bias]
    (send,) = staged_call(
        functools.partial(pack_kernel, sz),
        "pack",
        scal,
        [project_weight, *[v.reshape(1, -1) for v in small]],
        [((n * sz.groups, sz.w_chunk + SMALL, LANES), bf16)],
        [pltpu.VMEM((SMALL, LANES), f32)],
    )
    got = exchange(send, ("head", "group"))
    x_slots = [x_mine] + [around(after(x_mine, send), d) for d in range(1, n)]
    pieces = staged_call(
        functools.partial(pieces_kernel, sz),
        "pieces",
        after(scal, send),
        [g_mine, up_weight, output_weight],
        [((sz.mine + 2 * sz.w_rows, sz.width), bf16)] * n,
    )
    g_slots = [pieces[0]] + [around(after(pieces[d], x_slots[1]), d) for d in range(1, n)]
    got_parts = [got] + [around_parts(got, d) for d in range(1, sz.parts)]

    my_part = my_blk % sz.parts
    my_seq = (my_blk // sz.parts) // sz.local
    scalars, bounds = attention_bounds(
        segments, token_valid, my_seq, my_part, geo, sz.heads, sz.sub
    )
    got_parts[0] = after(got_parts[0], scalars, bounds)
    send, w_slice, vec = call(
        project_kernel,
        "project",
        [*got_parts, *x_slots],
        [
            ((sz.blocks, sz.half + sz.part_rows, LANES), bf16),
            far((sz.width, (1 + sz.local) * LANES), bf16),
            far((SMALL, sz.width), f32),
        ],
        [pltpu.VMEM((sz.devices * SMALL, LANES), f32)],
    )
    column = jnp.concatenate([v[sz.mine :] for v in g_slots], axis=0)
    columns = [column] + [around_groups(column, d) for d in range(1, sz.groups)]
    downs = [after(down_weight, x_slots[1])]
    downs += [around_groups(downs[0], d) for d in range(1, sz.groups)]
    task = exchange(send, BLK)
    task = after(task, column, *downs)
    others = [around_parts(task, step) for step in range(1, sz.parts)]
    o_task, ot, lse = attention_forward(geo, scalars, [task, *others], bounds)
    columns += [around_parts(after(v, o_task), d) for d in range(1, sz.parts) for v in columns]
    downs += [around_parts(after(v, o_task), d) for d in range(1, sz.parts) for v in downs]
    square = ((sz.width, sz.width), bf16)
    w_up, w_out, w_down = call(assemble_kernel, "assemble", [*columns, *downs], [square] * 3)
    mixed = exchange(o_task, BLK)
    turned = far((sz.width, sz.tokens), bf16)
    n_one, u_one = call(
        norm_again_kernel, "norm_again", [after(vec, o_task), *x_slots], [turned, turned]
    )
    mixed = after(mixed, n_one, *columns)
    m_slots = [mixed] + [around(mixed, d) for d in range(1, n)]

    outs = call(
        feed_kernel,
        "feed",
        [vec, w_up, w_out, w_down, *x_slots, *g_slots, *m_slots],
        [far(token_shape, f32)]
        + [(token_shape, bf16)] * (n - 1)
        + [far(token_shape, f32)]
        + [far(token_shape, bf16)] * (n - 1)
        + [far(token_shape, f32)]
        + [((n, sz.mine, sz.hidden_slice), bf16)] * 2
        + [((n, *token_shape), bf16), far(token_shape, bf16), far((SMALL, sz.width), f32)],
        [
            pltpu.VMEM((n, *token_shape), bf16),
        ],
    )
    grad_two, feed = outs[:n], outs[n : 2 * n]
    middle, activated, grad_hidden, n_two, mixed_own, feed_sums = outs[2 * n :]
    grad_two = [grad_two[0]] + [around(grad_two[d], -d) for d in range(1, n)]

    def shared(rows):
        shape = (sz.groups, rows, sz.width)
        return [far(shape, f32), far(shape, bf16)]

    keep, give = call(
        feed_grad_kernel,
        "feed_grad",
        [activated, grad_hidden, n_two, *g_slots],
        shared(sz.f_rows + n * sz.w_rows),
    )

    grad_middle, branch, send, branch_sums, keep_out, give_out = call(
        middle_grad_kernel,
        "middle_grad",
        [vec, w_out, middle, g_mine, mixed_own, *grad_two],
        [
            far(token_shape, f32),
            far(token_shape, bf16),
            ((sz.devices, sz.run // 2, LANES), bf16),
            far((SMALL, sz.width), f32),
            *shared(n * sz.w_rows),
        ],
    )
    do_task = exchange(send, ALL)
    given = around_parts(give, 1)
    down_shape, rest_shape = (sz.f_rows, sz.width), (2 * n * sz.w_rows, sz.width)
    sums = call(
        part_sum_kernel,
        "part_sum",
        [keep, given, keep_out, around_parts(give_out, 1)],
        [far(down_shape, f32)]
        + [far(down_shape, bf16)] * (sz.groups - 1)
        + [far(rest_shape, f32)]
        + [(rest_shape, bf16)] * (sz.groups - 1),
    )
    down_sum, w_sum = sums[: sz.groups], sums[sz.groups :]
    w_pieces = [around_groups(w_sum[d], d) for d in range(1, sz.groups)]
    dq, dkv, *dkv_others = attention_backward(
        geo, do_tile_grouped, scalars, [task, *others], do_task, bounds, ot, lse
    )
    dkv_others[0] = after(dkv_others[0], *w_pieces)
    for step in range(1, sz.parts):
        back = within_group(sz.blocks, sz.parts, -step)
        dkv = dkv + lax.ppermute(dkv_others[step - 1], BLK, back).astype(f32)
    send = jnp.concatenate([dq, dkv.astype(bf16)], axis=1)
    got = exchange(send, BLK)
    piece, *rest = call(
        split_kernel,
        "split",
        [feed_sums, branch_sums, after(w_sum[0], send), *w_pieces, *feed[1:]],
        [far((2 * sz.w_rows, sz.width), bf16)]
        + [far((sz.mine + 2 * sz.w_rows, sz.width), bf16)] * (n - 1)
        + [far((sz.devices * SMALL, LANES), f32)],
    )
    early = rest.pop()
    rest = [around(v, -d - 1) for d, v in enumerate(rest)]
    got = after(got, rest[0], rest[2])
    wide = (1 + sz.local) * LANES
    send_shape = (n * sz.groups, sz.w_chunk + 2 * SMALL, LANES)
    keep, give, *outs = pl.pallas_call(
        functools.partial(project_grad_kernel, sz),
        out_shape=(
            pltpu.HBM(send_shape, bf16),
            pltpu.HBM(send_shape, bf16),
            pltpu.HBM(token_shape, f32),
            *[pltpu.HBM(token_shape, bf16)] * (n - 1),
        ),
        in_specs=[pl.BlockSpec(memory_space=pltpu.SMEM), pl.BlockSpec(memory_space=pltpu.VMEM)]
        + [pl.BlockSpec(memory_space=pltpu.HBM)] * 4,
        out_specs=tuple([pl.BlockSpec(memory_space=pltpu.HBM)] * (2 + n)),
        scratch_shapes=[
            pltpu.VMEM(got.shape, bf16),
            pltpu.VMEM((sz.width, sz.tokens), bf16),
            pltpu.VMEM((sz.width, sz.tokens), bf16),
            pltpu.VMEM((sz.width, wide), bf16),
            pltpu.VMEM((sz.tokens, wide), bf16),
            pltpu.VMEM((send_shape[0], sz.parts, *send_shape[1:]), bf16),
            pltpu.VMEM(token_shape, f32),
            pltpu.VMEM((n - 1, *token_shape), bf16),
            pltpu.SemaphoreType.DMA((6 + n,)),
        ],
        compiler_params=pltpu.CompilerParams(vmem_limit_bytes=63 * 2**20),
        cost_estimate=pl.CostEstimate(
            flops=COST["project_grad"], bytes_accessed=10**6, transcendentals=0
        ),
        name="project_grad",
    )(scal, early, got, n_one, u_one, w_slice)
    (send,) = call(fold_kernel, "fold", [keep, around_parts(give, 1)], [(send_shape, bf16)])
    got = exchange(send, ("head", "group"))
    grad_one = [outs[0]] + [around(outs[d], -d) for d in range(1, n)]
    down_grad = down_sum[0]
    for d in range(1, sz.groups):
        down_grad = down_grad + around_groups(after(down_sum[d], outs[1]), d).astype(f32)
    (input_grad,) = call(
        input_grad_kernel,
        "input_grad",
        [vec, grad_middle, x_mine, *grad_one],
        [(token_shape, bf16)],
    )
    layer_output = middle + feed[0] + vec[5:6]
    for v in rest:
        layer_output = layer_output + v[: sz.mine].astype(f32)
    layer_output = layer_output.astype(bf16)
    w_grad, up_grad, out_grad, *owned = call(
        final_kernel,
        "final",
        [got, piece, *rest],
        [
            ((sz.w_rows, 3 * sz.width), f32),
            ((sz.w_rows, n * sz.hidden_slice), f32),
            ((sz.w_rows, sz.width), f32),
        ]
        + [((1, v.shape[0]), f32) for v in small],
    )
    owned = [v.reshape(-1) for v in owned]
    return (
        layer_output.reshape(layer_input.shape),
        input_grad.reshape(layer_input.shape),
        owned[0],
        owned[1],
        w_grad,
        owned[6],
        out_grad,
        owned[2],
        owned[3],
        owned[4],
        up_grad,
        owned[7],
        down_grad,
        owned[5],
    )


def solution(mesh):
    heads, blocks = mesh.shape["head"], mesh.shape["blk"]

    def layer(*arguments):
        layer_input, up_weight = arguments[0], arguments[11]
        seqs, _, tokens, width = layer_input.shape
        sz = Sizes(heads, blocks, seqs, tokens // heads, width, up_weight.shape[1])
        if sz.fits():
            split = (heads, blocks // sz.parts, sz.parts)
            inner = jax.sharding.Mesh(mesh.devices.reshape(split), ALL)
            body, blk, everywhere = functools.partial(on_device_fused, sz), BLK, ALL
        else:
            inner, body, blk, everywhere = mesh, on_device_general, "blk", BOTH
        rows = P(None, blk, "head", None)
        vector, matrix = P(everywhere), P(everywhere, None)
        weights = (vector, vector, matrix, vector, matrix, vector)
        weights += (vector, vector, matrix, vector, matrix, vector)
        return jax.shard_map(
            body,
            mesh=inner,
            in_specs=(rows, P(), P(), *weights, rows),
            out_specs=(rows, rows, *weights),
            check_vma=False,
        )(*arguments)

    return layer
```

```python
import functools

import jax
import jax.numpy as jnp
from jax import lax
from jax.experimental import pallas as pl
from jax.experimental.pallas import tpu as pltpu
from jax.sharding import PartitionSpec as P

H = 8
HD = 64
LANES = 128
EPSILON = 1e-05
NEG_FILL = -1e30
TILE_Q = 256

bf16 = jnp.bfloat16
f32 = jnp.float32
i32 = jnp.int32
BOTH = ("head", "blk")


def dot_nn(a, b):
    return lax.dot_general(a, b, (((1,), (0,)), ((), ())), preferred_element_type=f32)


def dot_nt(a, b):
    return lax.dot_general(a, b, (((1,), (1,)), ((), ())), preferred_element_type=f32)


def dot_tn(a, b):
    return lax.dot_general(a, b, (((0,), (0,)), ((), ())), preferred_element_type=f32)


def norm_forward(values, gain, shift):
    centred = values - jnp.mean(values, axis=-1, keepdims=True)
    variance = jnp.mean(centred * centred, axis=-1, keepdims=True)
    inverse_root = lax.rsqrt(variance + EPSILON)
    unit_value = centred * inverse_root
    return (unit_value * gain + shift, unit_value, inverse_root)


def norm_input_grad(upstream, unit_value, inverse_root, gain):
    scaled = upstream * gain
    inner = scaled - jnp.mean(scaled, axis=-1, keepdims=True)
    inner = inner - unit_value * jnp.mean(scaled * unit_value, axis=-1, keepdims=True)
    return inverse_root * inner


class AttentionShape:
    def __init__(self, blocks, part_rows, parts, run, stride):
        self.blocks = blocks
        self.per_tile = max(1, TILE_Q // part_rows)
        self.tiles = blocks // self.per_tile
        self.tile = self.per_tile * part_rows
        self.part_rows = part_rows
        self.half = part_rows // 2
        self.parts = parts
        self.run = run
        self.stride = stride
        self.span = self.tile * parts


def unpack_rows(packed):
    return jnp.concatenate([packed[:, :HD], packed[:, HD:]], axis=0)


def pack_rows(rows):
    half = rows.shape[0] // 2
    return jnp.concatenate([rows[:half], rows[half:]], axis=1)


def key_base(geo):
    rows = lax.broadcasted_iota(i32, (geo.tile, 1), 0)
    return (rows // geo.run) * geo.stride + rows % geo.run


def task_tile(ref, geo, tile, first, count):
    block = ref[pl.ds(tile * geo.per_tile, geo.per_tile), first : first + count, :]
    return block.reshape(geo.per_tile * count, LANES)


ONES = 16
CHUNKS_AT_ONCE = 4


def forward_kernel(geo, scal_ref, *refs):
    part_refs = refs[: geo.parts]
    bounds_ref, out_ref, ot_ref, lse_ref, vt_ref = refs[geo.parts :]
    base = jnp.broadcast_to(key_base(geo), (geo.tile, geo.tile))
    ones = jnp.ones((ONES, geo.tile), bf16)
    for part in range(geo.parts):
        for tile in range(geo.tiles):
            keys = task_tile(part_refs[part], geo, tile, geo.half, geo.part_rows)
            vt_ref[part, tile, :ONES] = ones
            vt_ref[part, tile, ONES:] = keys.T[HD:]
    for tile in range(geo.tiles):
        q = unpack_rows(task_tile(part_refs[0], geo, tile, 0, geo.half))
        q = q * jnp.asarray(HD**-0.5, bf16)
        qz = jnp.concatenate([q, jnp.zeros_like(q)], axis=1)
        start = bounds_ref[tile, 0:1]
        last = bounds_ref[tile, 1:2]
        own = bounds_ref[tile, 2:3]

        def step(key_tiles, carry):
            chunks = [(key_tile, part) for key_tile in key_tiles for part in range(geo.parts)]
            for at in range(0, len(chunks), CHUNKS_AT_ONCE):
                carry = some(chunks[at : at + CHUNKS_AT_ONCE], carry)
            return carry

        def some(chunks, carry):
            run_max, acc = carry
            masked = []
            new_max = run_max
            for key_tile, part in chunks:
                offset = key_tile * geo.span + scal_ref[part]
                keys = task_tile(part_refs[part], geo, key_tile, geo.half, geo.part_rows)
                scores = dot_nt(keys, qz)
                allowed = (base >= start - offset) & (base <= last - offset)
                if key_tile == tile and part == 0:
                    allowed = allowed | (base == own - offset)
                masked.append(jnp.where(allowed, scores, NEG_FILL))
                new_max = jnp.maximum(new_max, jnp.max(masked[-1], axis=0, keepdims=True))
            acc = acc * jnp.exp(run_max - new_max)
            for (key_tile, part), scores in zip(chunks, masked):
                probs = jnp.exp(scores - new_max).astype(bf16)
                acc = acc + dot_nn(vt_ref[part, key_tile], probs)
            return (new_max, acc)

        carry = (
            jnp.full((1, geo.tile), NEG_FILL, f32),
            jnp.zeros((ONES + HD, geo.tile), f32),
        )
        near = max(0, tile - 1)
        carry = step(range(tile, near - 1, -1), carry)
        if near:
            carry = lax.cond(
                scal_ref[geo.parts + tile] < near,
                functools.partial(step, range(near)),
                lambda same: same,
                carry,
            )
        run_max, acc = carry
        run_sum = acc[0:1]
        attended = acc[ONES:] / run_sum
        ot_ref[tile] = attended
        lse_ref[tile] = jnp.broadcast_to(run_max + jnp.log(run_sum), (8, geo.tile))
        packed = pack_rows(attended.T).astype(bf16)
        for i in range(geo.per_tile):
            out_ref[tile * geo.per_tile + i] = packed[i * geo.half : (i + 1) * geo.half]


def backward_kernel(geo, do_tile, scal_ref, *refs):
    part_refs = refs[: geo.parts]
    do_ref, bounds_ref, ot_ref, lse_ref, dq_ref = refs[geo.parts : geo.parts + 5]
    grad_refs = refs[geo.parts + 5 : 2 * geo.parts + 5]
    acc_ref, kvt_ref = refs[2 * geo.parts + 5 :]
    base = jnp.broadcast_to(key_base(geo), (geo.tile, geo.tile))
    acc_ref[...] = jnp.zeros_like(acc_ref)
    for part in range(geo.parts):
        for tile in range(geo.tiles):
            keys = task_tile(part_refs[part], geo, tile, geo.half, geo.part_rows)
            kvt_ref[part, tile] = keys.T
    for tile in range(geo.tiles):
        q = unpack_rows(task_tile(part_refs[0], geo, tile, 0, geo.half))
        q = q * jnp.asarray(HD**-0.5, bf16)
        do = unpack_rows(do_tile(do_ref, geo, tile))
        zeros = jnp.zeros_like(q)
        qz = jnp.concatenate([q, zeros], axis=1)
        doz = jnp.concatenate([zeros, do], axis=1)
        q_do = jnp.concatenate([qz, doz], axis=0)
        delta = jnp.sum(do.astype(f32).T * ot_ref[tile], axis=0, keepdims=True)
        log_total = lse_ref[tile, 0:1]
        start = bounds_ref[tile, 0:1]
        last = bounds_ref[tile, 1:2]
        own = bounds_ref[tile, 2:3]

        def chunk(part, key_tile, acc):
            offset = key_tile * geo.span + scal_ref[part]
            keys = task_tile(part_refs[part], geo, key_tile, geo.half, geo.part_rows)
            scores = dot_nt(keys, qz)
            allowed = (base >= start - offset) & (base <= last - offset)
            if key_tile == tile and part == 0:
                allowed = allowed | (base == own - offset)
            probs = jnp.exp(jnp.where(allowed, scores, NEG_FILL) - log_total)
            grad_probs = dot_nt(keys, doz)
            grad_scores = (probs * (grad_probs - delta)).astype(bf16)
            both = jnp.concatenate([grad_scores, probs.astype(bf16)], axis=1)
            acc_ref[part, key_tile] += dot_nn(both, q_do)
            return acc + dot_nn(kvt_ref[part, key_tile], grad_scores)

        def step(key_tiles, acc):
            for key_tile in key_tiles:
                for part in range(geo.parts):
                    acc = chunk(part, key_tile, acc)
            return acc

        near = max(0, tile - 1) if geo.parts > 2 else 0
        acc = step(range(tile, near - 1, -1), jnp.zeros((2 * HD, geo.tile), f32))
        if near:
            acc = lax.cond(
                scal_ref[geo.parts + tile] < near,
                functools.partial(step, range(near)),
                lambda same: same,
                acc,
            )
        packed = pack_rows((acc[:HD] * (HD**-0.5)).T).astype(bf16)
        for i in range(geo.per_tile):
            dq_ref[tile * geo.per_tile + i] = packed[i * geo.half : (i + 1) * geo.half]
    for part in range(geo.parts):
        for tile in range(geo.tiles):
            for i in range(geo.per_tile):
                rows = acc_ref[part, tile, i * geo.part_rows : (i + 1) * geo.part_rows]
                grad_refs[part][tile * geo.per_tile + i] = rows.astype(grad_refs[part].dtype)


COST = {
    "assemble": 100000000,
    "attention_backward": 30000000000,
    "attention_forward": 30000000000,
    "feed": 30000000000,
    "feed_grad": 100000000,
    "final": 100000000,
    "fold": 30000000000,
    "input_grad": 100000000,
    "input_partial": 30000000000,
    "middle_grad": 30000000000,
    "norm_again": 100000000,
    "part_sum": 30000000000,
    "project": 30000000000,
    "project_grad": 30000000000,
    "split": 100000000,
}


VMEM_LIMIT = 16 * 2**20


def far(shape, dtype):
    return (pltpu.HBM(shape, dtype),)


def local_call(kernel, name, scalars, arrays, outs, scratch=(), limit=VMEM_LIMIT):
    return pl.pallas_call(
        kernel,
        out_shape=tuple(o[0] if len(o) == 1 else jax.ShapeDtypeStruct(*o) for o in outs),
        in_specs=[pl.BlockSpec(memory_space=pltpu.SMEM)]
        + [pl.BlockSpec(memory_space=pltpu.VMEM)] * len(arrays),
        out_specs=tuple([pl.BlockSpec(memory_space=pltpu.VMEM)] * len(outs)),
        scratch_shapes=list(scratch),
        compiler_params=pltpu.CompilerParams(vmem_limit_bytes=limit),
        cost_estimate=pl.CostEstimate(flops=COST.get(name, 10**8), bytes_accessed=10**6, transcendentals=0),
        name=name,
    )(scalars, *arrays)


def attention_limit(geo):
    return VMEM_LIMIT if geo.parts == 2 else 3 * VMEM_LIMIT


def attention_forward(geo, scalars, part_arrays, bounds):
    return local_call(
        functools.partial(forward_kernel, geo),
        "attention_forward",
        scalars,
        [*part_arrays, bounds],
        [
            ((geo.blocks, geo.half, LANES), bf16),
            far((geo.tiles, HD, geo.tile), f32),
            far((geo.tiles, 8, geo.tile), f32),
        ],
        [pltpu.VMEM((geo.parts, geo.tiles, ONES + HD, geo.tile), bf16)],
        limit=attention_limit(geo),
    )


def attention_backward(geo, do_tile, scalars, part_arrays, do, bounds, ot, lse):
    grads = [((geo.blocks, geo.part_rows, LANES), f32)]
    grads += [((geo.blocks, geo.part_rows, LANES), bf16)] * (geo.parts - 1)
    return local_call(
        functools.partial(backward_kernel, geo, do_tile),
        "attention_backward",
        scalars,
        [*part_arrays, do, bounds, ot, lse],
        [((geo.blocks, geo.half, LANES), bf16), *grads],
        [
            pltpu.VMEM((geo.parts, geo.tiles, geo.tile, LANES), f32),
            pltpu.VMEM((geo.parts, geo.tiles, LANES, geo.tile), bf16),
        ],
        limit=attention_limit(geo),
    )


def do_tile_grouped(do_ref, geo, tile):
    heads = do_ref.shape[0] // geo.blocks
    pieces = []
    for i in range(geo.per_tile):
        for head in range(heads):
            pieces.append(do_ref[head * geo.blocks + tile * geo.per_tile + i])
    return jnp.concatenate(pieces, axis=0)


def do_tile_plain(do_ref, geo, tile):
    return task_tile(do_ref, geo, tile, 0, geo.half)


def query_positions(blocks, heads, run, sub, part, geo):
    half = run // 2
    block = jnp.arange(blocks, dtype=i32).reshape(geo.tiles, 1, geo.per_tile, 1, 1)
    upper = jnp.arange(2, dtype=i32).reshape(1, 2, 1, 1, 1)
    head = jnp.arange(heads, dtype=i32).reshape(1, 1, 1, heads, 1)
    row = jnp.arange(half, dtype=i32).reshape(1, 1, 1, 1, half)
    at = block * (heads * sub) + head * sub + part * run + upper * half + row
    return at.reshape(geo.tiles, 1, geo.tile)


def attention_bounds(segments, token_valid, my_seq, my_part, geo, heads, sub):
    seg = lax.dynamic_index_in_dim(segments, my_seq, 0, keepdims=False)
    valid = jnp.sum(lax.dynamic_index_in_dim(token_valid, my_seq, 0, keepdims=False))
    own = query_positions(geo.blocks, heads, geo.run, sub, my_part, geo)
    half = geo.run // 2
    own_seg = seg.reshape(geo.blocks * heads, geo.parts, geo.run)
    own_seg = lax.dynamic_index_in_dim(own_seg, my_part, 1, keepdims=False)
    own_seg = own_seg.reshape(geo.tiles, geo.per_tile, heads, 2, half).transpose(0, 3, 1, 2, 4)
    own_seg = own_seg.reshape(-1, 1)
    start = jnp.sum((seg[None, :] < own_seg).astype(i32), axis=1).reshape(geo.tiles, 1, geo.tile)
    last = jnp.minimum(own, valid - 1)
    bounds = jnp.concatenate([start, last, own, jnp.zeros((geo.tiles, 5, geo.tile), i32)], axis=1)
    first_seg = seg.reshape(geo.tiles, geo.span)[:, :1]
    first_tile = jnp.sum((seg[None, :] < first_seg).astype(i32), axis=1) // geo.span
    part_at = ((my_part - jnp.arange(geo.parts, dtype=i32)) % geo.parts) * geo.run
    return jnp.concatenate([part_at, first_tile]), bounds


def gather_head(x):
    return lax.all_gather(x, "head", axis=0, tiled=False)


def exchange(x, axis):
    return lax.all_to_all(x, axis, split_axis=0, concat_axis=0, tiled=True)


def within_group(blocks, parts, step):
    return [
        (t * parts + i, t * parts + (i + step) % parts)
        for t in range(blocks // parts)
        for i in range(parts)
    ]


def on_device_general(
    layer_input,
    segments,
    token_valid,
    attention_gain,
    attention_shift,
    project_weight,
    project_bias,
    output_weight,
    output_bias,
    feed_gain,
    feed_shift,
    up_weight,
    up_bias,
    down_weight,
    down_bias,
    cotangent,
):
    heads = lax.axis_size("head")
    blocks = lax.axis_size("blk")
    my_head = lax.axis_index("head")
    my_blk = lax.axis_index("blk")
    devices = heads * blocks
    seqs, _, sub, width = layer_input.shape
    hidden_width = up_weight.shape[1]
    hidden_slice = hidden_width // heads
    rows = sub * heads
    length = rows * blocks
    mine = seqs * sub
    tokens = seqs * rows
    local = H // heads
    cols = local * HD
    parts = blocks // (seqs * local)
    run = sub // parts
    part_rows = heads * run
    half = part_rows // 2
    w_rows = width // devices
    f_rows = hidden_width // devices
    geo = AttentionShape(blocks, part_rows, parts, run, sub)

    wp = project_weight.reshape(w_rows, 3, heads, local, HD)
    wq = wp[:, 0].transpose(1, 0, 2, 3).reshape(heads, w_rows, cols)
    wq = jnp.pad(wq, ((0, 0), (0, 0), (0, LANES - cols)))
    wkv = wp[:, 1:].transpose(2, 3, 0, 1, 4).reshape(heads, local * w_rows, LANES)
    small = [attention_gain, attention_shift, output_bias, feed_gain, feed_shift, down_bias]
    small += [project_bias, up_bias]
    counts = [v.shape[0] for v in small]
    small = jnp.concatenate(small)
    small_rows = -(-small.shape[0] // LANES)
    small = jnp.pad(small, (0, small_rows * LANES - small.shape[0])).reshape(1, small_rows, LANES)
    chunk = jnp.concatenate([wq, wkv, jnp.broadcast_to(small, (heads, small_rows, LANES))], axis=1)
    chunk_rows = chunk.shape[1]
    send = jnp.broadcast_to(chunk[:, None], (heads, blocks, chunk_rows, LANES))
    got = exchange(send.reshape(devices, chunk_rows, LANES), BOTH)
    w_groups = [
        got[:, i * w_rows : (i + 1) * w_rows].reshape(width, LANES) for i in range(1 + local)
    ]
    w_slice = jnp.concatenate(w_groups, axis=1)
    flat = got[:, (1 + local) * w_rows :].reshape(devices, small_rows * LANES).astype(f32)
    vectors = []
    at = 0
    for count in counts:
        vectors.append(flat[:, at : at + count].reshape(-1))
        at += count
    gain_one, shift_one, b_output, gain_two, shift_two, b_down, b_project, b_up = vectors

    x_mine = layer_input.reshape(mine, width)
    g_mine = cotangent.reshape(mine, width)
    x_all = gather_head(x_mine).reshape(heads, seqs, sub, width).transpose(1, 0, 2, 3)
    g_all = gather_head(g_mine).reshape(heads, seqs, sub, width).transpose(1, 0, 2, 3)
    x_all = x_all.reshape(tokens, width).astype(f32)
    g_all = g_all.reshape(tokens, width)

    up_parts = up_weight.reshape(w_rows, heads, hidden_slice).transpose(1, 0, 2)
    out_parts = jnp.broadcast_to(output_weight[None], (heads, w_rows, width))
    if hidden_slice == width:
        both = exchange(jnp.concatenate([up_parts, out_parts], axis=1), "head")
        shard = jnp.concatenate([both.reshape(2 * heads * w_rows, width), down_weight], axis=0)
        full = lax.all_gather(shard, "blk", axis=0, tiled=False)
        pair = full[:, : 2 * heads * w_rows].reshape(blocks, heads, 2, w_rows, width)
        w_up = pair[:, :, 0].transpose(1, 0, 2, 3).reshape(width, hidden_slice)
        w_out = pair[:, :, 1].transpose(1, 0, 2, 3).reshape(width, width)
        w_down = full[:, 2 * heads * w_rows :].reshape(hidden_slice, width)
    else:
        up_parts = lax.all_gather(exchange(up_parts, "head"), "blk", axis=0, tiled=False)
        out_parts = lax.all_gather(exchange(out_parts, "head"), "blk", axis=0, tiled=False)
        w_up = up_parts.transpose(1, 0, 2, 3).reshape(width, hidden_slice)
        w_out = out_parts.transpose(1, 0, 2, 3).reshape(width, width)
        w_down = lax.all_gather(down_weight, "blk", axis=0, tiled=True)

    n_one, u_one, rs_one = norm_forward(x_all, gain_one, shift_one)
    n_one = n_one.astype(bf16)
    qkv = dot_nn(n_one, w_slice)
    b_q = lax.dynamic_slice(b_project, (my_head * cols,), (cols,))
    b_v = lax.dynamic_slice(b_project, (width + my_head * cols,), (cols,))
    queries = (qkv[:, :cols] + b_q).astype(bf16)
    pairs = qkv[:, LANES:].reshape(tokens, local, 2, HD)
    b_pair = jnp.stack([jnp.zeros((local, HD), f32), b_v.reshape(local, HD)], axis=1)
    pairs = (pairs + b_pair).astype(bf16)
    queries = queries.reshape(seqs, heads, parts, 2, run // 2, local, HD)
    queries = queries.transpose(0, 5, 2, 1, 4, 3, 6).reshape(blocks, half, LANES)
    pairs = pairs.reshape(seqs, heads, parts, run, local, LANES).transpose(0, 4, 2, 1, 3, 5)
    pairs = pairs.reshape(blocks, part_rows, LANES)
    task = exchange(jnp.concatenate([queries, pairs], axis=1), "blk")
    part_arrays = [task]
    for step in range(1, parts):
        part_arrays.append(lax.ppermute(task, "blk", within_group(blocks, parts, step)))

    my_part = my_blk % parts
    my_seq = (my_blk // parts) // local
    scalars, bounds = attention_bounds(segments, token_valid, my_seq, my_part, geo, heads, sub)
    o_task, ot, lse = attention_forward(geo, scalars, part_arrays, bounds)

    got = exchange(o_task, "blk")
    mixed = got.reshape(seqs, local, parts, heads, run // 2, 2, HD)
    mixed = mixed.transpose(0, 3, 2, 5, 4, 1, 6)
    mixed = mixed.reshape(tokens, cols)
    mixed_all = lax.all_gather(mixed, "head", axis=1, tiled=True)

    middle = x_all + dot_nn(mixed_all, w_out) + b_output
    n_two, u_two, rs_two = norm_forward(middle, gain_two, shift_two)
    n_two = n_two.astype(bf16)
    b_up_slice = lax.dynamic_slice(b_up, (my_head * hidden_slice,), (hidden_slice,))
    hidden = dot_nn(n_two, w_up) + b_up_slice
    sigma = jax.nn.sigmoid(1.702 * hidden)
    activated = (hidden * sigma).astype(bf16)
    feed = dot_nn(activated, w_down)
    grad_act = dot_nt(g_all, w_down)
    grad_hidden = (grad_act * (sigma + 1.702 * hidden * sigma * (1.0 - sigma))).astype(bf16)
    grad_two = dot_nt(grad_hidden, w_up)

    def to_owners(partial):
        partial = partial.astype(bf16).reshape(seqs, heads, sub, width).transpose(1, 0, 2, 3)
        return exchange(partial.reshape(heads, mine, width), "head")

    def my_tokens(values):
        values = values.reshape(seqs, heads, sub, values.shape[-1])
        values = lax.dynamic_index_in_dim(values, my_head, 1, keepdims=False)
        return values.reshape(mine, values.shape[-1])

    grad_two_mine = jnp.sum(to_owners(grad_two).astype(f32), axis=0)
    grad_middle = g_mine.astype(f32) + norm_input_grad(
        grad_two_mine, my_tokens(u_two), my_tokens(rs_two), gain_two
    )
    grad_branch = grad_middle.astype(bf16)
    grad_mixed = dot_nt(grad_branch, w_out).astype(bf16)
    grad_mixed = grad_mixed.reshape(seqs, parts, 2, run // 2, heads, local, HD)
    grad_mixed = grad_mixed.transpose(4, 0, 5, 1, 3, 2, 6).reshape(devices, run // 2, LANES)
    got = exchange(grad_mixed, BOTH).reshape(heads, blocks, run // 2, LANES)
    do_task = got.transpose(1, 0, 2, 3).reshape(blocks, half, LANES)

    feed_mine = jnp.sum(to_owners(feed).astype(f32), axis=0)
    layer_output = my_tokens(middle) + feed_mine + b_down

    grad_down = dot_tn(activated, g_all).astype(bf16).reshape(blocks, -1, width)
    grad_up = dot_tn(n_two, grad_hidden).astype(bf16)
    grad_up = grad_up.reshape(heads, blocks, w_rows, hidden_slice).transpose(1, 0, 2, 3)
    branch_all = gather_head(grad_branch).reshape(heads, seqs, sub, width).transpose(1, 0, 2, 3)
    grad_out = dot_tn(mixed, branch_all.reshape(tokens, width)).astype(bf16)

    def over_blocks(partial):
        return lax.psum_scatter(partial, "blk", scatter_dimension=0, tiled=True)

    if hidden_slice == width:
        summed = over_blocks(
            jnp.concatenate(
                [grad_down.reshape(blocks, f_rows, width), grad_up.reshape(blocks, -1, width)],
                axis=1,
            ).reshape(-1, width)
        )
        own_down = summed[:f_rows]
        own_up = summed[f_rows:]
    else:
        own_down = over_blocks(grad_down.reshape(-1, width))
        own_up = over_blocks(grad_up.reshape(-1, hidden_slice))
    own_out = over_blocks(grad_out)
    own_up = exchange(own_up.reshape(heads, w_rows, hidden_slice), "head")
    own_up = own_up.transpose(1, 0, 2).reshape(w_rows, hidden_width)

    dq_task, dkv, *others = attention_backward(
        geo, do_tile_plain, scalars, part_arrays, do_task, bounds, ot, lse
    )
    for step in range(1, parts):
        back = within_group(blocks, parts, -step)
        dkv = dkv + lax.ppermute(others[step - 1], "blk", back).astype(f32)
    got = exchange(jnp.concatenate([dq_task, dkv.astype(bf16)], axis=1), "blk")
    dq = got[:, :half].reshape(seqs, local, parts, heads, run // 2, 2, HD)
    dq = dq.transpose(0, 3, 2, 5, 4, 1, 6)
    dq = dq.reshape(tokens, cols)
    dkv = got[:, half:].reshape(seqs, local, parts, heads, run, LANES).transpose(0, 3, 2, 4, 1, 5)
    dkv = dkv.reshape(tokens, local * LANES)
    dq = jnp.pad(dq, ((0, 0), (0, LANES - cols)))
    d_proj = jnp.concatenate([dq, dkv], axis=1)

    grad_one = dot_nt(d_proj, w_slice)
    grad_one_mine = jnp.sum(to_owners(grad_one).astype(f32), axis=0)
    x_f32 = x_mine.astype(f32)
    input_grad = grad_middle + norm_input_grad(
        grad_one_mine, my_tokens(u_one), my_tokens(rs_one), gain_one
    )

    grad_w = dot_tn(n_one, d_proj).astype(bf16)
    col_sums = jnp.sum(d_proj.astype(f32), axis=0)
    bias_q = col_sums[:cols]
    bias_v = col_sums[LANES:].reshape(local, 2, HD)[:, 1].reshape(cols)
    bias_grad = jnp.zeros((2 * width,), f32)
    bias_grad = lax.dynamic_update_slice(bias_grad, bias_q, (my_head * cols,))
    bias_grad = lax.dynamic_update_slice(bias_grad, bias_v, (width + my_head * cols,))
    up_bias_grad = lax.dynamic_update_slice(
        jnp.zeros((hidden_width,), f32),
        jnp.sum(grad_hidden.astype(f32), axis=0),
        (my_head * hidden_slice,),
    )
    tiny = [
        jnp.sum(grad_one * u_one, axis=0),
        jnp.sum(grad_one, axis=0),
        jnp.sum(grad_branch.astype(f32), axis=0),
        jnp.sum(grad_two * u_two, axis=0),
        jnp.sum(grad_two, axis=0),
        jnp.sum(g_mine.astype(f32), axis=0),
        bias_grad,
        up_bias_grad,
    ]
    tiny = jnp.concatenate([v.reshape(devices, -1) for v in tiny], axis=1)
    high = tiny.astype(bf16)
    low = (tiny - high.astype(f32)).astype(bf16)
    tiny = jnp.concatenate([high, low], axis=1)
    tiny_rows = -(-tiny.shape[1] // LANES)
    tiny = jnp.pad(tiny, ((0, 0), (0, tiny_rows * LANES - tiny.shape[1])))
    tiny = tiny.reshape(devices, tiny_rows, LANES)
    grad_w = [
        grad_w[:, i * LANES : (i + 1) * LANES].reshape(devices, w_rows, LANES)
        for i in range(1 + local)
    ]
    got = exchange(jnp.concatenate(grad_w + [tiny], axis=1), BOTH)
    got = got.astype(f32)
    n_w = (1 + local) * w_rows
    own_w = jnp.sum(got[:, :n_w].reshape(heads, blocks, n_w, LANES), axis=1)
    own_q = own_w[:, :w_rows, :cols].transpose(1, 0, 2).reshape(w_rows, width)
    own_kv = own_w[:, w_rows:].reshape(heads, local, w_rows, 2, HD)
    own_kv = own_kv.transpose(2, 3, 0, 1, 4).reshape(w_rows, 2 * width)
    own_w = jnp.concatenate([own_q, own_kv], axis=1)
    summed = jnp.sum(got[:, n_w:].reshape(devices, -1), axis=0)
    total = sum(counts)
    summed = summed[:total] + summed[total : 2 * total]
    owned = []
    at = 0
    for count in counts:
        owned.append(summed[at : at + count])
        at += count

    return (
        layer_output.astype(bf16).reshape(layer_input.shape),
        input_grad.astype(bf16).reshape(layer_input.shape),
        owned[0],
        owned[1],
        own_w,
        owned[6],
        own_out.astype(f32),
        owned[2],
        owned[3],
        owned[4],
        own_up.astype(f32),
        owned[7],
        own_down.astype(f32),
        owned[5],
    )


class Sizes:
    def __init__(self, heads, blocks, seqs, sub, width, hidden_width):
        self.heads = heads
        self.blocks = blocks
        self.seqs = seqs
        self.sub = sub
        self.width = width
        self.devices = heads * blocks
        self.mine = seqs * sub
        self.tokens = self.mine * heads
        self.local = H // heads
        self.parts = blocks // (seqs * self.local)
        self.run = sub // self.parts
        self.part_rows = heads * self.run
        self.half = self.part_rows // 2
        self.w_rows = width // self.devices
        self.f_rows = hidden_width // self.devices
        self.hidden_slice = hidden_width // heads
        self.w_chunk = (1 + self.local) * self.w_rows
        self.head_rows = self.blocks * self.w_rows
        self.groups = blocks // self.parts

    def fits(self):
        return (
            self.local == 2
            and self.parts == 2
            and self.run % 32 == 0
            and self.w_rows == 16
            and self.hidden_slice == self.width
            and self.mine % 16 == 0
            and self.f_rows % 16 == 0
        )

    def task(self, seq, local, part):
        return (seq * self.local + local) * self.parts + part


SMALL = 8


def my_head_of(sz, scal_ref):
    return scal_ref[0] // sz.blocks


def my_blk_of(sz, scal_ref):
    return lax.rem(scal_ref[0], sz.blocks)


def slot_head(sz, scal_ref, slot):
    return lax.rem(my_head_of(sz, scal_ref) - slot + sz.heads, sz.heads)


def halves(first, second):
    low = jnp.concatenate([first[:, :HD], second[:, :HD]], axis=1)
    high = jnp.concatenate([first[:, HD:], second[:, HD:]], axis=1)
    return low, high


def staged(count, refs):
    scratch = refs[len(refs) - count - 1 :]
    held, sems = scratch[:count], scratch[count]
    copies = [pltpu.make_async_copy(refs[i], held[i], sems.at[i]) for i in range(count)]
    for copy in copies:
        copy.start()
    for copy in copies:
        copy.wait()
    return held


def staged_call(kernel, name, scalars, arrays, outs, scratch=()):
    return pl.pallas_call(
        kernel,
        out_shape=tuple(jax.ShapeDtypeStruct(*o) for o in outs),
        in_specs=[pl.BlockSpec(memory_space=pltpu.SMEM)]
        + [pl.BlockSpec(memory_space=pltpu.HBM)] * len(arrays),
        out_specs=tuple([pl.BlockSpec(memory_space=pltpu.VMEM)] * len(outs)),
        scratch_shapes=list(scratch)
        + [pltpu.VMEM(v.shape, v.dtype) for v in arrays]
        + [pltpu.SemaphoreType.DMA((len(arrays),))],
        compiler_params=pltpu.CompilerParams(vmem_limit_bytes=63 * 2**20),
        name=name,
    )(scalars, *arrays)


def pack_kernel(sz, scal_ref, *refs):
    count = 1 + SMALL
    send_ref, small_scr = refs[count : count + 2]
    small_scr[...] = jnp.zeros_like(small_scr)
    wp_ref, *small_refs = staged(count, refs)
    for i, ref in enumerate(small_refs):
        small_scr[i : i + 1, : ref.shape[1]] = ref[...].astype(f32)
    small = small_scr[...].astype(bf16)
    for head in range(sz.heads):
        at = head * LANES
        q = wp_ref[:, at : at + LANES]
        k = wp_ref[:, sz.width + at : sz.width + at + LANES]
        v = wp_ref[:, 2 * sz.width + at : 2 * sz.width + at + LANES]
        low, high = halves(k, v)
        chunk = jnp.concatenate([q, low, high], axis=0)
        for group in range(sz.groups):
            send_ref[head * sz.groups + group, : sz.w_chunk] = chunk
            send_ref[head * sz.groups + group, sz.w_chunk :] = small


def pieces_kernel(sz, scal_ref, *refs):
    piece_refs = refs[3 : 3 + sz.heads]
    g_ref, up_ref, wo_ref = staged(3, refs)
    for step, ref in enumerate(piece_refs):
        to = lax.rem(my_head_of(sz, scal_ref) + step, sz.heads)
        at = pl.multiple_of(to * sz.hidden_slice, LANES)
        ref[: sz.mine] = g_ref[...]
        ref[sz.mine : sz.mine + sz.w_rows] = up_ref[:, pl.ds(at, sz.hidden_slice)]
        ref[sz.mine + sz.w_rows :] = wo_ref[...]


def spread(small, per, offset, count):
    lane = lax.broadcasted_iota(i32, (LANES, count), 0)
    at = lax.broadcasted_iota(i32, (LANES, count), 1) + offset
    pick = jnp.where(at % per == lane, 1.0, 0.0).astype(bf16)
    wide = dot_nn(small, pick)
    source = lax.broadcasted_iota(i32, wide.shape, 0) // SMALL
    column = (lax.broadcasted_iota(i32, wide.shape, 1) + offset) // per
    wide = jnp.where(source == column, wide, 0.0)
    return jnp.sum(wide.reshape(-1, SMALL, count), axis=0)


def collect(values, per, offset, rows, devices):
    count = values.shape[1]
    tall = jnp.broadcast_to(values[None], (devices, SMALL, count)).reshape(devices * SMALL, count)
    row = lax.broadcasted_iota(i32, tall.shape, 0)
    column = (lax.broadcasted_iota(i32, tall.shape, 1) + offset) // per
    index = row % SMALL
    keep = (row // SMALL == column) & (index >= rows[0]) & (index < rows[1])
    tall = jnp.where(keep, tall, 0.0)
    lane = lax.broadcasted_iota(i32, (count, LANES), 1)
    at = lax.broadcasted_iota(i32, (count, LANES), 0) + offset
    pick = jnp.where(at % per == lane, 1.0, 0.0).astype(bf16)
    return dot_nn(tall.astype(bf16), pick)


def source_blk(sz, scal_ref, group_slot, part_slot):
    group = lax.rem(my_blk_of(sz, scal_ref) // sz.parts - group_slot + sz.groups, sz.groups)
    part = lax.rem(my_blk_of(sz, scal_ref) % sz.parts - part_slot + sz.parts, sz.parts)
    return group * sz.parts + part


def project_kernel(sz, scal_ref, *refs):
    got_refs, refs = refs[: sz.parts], refs[sz.parts :]
    x_refs = refs[: sz.heads]
    send_ref, w_ref, vec_ref, small_scr = refs[sz.heads :]
    head = my_head_of(sz, scal_ref)
    for part_slot, ref in enumerate(got_refs):
        part = lax.rem(my_blk_of(sz, scal_ref) + sz.parts - part_slot, sz.parts)
        for src in range(sz.heads * sz.groups):
            dev = src // sz.groups * sz.blocks + src % sz.groups * sz.parts + part
            at = pl.multiple_of(dev * sz.w_rows, sz.w_rows)
            for i in range(1 + sz.local):
                piece = ref[src, i * sz.w_rows : (i + 1) * sz.w_rows]
                w_ref[pl.ds(at, sz.w_rows), i * LANES : (i + 1) * LANES] = piece
            at = pl.multiple_of(dev * SMALL, SMALL)
            small_scr[pl.ds(at, SMALL)] = ref[src, sz.w_chunk :].astype(f32)
    small = small_scr[...].astype(bf16)
    vec = spread(small, sz.w_rows, 0, sz.width)
    per = 2 * sz.w_rows
    b_q = spread(small, per, head * LANES, LANES)[6:7]
    b_v = spread(small, per, sz.width + head * LANES, LANES)[6:7]
    b_up = spread(small, 4 * sz.w_rows, head * sz.hidden_slice, sz.hidden_slice)
    row = lax.broadcasted_iota(i32, vec.shape, 0)
    vec = jnp.where(row == 7, b_up, vec)
    vec_ref[...] = vec
    zero = jnp.zeros((1, HD), f32)
    bias = jnp.concatenate([b_q, zero, b_v[:, :HD], zero, b_v[:, HD:]], axis=1)
    gain, shift = vec[0:1], vec[1:2]
    for slot in range(sz.heads):
        x = x_refs[slot][...].astype(f32)
        normed = norm_forward(x, gain, shift)[0].astype(bf16)
        qkv = (dot_nn(normed, w_ref[...]) + bias).astype(bf16)
        to = slot_head(sz, scal_ref, slot)
        half_run = sz.run // 2
        for seq in range(sz.seqs):
            for part in range(sz.parts):
                at = seq * sz.sub + part * sz.run
                low, high = halves(qkv[at : at + half_run, :LANES], qkv[at + half_run : at + sz.run, :LANES])
                packed = (low, high)
                for local in range(sz.local):
                    task = sz.task(seq, local, part)
                    q_at = pl.multiple_of(to * half_run, half_run)
                    send_ref[task, pl.ds(q_at, half_run)] = packed[local]
                    kv_at = pl.multiple_of(sz.half + to * sz.run, sz.run)
                    send_ref[task, pl.ds(kv_at, sz.run)] = qkv[
                        at : at + sz.run, (1 + local) * LANES : (2 + local) * LANES
                    ]


def assemble_kernel(sz, scal_ref, *refs):
    chunks = sz.parts * sz.groups
    mixed_refs, down_refs = refs[:chunks], refs[chunks : 2 * chunks]
    up_ref, wo_ref, down_ref = refs[2 * chunks :]
    for part_slot in range(sz.parts):
        for group_slot in range(sz.groups):
            i = part_slot * sz.groups + group_slot
            blk = source_blk(sz, scal_ref, group_slot, part_slot)
            at = pl.multiple_of(blk * sz.f_rows, sz.f_rows)
            down_ref[pl.ds(at, sz.f_rows)] = down_refs[i][...]
            for slot in range(sz.heads):
                head = slot_head(sz, scal_ref, slot)
                at = pl.multiple_of(head * sz.head_rows + blk * sz.w_rows, sz.w_rows)
                first = 2 * slot * sz.w_rows
                up_ref[pl.ds(at, sz.w_rows)] = mixed_refs[i][first : first + sz.w_rows]
                at = pl.multiple_of(slot * sz.head_rows + blk * sz.w_rows, sz.w_rows)
                first += sz.w_rows
                wo_ref[pl.ds(at, sz.w_rows)] = mixed_refs[i][first : first + sz.w_rows]


def feed_kernel(sz, scal_ref, vec_ref, up_ref, wo_ref, down_ref, *refs):
    n = sz.heads
    x_refs, g_refs, m_refs = refs[:n], refs[n : 2 * n], refs[2 * n : 3 * n]
    outs = refs[3 * n :]
    part_refs, feed_refs = outs[:n], outs[n : 2 * n]
    mid_ref, act_ref, dh_ref, n_ref, mix_own_ref, sum_ref, mix_scr = outs[2 * n :]
    half_run = sz.run // 2
    for slot in range(n):
        for seq in range(sz.seqs):
            for part in range(sz.parts):
                first = m_refs[slot][sz.task(seq, 0, part)]
                second = m_refs[slot][sz.task(seq, 1, part)]
                low, high = halves(first, second)
                for head in range(n):
                    at = seq * sz.sub + part * sz.run
                    cols = slice(slot * LANES, (slot + 1) * LANES)
                    rows = slice(head * half_run, (head + 1) * half_run)
                    mix_scr[head, at : at + half_run, cols] = low[rows]
                    mix_scr[head, at + half_run : at + sz.run, cols] = high[rows]
    w_down = down_ref[...]
    b_out, gain, shift, b_up = vec_ref[2:3], vec_ref[3:4], vec_ref[4:5], vec_ref[7:8]
    sums = jnp.zeros((3, sz.width), f32)
    group = 2
    for first in range(0, n, group):
        slots = range(first, first + group)
        x = jnp.concatenate([x_refs[s][...] for s in slots], axis=0).astype(f32)
        g = jnp.concatenate([g_refs[s][: sz.mine] for s in slots], axis=0)
        mixed = jnp.concatenate([mix_scr[slot_head(sz, scal_ref, s)] for s in slots], axis=0)
        middle = x + dot_nn(mixed, wo_ref[...]) + b_out
        normed, unit, _ = norm_forward(middle, gain, shift)
        normed = normed.astype(bf16)
        hidden = dot_nn(normed, up_ref[...]) + b_up
        sigma = 1.0 / (1.0 + jnp.exp(-1.702 * hidden))
        activated = (hidden * sigma).astype(bf16)
        slope = sigma + 1.702 * hidden * sigma * (1.0 - sigma)
        grad_hidden = (dot_nt(g, w_down) * slope).astype(bf16)
        grad_two = dot_nt(grad_hidden, up_ref[...])
        feed = dot_nn(activated, w_down)
        sums = sums + jnp.concatenate(
            [
                jnp.sum(grad_two * unit, axis=0, keepdims=True),
                jnp.sum(grad_two, axis=0, keepdims=True),
                jnp.sum(grad_hidden.astype(f32), axis=0, keepdims=True),
            ],
            axis=0,
        )
        for i, s in enumerate(slots):
            rows = slice(i * sz.mine, (i + 1) * sz.mine)
            part_refs[s][...] = grad_two[rows].astype(part_refs[s].dtype)
            feed_refs[s][...] = feed[rows].astype(feed_refs[s].dtype)
            if s == 0:
                mid_ref[...] = middle[rows]
                mix_own_ref[...] = mixed[rows]
            act_ref[s] = activated[rows]
            dh_ref[s] = grad_hidden[rows]
            n_ref[s] = normed[rows]
    sum_ref[...] = jnp.concatenate([sums, jnp.zeros((5, sz.width), f32)], axis=0)


def give_and_keep(sz, scal_ref, values, rows, keep_ref, give_ref):
    part = my_blk_of(sz, scal_ref) % sz.parts
    for blk in range(sz.blocks):
        group = blk // sz.parts
        piece = values(blk)
        @pl.when(part == blk % sz.parts)
        def _():
            keep_ref[group] = piece

        @pl.when(part != blk % sz.parts)
        def _():
            give_ref[group] = piece.astype(bf16)


def feed_grad_kernel(sz, scal_ref, act_ref, dh_ref, n_ref, *refs):
    g_refs = refs[: sz.heads]
    keep_ref, give_ref = refs[sz.heads :]
    g = jnp.concatenate([ref[: sz.mine] for ref in g_refs], axis=0)
    act = act_ref[...].reshape(sz.tokens, sz.hidden_slice)
    down = dot_tn(act, g)
    up = dot_tn(n_ref[...].reshape(sz.tokens, sz.width), dh_ref[...].reshape(sz.tokens, sz.hidden_slice))

    def piece(blk):
        pieces = [down[blk * sz.f_rows : (blk + 1) * sz.f_rows]]
        for head in range(sz.heads):
            at = head * sz.head_rows + blk * sz.w_rows
            pieces.append(up[at : at + sz.w_rows])
        return jnp.concatenate(pieces, axis=0)

    give_and_keep(sz, scal_ref, piece, sz.f_rows + sz.heads * sz.w_rows, keep_ref, give_ref)


def part_sum_kernel(sz, scal_ref, *refs):
    keep_ref, got_ref, keep_out_ref, got_out_ref, *refs = refs
    down_refs, rest_refs = refs[: sz.groups], refs[sz.groups :]
    rows = keep_ref.shape[1] - sz.f_rows
    for step in range(sz.groups):
        to = lax.rem(my_blk_of(sz, scal_ref) // sz.parts + step, sz.groups)
        total = keep_ref[to] + got_ref[to].astype(f32)
        total_out = keep_out_ref[to] + got_out_ref[to].astype(f32)
        dtype = rest_refs[step].dtype
        down_refs[step][...] = total[: sz.f_rows].astype(dtype)
        rest_refs[step][:rows] = total[sz.f_rows :].astype(dtype)
        rest_refs[step][rows:] = total_out.astype(dtype)


def middle_grad_kernel(sz, scal_ref, vec_ref, wo_ref, mid_ref, g_ref, mix_ref, *refs):
    n = sz.heads
    part_refs = refs[:n]
    grad_ref, branch_ref, send_ref, sum_ref, keep_ref, give_ref = refs[n:]
    upstream = part_refs[0][...]
    for ref in part_refs[1:]:
        upstream = upstream + ref[...].astype(f32)
    gain, shift = vec_ref[3:4], vec_ref[4:5]
    _, unit, root = norm_forward(mid_ref[...], gain, shift)
    g = g_ref[...].astype(f32)
    grad = g + norm_input_grad(upstream, unit, root, gain)
    grad_ref[...] = grad
    branch = grad.astype(bf16)
    branch_ref[...] = branch
    sum_ref[...] = jnp.concatenate(
        [
            jnp.sum(branch.astype(f32), axis=0, keepdims=True),
            jnp.sum(g, axis=0, keepdims=True),
            jnp.zeros((6, sz.width), f32),
        ],
        axis=0,
    )
    mixed = dot_nt(branch, wo_ref[...]).astype(bf16)
    half_run = sz.run // 2
    for slot in range(n):
        to = slot_head(sz, scal_ref, slot)
        for seq in range(sz.seqs):
            for part in range(sz.parts):
                at = seq * sz.sub + part * sz.run
                cols = slice(slot * LANES, (slot + 1) * LANES)
                packed = halves(mixed[at : at + half_run, cols], mixed[at + half_run : at + sz.run, cols])
                for local in range(sz.local):
                    send_ref[to * sz.blocks + sz.task(seq, local, part)] = packed[local]
    out_grad(sz, scal_ref, mix_ref[...], branch, keep_ref, give_ref)


def out_grad(sz, scal_ref, mixed, branch, keep_ref, give_ref):
    grad = dot_tn(mixed, branch)
    part = my_blk_of(sz, scal_ref) % sz.parts
    for slot in range(sz.heads):
        head = slot_head(sz, scal_ref, slot)
        to = pl.multiple_of(head * sz.w_rows, sz.w_rows)
        for blk in range(sz.blocks):
            at = slot * sz.head_rows + blk * sz.w_rows
            piece = grad[at : at + sz.w_rows]

            @pl.when(part == blk % sz.parts)
            def _():
                keep_ref[blk // sz.parts, pl.ds(to, sz.w_rows)] = piece

            @pl.when(part != blk % sz.parts)
            def _():
                give_ref[blk // sz.parts, pl.ds(to, sz.w_rows)] = piece.astype(bf16)


def norm_again_kernel(sz, scal_ref, vec_ref, *refs):
    x_refs = refs[: sz.heads]
    n_ref, u_ref = refs[sz.heads :]
    gain, shift = vec_ref[0:1], vec_ref[1:2]
    for slot in range(sz.heads):
        normed, unit, _ = norm_forward(x_refs[slot][...].astype(f32), gain, shift)
        at = slice(slot * sz.mine, (slot + 1) * sz.mine)
        n_ref[:, at] = normed.astype(bf16).T
        u_ref[:, at] = unit.astype(bf16).T


def both_levels(values, *where):
    high = values.astype(bf16).astype(f32)
    return collect(high, *where) + collect(values - high, *where)


def project_grad_kernel(sz, scal_ref, early_ref, *refs):
    far_refs, (keep_ref, give_ref), refs = refs[:4], refs[4:6], refs[6:]
    part_refs, refs = refs[: sz.heads], refs[sz.heads :]
    got_ref, n_ref, u_ref, w_ref, d_ref, send_scr, own_scr, part_scr, sems = refs
    copies = [
        pltpu.make_async_copy(far_refs[i], ref, sems.at[i])
        for i, ref in enumerate((got_ref, n_ref, u_ref, w_ref))
    ]
    n_w = sz.w_chunk
    mine = lax.rem(my_blk_of(sz, scal_ref), sz.parts)
    copies += [
        pltpu.make_async_copy(send_scr.at[:, sz.parts - 1 - mine], give_ref, sems.at[4]),
        pltpu.make_async_copy(send_scr.at[:, mine], keep_ref, sems.at[5]),
        pltpu.make_async_copy(own_scr, part_refs[0], sems.at[6]),
    ]
    copies += [
        pltpu.make_async_copy(part_scr.at[s - 1], part_refs[s], sems.at[6 + s])
        for s in range(1, sz.heads)
    ]
    for copy in copies[:4]:
        copy.start()
    head = my_head_of(sz, scal_ref)
    half_run = sz.run // 2
    copies[0].wait()
    for slot in range(sz.heads):
        to = slot_head(sz, scal_ref, slot)
        q_at = pl.multiple_of(to * half_run, half_run)
        kv_at = pl.multiple_of(sz.half + to * sz.run, sz.run)
        for seq in range(sz.seqs):
            for part in range(sz.parts):
                at = slot * sz.mine + seq * sz.sub + part * sz.run
                first = got_ref[sz.task(seq, 0, part), pl.ds(q_at, half_run)]
                second = got_ref[sz.task(seq, 1, part), pl.ds(q_at, half_run)]
                low, high = halves(first, second)
                d_ref[at : at + half_run, :LANES] = low
                d_ref[at + half_run : at + sz.run, :LANES] = high
                for local in range(sz.local):
                    d_ref[at : at + sz.run, (1 + local) * LANES : (2 + local) * LANES] = got_ref[
                        sz.task(seq, local, part), pl.ds(kv_at, sz.run)
                    ]
    d_proj = d_ref[...]
    copies[1].wait()
    grad_w = dot_nn(n_ref[...], d_proj).astype(bf16)
    for dev in range(sz.devices):
        rows = slice(dev * sz.w_rows, (dev + 1) * sz.w_rows)
        for i in range(1 + sz.local):
            cols = slice(i * LANES, (i + 1) * LANES)
            to = (dev // sz.parts, dev % sz.parts)
            send_scr[*to, i * sz.w_rows : (i + 1) * sz.w_rows] = grad_w[rows, cols]
    copies[2].wait()
    copies[3].wait()
    weights = w_ref[...].astype(f32)
    ones = jnp.ones((16, sz.tokens), bf16)
    column = dot_nn(ones, d_proj)[:SMALL]
    terms = [dot_nn(u_ref[...], d_proj) * weights, column[0:1] * weights]
    ones = jnp.ones((16, (1 + sz.local) * LANES), bf16)
    sums = []
    for term in terms:
        high = term.astype(bf16)
        low = (term - high.astype(f32)).astype(bf16)
        sums.append((dot_nt(ones, high) + dot_nt(ones, low))[0:1])
    wide = jnp.concatenate([*sums, jnp.zeros((SMALL - 2, sz.width), f32)], axis=0)
    sum_q = column[:, :LANES]
    sum_v = jnp.concatenate([column[:, LANES + HD : 2 * LANES], column[:, 2 * LANES + HD :]], axis=1)
    per = sz.w_rows
    small = (
        early_ref[...]
        + both_levels(wide, per, 0, (0, 2), sz.devices)
        + both_levels(sum_q, 2 * per, head * LANES, (6, 7), sz.devices)
        + both_levels(sum_v, 2 * per, sz.width + head * LANES, (6, 7), sz.devices)
    )
    small = two_levels(small.reshape(-1, sz.parts, SMALL, LANES))
    send_scr[:, :, n_w:, :] = small
    copies[4].start()
    copies[5].start()
    grad_one = dot_nt(d_proj, w_ref[...])
    own_scr[...] = grad_one[: sz.mine]
    part_scr[...] = grad_one[sz.mine :].astype(bf16).reshape(part_scr.shape)
    for copy in copies[6:]:
        copy.start()
    for copy in copies[4:]:
        copy.wait()


def two_levels(small):
    high = small.astype(bf16).astype(f32)
    return jnp.concatenate([high, small - high], axis=-2).astype(bf16)


def fold_kernel(sz, scal_ref, keep_ref, got_ref, send_ref):
    n_w = sz.w_chunk
    total = keep_ref[...].astype(f32) + got_ref[...].astype(f32)
    send_ref[:, :n_w] = total[:, :n_w].astype(bf16)
    send_ref[:, n_w:] = two_levels(total[:, n_w : n_w + SMALL] + total[:, n_w + SMALL :])


def input_grad_kernel(sz, scal_ref, vec_ref, grad_ref, x_ref, *refs):
    out_ref = refs[sz.heads]
    upstream = refs[0][...]
    for ref in refs[1 : sz.heads]:
        upstream = upstream + ref[...].astype(f32)
    gain, shift = vec_ref[0:1], vec_ref[1:2]
    _, unit, root = norm_forward(x_ref[...].astype(f32), gain, shift)
    out_ref[...] = (grad_ref[...] + norm_input_grad(upstream, unit, root, gain)).astype(bf16)


def split_kernel(sz, scal_ref, sum_a_ref, sum_b_ref, own_ref, *refs):
    n = sz.heads
    early_ref, refs = refs[-1], refs[:-1]
    wide = jnp.concatenate(
        [sum_a_ref[0:2], sum_b_ref[0:1], sum_a_ref[0:2], sum_b_ref[1:2], sum_a_ref[2:3]]
        + [jnp.zeros((1, sz.width), f32)],
        axis=0,
    )
    up_bias = jnp.broadcast_to(sum_a_ref[2:3], (SMALL, sz.width))
    at = my_head_of(sz, scal_ref) * sz.hidden_slice
    early_ref[...] = both_levels(wide, sz.w_rows, 0, (2, 6), sz.devices) + both_levels(
        up_bias, 4 * sz.w_rows, at, (7, 8), sz.devices
    )
    got_refs, feed_refs, refs = refs[: sz.groups - 1], refs[sz.groups - 1 :][: n - 1], refs[-n:]
    piece_ref, *send_refs = refs

    def total(rows):
        value = own_ref[rows]
        for ref in got_refs:
            value = value + ref[rows].astype(f32)
        return value

    for slot in range(n):
        to = slot_head(sz, scal_ref, slot)
        at = pl.multiple_of(to * sz.w_rows, sz.w_rows)
        up = total(pl.ds(at, sz.w_rows)).astype(bf16)
        out = total(pl.ds(at + n * sz.w_rows, sz.w_rows))
        ref = send_refs[slot - 1] if slot else piece_ref
        base = sz.mine if slot else 0
        if slot:
            ref[: sz.mine] = feed_refs[slot - 1][...]
        ref[base : base + sz.w_rows] = up
        ref[base + sz.w_rows :] = out.astype(bf16)


def final_kernel(sz, scal_ref, got_ref, *refs):
    piece_refs, refs = refs[: sz.heads], refs[sz.heads :]
    w_ref, up_ref, out_ref, *small_refs = refs
    out = piece_refs[0][sz.w_rows :].astype(f32)
    for ref in piece_refs[1:]:
        out = out + ref[sz.mine + sz.w_rows :].astype(f32)
    out_ref[...] = out
    for slot in range(sz.heads):
        at = pl.multiple_of(slot_head(sz, scal_ref, slot) * sz.hidden_slice, LANES)
        base = sz.mine if slot else 0
        piece = piece_refs[(sz.heads - slot) % sz.heads][base : base + sz.w_rows]
        up_ref[:, pl.ds(at, sz.hidden_slice)] = piece.astype(f32)
    for head in range(sz.heads):
        total = jnp.zeros((sz.w_chunk, LANES), f32)
        for group in range(sz.groups):
            total = total + got_ref[head * sz.groups + group, : sz.w_chunk].astype(f32)
        at = head * LANES
        w_ref[:, at : at + LANES] = total[: sz.w_rows]
        low, high = halves(total[sz.w_rows : 2 * sz.w_rows], total[2 * sz.w_rows :])
        w_ref[:, sz.width + at : sz.width + at + LANES] = low
        w_ref[:, 2 * sz.width + at : 2 * sz.width + at + LANES] = high
    small = jnp.sum(got_ref[:, sz.w_chunk :, :].astype(f32), axis=0)
    small = small[:SMALL] + small[SMALL:]
    for i, ref in enumerate(small_refs):
        ref[...] = small[i : i + 1, : ref.shape[1]]


BLK = ("group", "part")
ALL = ("head", "group", "part")


def on_device_fused(
    sz,
    layer_input,
    segments,
    token_valid,
    attention_gain,
    attention_shift,
    project_weight,
    project_bias,
    output_weight,
    output_bias,
    feed_gain,
    feed_shift,
    up_weight,
    up_bias,
    down_weight,
    down_bias,
    cotangent,
):
    n = sz.heads
    my_head = lax.axis_index("head")
    my_blk = lax.axis_index(BLK)
    scal = (my_head * sz.blocks + my_blk).astype(i32).reshape(1)
    geo = AttentionShape(sz.blocks, sz.part_rows, sz.parts, sz.run, sz.sub)
    token_shape = (sz.mine, sz.width)

    def call(kernel, name, arrays, outs, scratch=(), limit=VMEM_LIMIT):
        kernel = functools.partial(kernel, sz)
        return local_call(kernel, name, scal, arrays, outs, scratch, limit)

    def around(x, step):
        return lax.ppermute(x, "head", [(i, (i + step) % n) for i in range(n)])

    def after(values, *earlier):
        return lax.optimization_barrier((values, *earlier))[0]

    def around_groups(x, step):
        pairs = [
            (g * sz.parts + p, (g + step) % sz.groups * sz.parts + p)
            for g in range(sz.groups)
            for p in range(sz.parts)
        ]
        return lax.ppermute(x, BLK, pairs)

    def around_parts(x, step):
        return lax.ppermute(x, BLK, within_group(sz.blocks, sz.parts, step))

    x_mine = layer_input.reshape(token_shape)
    g_mine = cotangent.reshape(token_shape)
    small = [attention_gain, attention_shift, output_bias, feed_gain, feed_shift, down_bias]
    small += [project_bias, up_bias]
    (send,) = staged_call(
        functools.partial(pack_kernel, sz),
        "pack",
        scal,
        [project_weight, *[v.reshape(1, -1) for v in small]],
        [((n * sz.groups, sz.w_chunk + SMALL, LANES), bf16)],
        [pltpu.VMEM((SMALL, LANES), f32)],
    )
    got = exchange(send, ("head", "group"))
    x_slots = [x_mine] + [around(after(x_mine, send), d) for d in range(1, n)]
    pieces = staged_call(
        functools.partial(pieces_kernel, sz),
        "pieces",
        after(scal, send),
        [g_mine, up_weight, output_weight],
        [((sz.mine + 2 * sz.w_rows, sz.width), bf16)] * n,
    )
    g_slots = [pieces[0]] + [around(after(pieces[d], x_slots[1]), d) for d in range(1, n)]
    got_parts = [got] + [around_parts(got, d) for d in range(1, sz.parts)]

    my_part = my_blk % sz.parts
    my_seq = (my_blk // sz.parts) // sz.local
    scalars, bounds = attention_bounds(
        segments, token_valid, my_seq, my_part, geo, sz.heads, sz.sub
    )
    got_parts[0] = after(got_parts[0], scalars, bounds)
    send, w_slice, vec = call(
        project_kernel,
        "project",
        [*got_parts, *x_slots],
        [
            ((sz.blocks, sz.half + sz.part_rows, LANES), bf16),
            far((sz.width, (1 + sz.local) * LANES), bf16),
            far((SMALL, sz.width), f32),
        ],
        [pltpu.VMEM((sz.devices * SMALL, LANES), f32)],
    )
    column = jnp.concatenate([v[sz.mine :] for v in g_slots], axis=0)
    columns = [column] + [around_groups(column, d) for d in range(1, sz.groups)]
    downs = [after(down_weight, x_slots[1])]
    downs += [around_groups(downs[0], d) for d in range(1, sz.groups)]
    task = exchange(send, BLK)
    task = after(task, column, *downs)
    others = [around_parts(task, step) for step in range(1, sz.parts)]
    o_task, ot, lse = attention_forward(geo, scalars, [task, *others], bounds)
    columns += [around_parts(after(v, o_task), d) for d in range(1, sz.parts) for v in columns]
    downs += [around_parts(after(v, o_task), d) for d in range(1, sz.parts) for v in downs]
    square = ((sz.width, sz.width), bf16)
    w_up, w_out, w_down = call(assemble_kernel, "assemble", [*columns, *downs], [square] * 3)
    mixed = exchange(o_task, BLK)
    turned = far((sz.width, sz.tokens), bf16)
    n_one, u_one = call(
        norm_again_kernel, "norm_again", [after(vec, o_task), *x_slots], [turned, turned]
    )
    mixed = after(mixed, n_one, *columns)
    m_slots = [mixed] + [around(mixed, d) for d in range(1, n)]

    outs = call(
        feed_kernel,
        "feed",
        [vec, w_up, w_out, w_down, *x_slots, *g_slots, *m_slots],
        [far(token_shape, f32)]
        + [(token_shape, bf16)] * (n - 1)
        + [far(token_shape, f32)]
        + [far(token_shape, bf16)] * (n - 1)
        + [far(token_shape, f32)]
        + [((n, sz.mine, sz.hidden_slice), bf16)] * 2
        + [((n, *token_shape), bf16), far(token_shape, bf16), far((SMALL, sz.width), f32)],
        [
            pltpu.VMEM((n, *token_shape), bf16),
        ],
    )
    grad_two, feed = outs[:n], outs[n : 2 * n]
    middle, activated, grad_hidden, n_two, mixed_own, feed_sums = outs[2 * n :]
    grad_two = [grad_two[0]] + [around(grad_two[d], -d) for d in range(1, n)]

    def shared(rows):
        shape = (sz.groups, rows, sz.width)
        return [far(shape, f32), far(shape, bf16)]

    keep, give = call(
        feed_grad_kernel,
        "feed_grad",
        [activated, grad_hidden, n_two, *g_slots],
        shared(sz.f_rows + n * sz.w_rows),
    )

    grad_middle, branch, send, branch_sums, keep_out, give_out = call(
        middle_grad_kernel,
        "middle_grad",
        [vec, w_out, middle, g_mine, mixed_own, *grad_two],
        [
            far(token_shape, f32),
            far(token_shape, bf16),
            ((sz.devices, sz.run // 2, LANES), bf16),
            far((SMALL, sz.width), f32),
            *shared(n * sz.w_rows),
        ],
    )
    do_task = exchange(send, ALL)
    given = around_parts(give, 1)
    down_shape, rest_shape = (sz.f_rows, sz.width), (2 * n * sz.w_rows, sz.width)
    sums = call(
        part_sum_kernel,
        "part_sum",
        [keep, given, keep_out, around_parts(give_out, 1)],
        [far(down_shape, f32)]
        + [far(down_shape, bf16)] * (sz.groups - 1)
        + [far(rest_shape, f32)]
        + [(rest_shape, bf16)] * (sz.groups - 1),
    )
    down_sum, w_sum = sums[: sz.groups], sums[sz.groups :]
    w_pieces = [around_groups(w_sum[d], d) for d in range(1, sz.groups)]
    dq, dkv, *dkv_others = attention_backward(
        geo, do_tile_grouped, scalars, [task, *others], do_task, bounds, ot, lse
    )
    dkv_others[0] = after(dkv_others[0], *w_pieces)
    for step in range(1, sz.parts):
        back = within_group(sz.blocks, sz.parts, -step)
        dkv = dkv + lax.ppermute(dkv_others[step - 1], BLK, back).astype(f32)
    send = jnp.concatenate([dq, dkv.astype(bf16)], axis=1)
    got = exchange(send, BLK)
    piece, *rest = call(
        split_kernel,
        "split",
        [feed_sums, branch_sums, after(w_sum[0], send), *w_pieces, *feed[1:]],
        [far((2 * sz.w_rows, sz.width), bf16)]
        + [far((sz.mine + 2 * sz.w_rows, sz.width), bf16)] * (n - 1)
        + [far((sz.devices * SMALL, LANES), f32)],
    )
    early = rest.pop()
    rest = [around(v, -d - 1) for d, v in enumerate(rest)]
    got = after(got, rest[0], rest[1])
    wide = (1 + sz.local) * LANES
    send_shape = (n * sz.groups, sz.w_chunk + 2 * SMALL, LANES)
    keep, give, *outs = pl.pallas_call(
        functools.partial(project_grad_kernel, sz),
        out_shape=(
            pltpu.HBM(send_shape, bf16),
            pltpu.HBM(send_shape, bf16),
            pltpu.HBM(token_shape, f32),
            *[pltpu.HBM(token_shape, bf16)] * (n - 1),
        ),
        in_specs=[pl.BlockSpec(memory_space=pltpu.SMEM), pl.BlockSpec(memory_space=pltpu.VMEM)]
        + [pl.BlockSpec(memory_space=pltpu.HBM)] * 4,
        out_specs=tuple([pl.BlockSpec(memory_space=pltpu.HBM)] * (2 + n)),
        scratch_shapes=[
            pltpu.VMEM(got.shape, bf16),
            pltpu.VMEM((sz.width, sz.tokens), bf16),
            pltpu.VMEM((sz.width, sz.tokens), bf16),
            pltpu.VMEM((sz.width, wide), bf16),
            pltpu.VMEM((sz.tokens, wide), bf16),
            pltpu.VMEM((send_shape[0], sz.parts, *send_shape[1:]), bf16),
            pltpu.VMEM(token_shape, f32),
            pltpu.VMEM((n - 1, *token_shape), bf16),
            pltpu.SemaphoreType.DMA((6 + n,)),
        ],
        compiler_params=pltpu.CompilerParams(vmem_limit_bytes=63 * 2**20),
        cost_estimate=pl.CostEstimate(
            flops=COST["project_grad"], bytes_accessed=10**6, transcendentals=0
        ),
        name="project_grad",
    )(scal, early, got, n_one, u_one, w_slice)
    (send,) = call(fold_kernel, "fold", [keep, around_parts(give, 1)], [(send_shape, bf16)])
    got = exchange(send, ("head", "group"))
    grad_one = [outs[0]] + [around(outs[d], -d) for d in range(1, n)]
    down_grad = down_sum[0]
    for d in range(1, sz.groups):
        down_grad = down_grad + around_groups(after(down_sum[d], outs[1]), d).astype(f32)
    (input_grad,) = call(
        input_grad_kernel,
        "input_grad",
        [vec, grad_middle, x_mine, *grad_one],
        [(token_shape, bf16)],
    )
    layer_output = middle + feed[0] + vec[5:6]
    for v in rest:
        layer_output = layer_output + v[: sz.mine].astype(f32)
    layer_output = layer_output.astype(bf16)
    w_grad, up_grad, out_grad, *owned = call(
        final_kernel,
        "final",
        [got, piece, *rest],
        [
            ((sz.w_rows, 3 * sz.width), f32),
            ((sz.w_rows, n * sz.hidden_slice), f32),
            ((sz.w_rows, sz.width), f32),
        ]
        + [((1, v.shape[0]), f32) for v in small],
    )
    owned = [v.reshape(-1) for v in owned]
    return (
        layer_output.reshape(layer_input.shape),
        input_grad.reshape(layer_input.shape),
        owned[0],
        owned[1],
        w_grad,
        owned[6],
        out_grad,
        owned[2],
        owned[3],
        owned[4],
        up_grad,
        owned[7],
        down_grad,
        owned[5],
    )


def solution(mesh):
    heads, blocks = mesh.shape["head"], mesh.shape["blk"]

    def layer(*arguments):
        layer_input, up_weight = arguments[0], arguments[11]
        seqs, _, tokens, width = layer_input.shape
        sz = Sizes(heads, blocks, seqs, tokens // heads, width, up_weight.shape[1])
        if sz.fits():
            split = (heads, blocks // sz.parts, sz.parts)
            inner = jax.sharding.Mesh(mesh.devices.reshape(split), ALL)
            body, blk, everywhere = functools.partial(on_device_fused, sz), BLK, ALL
        else:
            inner, body, blk, everywhere = mesh, on_device_general, "blk", BOTH
        rows = P(None, blk, "head", None)
        vector, matrix = P(everywhere), P(everywhere, None)
        weights = (vector, vector, matrix, vector, matrix, vector)
        weights += (vector, vector, matrix, vector, matrix, vector)
        return jax.shard_map(
            body,
            mesh=inner,
            in_specs=(rows, P(), P(), *weights, rows),
            out_specs=(rows, rows, *weights),
            check_vma=False,
        )(*arguments)

    return layer
```
